32 devices in a mesh: clip: 4 (over y, x), row: 8 (over z, core).
Axes of the slice: x: 2, y: 2, z: 4, core: 2. Of those that a mesh axis runs over, the one named last changes fastest.
Arguments:
- clip_input: bfloat16 [16, 8, 8, 16, 2048], P('clip', None, 'row'), may hold values from -6 to 6
- temporal: bfloat16 [3, 2048, 512], replicated, may hold values from -0.078125 to 0.078125
- spatial: bfloat16 [3, 3, 512, 512], replicated, may hold values from -0.09375 to 0.09375
- expand: bfloat16 [512, 2048], replicated, may hold values from -0.25 to 0.25
- mid_gain: float32 [2, 512], replicated, may hold values from 0.5 to 1.5
- mid_shift: float32 [2, 512], replicated, may hold values from -3 to 3
- out_gain: float32 [2048], replicated, may hold values from 0.5 to 1.5
- out_shift: float32 [2048], replicated, may hold values from -2 to 2
- short_weight: bfloat16 [2048, 512], replicated, may hold values from -0.125 to 0.125
- bank_weight: bfloat16 [2048, 512], replicated, may hold values from -0.125 to 0.125
- block_weight: bfloat16 [2, 4, 512, 512], replicated, may hold values from -0.25 to 0.25
- norm_gain: float32 [2, 512], replicated, may hold values from 0.5 to 1.5
- norm_shift: float32 [2, 512], replicated, may hold values from -2 to 2
- class_weight: bfloat16 [2560, 80], replicated, may hold values from -0.125 to 0.125
- bank_feats: bfloat16 [16, 640, 2048], P('clip', 'row'), may hold values from -9 to 9
- bank_mask: int32 [16, 640], P('clip'), may hold values from 0 to 1, as said below
- box_coords: int32 [1024, 4], P('clip'), may hold values from 0 to 64, as said below
- box_clip: int32 [1024], P('clip'), may hold values from 0 to 15, as said below
- box_valid: int32 [1024], P(('clip', 'row')), may hold values 0 or 1
- labels: int32 [1024, 80], P(('clip', 'row')), may hold values 0 or 1
Outputs:
- scores: float32 [1024, 80], P(('clip', 'row'))
- input_gradient: float32 [16, 8, 8, 16, 2048], P('clip', None, 'row')
- temporal_gradient: float32 [3, 2048, 512], P(None, 'row')
- spatial_gradient: float32 [3, 3, 512, 512], P(None, None, 'row')
- expand_gradient: float32 [512, 2048], P(None, 'row')
- mid_gain_gradient: float32 [2, 512], P(None, 'row')
- mid_shift_gradient: float32 [2, 512], P(None, 'row')
- out_gain_gradient: float32 [2048], P('row')
- out_shift_gradient: float32 [2048], P('row')
- short_gradient: float32 [2048, 512], P('row')
- bank_gradient: float32 [2048, 512], P('row')
- block_gradient: float32 [2, 4, 512, 512], P(None, None, 'row')
- norm_gain_gradient: float32 [2, 512], P(None, 'row')
- norm_shift_gradient: float32 [2, 512], P(None, 'row')
- class_gradient: float32 [2560, 80], P('row')
The draws below stay inside these ranges and needn't reach their ends.
Inputs may be any that keep to these rules, and one draw needn't show every extreme that they name: `box_coords`: each row is (top, bottom, left, right) with top + 4 <= bottom <= 32 and left + 4 <= right <= 64; in every group of 256 box slots some box covers the whole map. `box_clip`: box i refers to a clip of its own group, i // 256 * 4 up to that plus 4 - 1; in every group the first and the last of these clips have boxes. `bank_mask`: every clip has at least one live bank slot.
All inputs are finite; a program needn't handle non-finite values. No bound on the sum of `box_valid` or of `labels` on one device may be relied on, other than what follows from the above.
Results may differ from the reference program's by a relative error of at most 0.017.
Values may be sent and summed in bfloat16 or wider, within the bound.
No kernel may reach another device: no remote copies, remote signals or barrier semaphores. Data moves between devices by JAX's collectives and lax.ppermute only.
A program may use at most 192 MiB of HBM per device.

```python
import math
from functools import partial
import jax
import jax.numpy as jnp
from jax import lax

C_IN = 2048
MID = 512
NL = 512
CLASSES = 80
FRAMES = 8
COLS = 16
BANK = 640
SAMPLES = 14
CLIPS_DEV = 4
CLIPS = 16
ROWS = 8
BOX_GROUP = 256
BOXES = 1024
CAT = 2560
N_CLIP = 4


def draw_box_coords(key, part):
    key = jax.random.fold_in(key, 11)
    pieces = jax.random.split(key, 5)
    row_span = 4 * ROWS
    col_span = 4 * COLS
    top_edge = jax.random.randint(pieces[0], (BOXES,), 0, row_span - 3)
    height_cells = jax.random.randint(pieces[1], (BOXES,), 4, row_span + 1)
    bottom_edge = jnp.minimum(top_edge + height_cells, row_span)
    left_edge = jax.random.randint(pieces[2], (BOXES,), 0, col_span - 3)
    width_cells = jax.random.randint(pieces[3], (BOXES,), 4, col_span + 1)
    right_edge = jnp.minimum(left_edge + width_cells, col_span)
    chosen = jax.random.randint(pieces[4], (BOXES // BOX_GROUP,), 0, BOX_GROUP)
    whole = jnp.arange(BOXES) % BOX_GROUP == jnp.repeat(chosen, BOX_GROUP, total_repeat_length=BOXES)
    top_edge = jnp.where(whole, 0, top_edge)
    bottom_edge = jnp.where(whole, row_span, bottom_edge)
    left_edge = jnp.where(whole, 0, left_edge)
    right_edge = jnp.where(whole, col_span, right_edge)
    return jnp.stack([top_edge, bottom_edge, left_edge, right_edge], axis=1).astype(jnp.int32)


def draw_box_clip(key, part):
    key = jax.random.fold_in(key, 23)
    pieces = jax.random.split(key, 3)
    groups = BOXES // BOX_GROUP
    within = jax.random.randint(pieces[0], (BOXES,), 0, CLIPS_DEV)
    first_slot = jax.random.randint(pieces[1], (groups,), 0, BOX_GROUP)
    second_slot = (first_slot + 1 + jax.random.randint(pieces[2], (groups,), 0, BOX_GROUP - 1)) % BOX_GROUP
    slot = jnp.arange(BOXES) % BOX_GROUP
    first_hit = slot == jnp.repeat(first_slot, BOX_GROUP, total_repeat_length=BOXES)
    second_hit = slot == jnp.repeat(second_slot, BOX_GROUP, total_repeat_length=BOXES)
    within = jnp.where(first_hit, 0, within)
    within = jnp.where(second_hit, CLIPS_DEV - 1, within)
    return (jnp.arange(BOXES) // BOX_GROUP * CLIPS_DEV + within).astype(jnp.int32)


def draw_bank_mask(key, part):
    key = jax.random.fold_in(key, 37)
    pieces = jax.random.split(key, 2)
    live = jax.random.randint(pieces[0], (CLIPS, BANK), 0, 16) < 15
    forced = jax.random.randint(pieces[1], (CLIPS,), 0, BANK)
    forced_row = jnp.arange(BANK)[None, :] == forced[:, None]
    return (live | forced_row).astype(jnp.int32)


def place_ends(entries, stream_key, least, top_value):
    dims = entries.shape
    place = [jax.random.randint(jax.random.fold_in(stream_key, axis), (), 0, dims[axis]) for axis in range(len(dims))]
    entries = entries.at[tuple(place)].set(least)
    longest = dims.index(max(dims))
    place[longest] = (place[longest] + 1) % dims[longest]
    return entries.at[tuple(place)].set(top_value)


def block_levels(key, shape, cuts, least, top_value):
    def one(dim, parts):
        steps = jax.random.uniform(jax.random.fold_in(jax.random.fold_in(key, 6), dim), (parts,), jnp.float32, least / len(cuts), top_value / len(cuts))
        return jnp.repeat(jnp.exp(steps), shape[dim] // parts).reshape((-1,) + (1,) * (len(shape) - dim - 1))

    loudness = one(*cuts[0])
    for cut in cuts[1:]:
        loudness = loudness * one(*cut)
    return loudness


def bell_draw(stream_key, shape, deviation, limit, cuts=(), held_as=jnp.bfloat16):
    level = block_levels(stream_key, shape, cuts, -0.22, 0.18) if cuts else 1.0
    values = jax.random.normal(stream_key, shape, jnp.float32) * deviation * level
    return jnp.minimum(jnp.maximum(values, -limit), limit).astype(held_as)


def setup_inputs(seed: int = 0) -> dict:
    key_list = jax.random.split(jax.random.key(seed), 21)
    clip_input = bell_draw(key_list[0], (CLIPS, FRAMES, ROWS, COLS, C_IN), 1.0, 6.0, ((0, 4), (2, 8)))
    temporal = bell_draw(key_list[1], (3, C_IN, MID), (3 * C_IN) ** -0.5, 0.078125)
    spatial = bell_draw(key_list[2], (3, 3, MID, MID), (9 * MID) ** -0.5, 0.09375)
    expand = bell_draw(key_list[3], (MID, C_IN), MID ** -0.5, 0.25)
    mid_gain = jnp.clip(1.0 + 0.1 * jax.random.normal(key_list[4], (2, MID), jnp.float32), 0.5, 1.5)
    mid_shift = bell_draw(key_list[5], (2, MID), 0.5, 3.0, (), jnp.float32)
    out_gain = jnp.clip(1.0 + 0.1 * jax.random.normal(key_list[6], (C_IN,), jnp.float32), 0.5, 1.5)
    out_shift = bell_draw(key_list[7], (C_IN,), 0.3, 2.0, (), jnp.float32)
    short_weight = bell_draw(key_list[8], (C_IN, NL), C_IN ** -0.5, 0.125)
    bank_weight = bell_draw(key_list[9], (C_IN, NL), C_IN ** -0.5, 0.125)
    block_weight = bell_draw(key_list[10], (2, 4, NL, NL), NL ** -0.5, 0.25)
    norm_gain = jnp.clip(1.0 + 0.1 * jax.random.normal(key_list[11], (2, NL), jnp.float32), 0.5, 1.5)
    norm_shift = bell_draw(key_list[12], (2, NL), 0.3, 2.0, (), jnp.float32)
    class_weight = bell_draw(key_list[13], (CAT, CLASSES), CAT ** -0.5, 0.125)
    bank_feats = bell_draw(key_list[14], (CLIPS, BANK, C_IN), 1.5, 9.0, ((0, 4), (1, 8)))
    bank_mask = draw_bank_mask(jax.random.fold_in(key_list[20], 71), 0)
    box_coords = draw_box_coords(jax.random.fold_in(key_list[20], 71), 0)
    box_clip = draw_box_clip(jax.random.fold_in(key_list[20], 71), 0)
    box_valid = place_ends((jax.random.randint(key_list[18], (BOXES,), 0, 4) < 3).astype(jnp.int32), jax.random.fold_in(key_list[18], 1), 0, 1)
    labels = place_ends((jax.random.randint(key_list[19], (BOXES, CLASSES), 0, 6) < 1).astype(jnp.int32), jax.random.fold_in(key_list[19], 1), 0, 1)
    return {"clip_input": clip_input, "temporal": temporal, "spatial": spatial, "expand": expand, "mid_gain": mid_gain, "mid_shift": mid_shift, "out_gain": out_gain, "out_shift": out_shift, "short_weight": short_weight, "bank_weight": bank_weight, "block_weight": block_weight, "norm_gain": norm_gain, "norm_shift": norm_shift, "class_weight": class_weight, "bank_feats": bank_feats, "bank_mask": bank_mask, "box_coords": box_coords, "box_clip": box_clip, "box_valid": box_valid, "labels": labels}


highest = lax.Precision.HIGHEST
epsilon = 1e-05

@jax.custom_vjp
def low(v):
    return lax.optimization_barrier(v.astype(jnp.bfloat16)).astype(jnp.float32)

@jax.custom_vjp
def low_back(v):
    return v

def low_keep(v):
    return (low(v), None)

def low_pass(kept, grad):
    return (grad,)

def back_keep(v):
    return (v, None)

def back_low(kept, grad):
    return (low(grad),)
low.defvjp(low_keep, low_pass)
low_back.defvjp(back_keep, back_low)

def axis_weights(low_edge, high_edge, cell_count, first_cell, span_count):
    samples = (jnp.arange(SAMPLES, dtype=jnp.float32) + 0.5) / SAMPLES
    start_pos = low_edge.astype(jnp.float32) * 0.25
    extent = (high_edge - low_edge).astype(jnp.float32) * 0.25
    points = start_pos[:, None] + extent[:, None] * samples[None, :]
    points = jnp.clip(points - 0.5, 0.0, cell_count - 1.0)
    centers = (first_cell + jnp.arange(span_count, dtype=jnp.int32)).astype(jnp.float32)
    tents = jnp.maximum(0.0, 1.0 - jnp.abs(points[:, :, None] - centers[None, None, :]))
    return lax.optimization_barrier(jnp.mean(tents, axis=1))

def box_weights(coords, clip_local, first_row, row_count, rows_total, clip_count, col_count):
    along_rows = axis_weights(coords[:, 0], coords[:, 1], rows_total, first_row, row_count)
    along_cols = axis_weights(coords[:, 2], coords[:, 3], col_count, 0, col_count)
    member = (clip_local[:, None] == jnp.arange(clip_count, dtype=jnp.int32)[None, :]).astype(jnp.float32)
    product = along_rows[:, None, :, None] * along_cols[:, None, None, :] * member[:, :, None, None]
    return low(product)

def time_conv(source, kernel):
    frames = source.shape[1]
    padded = jnp.pad(source, ((0, 0), (1, 1), (0, 0), (0, 0), (0, 0)))
    summed = jnp.zeros(source.shape[:4] + (kernel.shape[2],), jnp.float32)
    for offset in range(3):
        summed = summed + jnp.einsum('ctrwk,km->ctrwm', padded[:, offset:offset + frames], kernel[offset], precision=highest)
    return summed

def plane_conv(source, kernel):
    row_count, col_count = (source.shape[2], source.shape[3])
    padded = jnp.pad(source, ((0, 0), (0, 0), (1, 1), (1, 1), (0, 0)))
    summed = jnp.zeros(source.shape[:4] + (kernel.shape[3],), jnp.float32)
    for row_shift in range(3):
        for col_shift in range(3):
            window = padded[:, :, row_shift:row_shift + row_count, col_shift:col_shift + col_count]
            summed = summed + jnp.einsum('ctrwk,km->ctrwm', window, kernel[row_shift, col_shift], precision=highest)
    return summed

def nl_block(stream, memory, weights, gain_row, shift_row, allowed):
    rows_in = low(stream).reshape(N_CLIP, BOX_GROUP, NL)
    query_rows = low_back(low(jnp.einsum('gbn,nm->gbm', rows_in, weights[0], precision=highest)))
    key_rows = low_back(low(jnp.einsum('gjn,nm->gjm', memory, weights[1], precision=highest)))
    value_rows = low_back(low(jnp.einsum('gjn,nm->gjm', memory, weights[2], precision=highest)))
    raw_scores = low_back(jnp.einsum('gbm,gjm->gbj', query_rows, key_rows, precision=highest))
    masked = jnp.where(allowed, raw_scores * (1.0 / math.sqrt(NL)), -jnp.inf)
    row_peak = lax.optimization_barrier(jnp.max(masked, axis=2, keepdims=True))
    exponent = jnp.exp(masked - row_peak)
    attention = exponent / lax.optimization_barrier(jnp.sum(exponent, axis=2, keepdims=True))
    attended = low_back(jnp.einsum('gbj,gjm->gbm', low(attention), value_rows, precision=highest))
    centred = attended - lax.optimization_barrier(jnp.mean(attended, axis=2, keepdims=True))
    normed = centred * lax.rsqrt(lax.optimization_barrier(jnp.mean(centred * centred, axis=2, keepdims=True)) + epsilon) * gain_row + shift_row
    hidden = low(jax.nn.silu(normed))
    branch = low_back(jnp.einsum('gbm,mn->gbn', hidden, weights[3], precision=highest))
    return stream + branch.reshape(BOXES, NL)

def forward(bank_input, allowed, roi_weight, valid_rows, target_rows, clip_input, temporal, spatial, expand, mid_gain, mid_shift, out_gain, out_shift, short_weight, bank_weight, block_weight, norm_gain, norm_shift, class_weight):
    temporal_sum = low_back(time_conv(clip_input, temporal))
    temporal_out = low(jax.nn.silu(temporal_sum * mid_gain[0] + mid_shift[0]))
    plane_sum = low_back(plane_conv(temporal_out, spatial))
    plane_out = low(jax.nn.silu(plane_sum * mid_gain[1] + mid_shift[1]))
    expand_sum = low_back(jnp.einsum('ctrwm,mk->ctrwk', plane_out, expand, precision=highest))
    final_arg = expand_sum * out_gain + out_shift + clip_input
    pooled = low(lax.optimization_barrier(jnp.mean(jax.nn.silu(final_arg), axis=1)))
    grouped = pooled.reshape(N_CLIP, CLIPS_DEV, ROWS, COLS, C_IN)
    features = jnp.einsum('gbcrw,gcrwk->gbk', roi_weight, grouped, precision=highest).reshape(BOXES, C_IN)
    box_rows = low_back(low(features))
    stream = low_back(jnp.dot(box_rows, short_weight, precision=highest))
    memory = low_back(low(jnp.einsum('cjk,kn->cjn', bank_input, bank_weight, precision=highest)))
    memory = memory.reshape(N_CLIP, CLIPS_DEV * BANK, NL)
    for block_index in range(2):
        stream = nl_block(stream, memory, block_weight[block_index], norm_gain[block_index], norm_shift[block_index], allowed)
    joined = jnp.concatenate([box_rows, low(stream)], axis=1)
    class_logits = low_back(jnp.dot(joined, class_weight, precision=highest))
    loss = jnp.sum(valid_rows[:, None] * (jax.nn.softplus(class_logits) - target_rows * class_logits)) / CLIPS
    return (loss, jax.nn.sigmoid(class_logits))

def reference(clip_input, temporal, spatial, expand, mid_gain, mid_shift, out_gain, out_shift, short_weight, bank_weight, block_weight, norm_gain, norm_shift, class_weight, bank_feats, bank_mask, box_coords, box_clip, box_valid, labels):
    group_of_box = jnp.arange(BOXES, dtype=jnp.int32) // BOX_GROUP
    clip_local = box_clip - group_of_box * CLIPS_DEV
    roi_weight = box_weights(box_coords, clip_local, 0, ROWS, ROWS, CLIPS_DEV, COLS)
    roi_weight = roi_weight.reshape(N_CLIP, BOX_GROUP, CLIPS_DEV, ROWS, COLS)
    member = clip_local[:, None] == jnp.arange(CLIPS_DEV, dtype=jnp.int32)[None, :]
    live_rows = bank_mask.reshape(N_CLIP, CLIPS_DEV, BANK) == 1
    allowed = member.reshape(N_CLIP, BOX_GROUP, CLIPS_DEV)[:, :, :, None] & live_rows[:, None, :, :]
    allowed = allowed.reshape(N_CLIP, BOX_GROUP, CLIPS_DEV * BANK)
    constants = (bank_feats.astype(jnp.float32), allowed, roi_weight, box_valid.astype(jnp.float32), labels.astype(jnp.float32))
    params = (clip_input.astype(jnp.float32), temporal.astype(jnp.float32), spatial.astype(jnp.float32), expand.astype(jnp.float32), mid_gain, mid_shift, out_gain, out_shift, short_weight.astype(jnp.float32), bank_weight.astype(jnp.float32), block_weight.astype(jnp.float32), norm_gain, norm_shift, class_weight.astype(jnp.float32))
    loss, pullback, scores = jax.vjp(partial(forward, *constants), *params, has_aux=True)
    gradients = pullback(jnp.ones((), jnp.float32))
    return (scores, gradients[0], gradients[1], gradients[2], gradients[3], gradients[4], gradients[5], gradients[6], gradients[7], gradients[8], gradients[9], gradients[10], gradients[11], gradients[12], gradients[13])
```

```python
import math

import jax
import jax.numpy as jnp
from jax import lax
from jax.sharding import PartitionSpec as P

SAMPLES = 14
LANES = 128
EPSILON = 1e-05
F32 = jnp.float32
BF16 = jnp.bfloat16


def dot(left, right, dims):
    return lax.dot_general(left, right, (dims, ((), ())), preferred_element_type=F32)


def mm(left, right):
    return dot(left, right, ((1,), (0,)))


def mm_nt(left, right):
    return dot(left, right, ((1,), (1,)))


def mm_tn(left, right):
    return dot(left, right, ((0,), (0,)))


def swap(values, axis, mask):
    count = lax.axis_size(axis)
    return lax.ppermute(values, axis, [(i, i ^ mask) for i in range(count)])


def tree_sum(parts):
    while len(parts) > 1:
        parts = [parts[i] + parts[i + 1] for i in range(0, len(parts), 2)]
    return parts[0]


def exchange(piece_of, axis, step, count, place):
    got = [piece_of(place)]
    for shift in range(1, count):
        got.append(swap(piece_of(place ^ shift), axis, shift * step))
    return got


def join_lanes(parts, place):
    count = len(parts)
    blocks = []
    for block in range(count):
        chosen = parts[0]
        for shift in range(1, count):
            chosen = jnp.where(place == (block ^ shift), parts[shift], chosen)
        blocks.append(chosen)
    return jnp.concatenate(blocks, axis=-1).astype(F32)


def pad_rows(values, rows):
    return jnp.pad(values, ((0, rows - values.shape[0]), (0, 0)))


def axis_weights(low_edge, high_edge, cell_count, first_cell, span_count):
    samples = (jnp.arange(SAMPLES, dtype=F32) + 0.5) / SAMPLES
    start_pos = low_edge.astype(F32) * 0.25
    extent = (high_edge - low_edge).astype(F32) * 0.25
    points = start_pos[:, None] + extent[:, None] * samples[None, :]
    points = jnp.clip(points - 0.5, 0.0, cell_count - 1.0)
    centers = (first_cell + jnp.arange(span_count, dtype=jnp.int32)).astype(F32)
    tents = jnp.maximum(0.0, 1.0 - jnp.abs(points[:, :, None] - centers[None, None, :]))
    return jnp.mean(tents, axis=1)


def box_weights(coords, clip_local, first_row, row_count, rows_total, clip_count, col_count):
    along_rows = axis_weights(coords[:, 0], coords[:, 1], rows_total, first_row, row_count)
    along_cols = axis_weights(coords[:, 2], coords[:, 3], col_count, 0, col_count)
    member = (clip_local[:, None] == jnp.arange(clip_count, dtype=jnp.int32)[None, :]).astype(F32)
    product = along_rows[:, None, :, None] * along_cols[:, None, None, :] * member[:, :, None, None]
    return product.astype(BF16)


def silu_slope(value_in):
    gate = jax.nn.sigmoid(value_in)
    return gate * (1.0 + value_in * (1.0 - gate))


def block_forward(stream, weights, gain_row, shift_row, memory, allowed, score_scale):
    stream_low = stream.astype(BF16)
    query = mm(stream_low, weights[0]).astype(BF16)
    query_key = mm_nt(query, weights[1]).astype(BF16)
    raw = mm_nt(query_key, memory)
    masked = jnp.where(allowed, raw * score_scale, -jnp.inf)
    peak = jnp.max(masked, axis=1, keepdims=True)
    exponent = jnp.exp(masked - peak)
    attention = exponent / jnp.sum(exponent, axis=1, keepdims=True)
    mixed = mm(attention.astype(BF16), memory).astype(BF16)
    attended = mm(mixed, weights[2])
    centred = attended - jnp.mean(attended, axis=1, keepdims=True)
    inverse = lax.rsqrt(jnp.mean(centred * centred, axis=1, keepdims=True) + EPSILON)
    hatted = centred * inverse
    normed = hatted * gain_row + shift_row
    hidden = jax.nn.silu(normed).astype(BF16)
    stream = stream + mm(hidden, weights[3])
    return stream, (stream_low, query, query_key, attention, mixed, hatted, inverse, normed, hidden)


def block_backward(back_stream, stored, weights, gain_row, memory, score_scale):
    stream_low, query, query_key, attention, mixed, hatted, inverse, normed, hidden = stored
    back_branch = back_stream.astype(BF16)
    back_normed = mm_nt(back_branch, weights[3]) * silu_slope(normed)
    gain_grad = jnp.sum(back_normed * hatted, axis=0)
    shift_grad = jnp.sum(back_normed, axis=0)
    back_hat = back_normed * gain_row
    back_attended = inverse * (
        back_hat
        - jnp.mean(back_hat, axis=1, keepdims=True)
        - hatted * jnp.mean(back_hat * hatted, axis=1, keepdims=True)
    )
    back_att_low = back_attended.astype(BF16)
    back_mixed = mm_nt(back_att_low, weights[2]).astype(BF16)
    back_attention = mm_nt(back_mixed, memory)
    inner = jnp.sum(attention * back_attention, axis=1, keepdims=True)
    back_raw = (attention * (back_attention - inner) * score_scale).astype(BF16)
    back_key_mix = mm(back_raw, memory).astype(BF16)
    back_query = mm(back_key_mix, weights[1]).astype(BF16)
    stream_in = back_stream + mm_nt(back_query, weights[0])
    lefts = (stream_low, back_key_mix, mixed, hidden)
    rights = (back_query, query, back_att_low, back_branch)
    return stream_in, lefts, rights, gain_grad, shift_grad, back_raw, back_mixed


def body(
    clip_input,
    temporal,
    spatial,
    expand,
    mid_gain,
    mid_shift,
    out_gain,
    out_shift,
    short_weight,
    bank_weight,
    block_weight,
    norm_gain,
    norm_shift,
    class_weight,
    bank_feats,
    bank_mask,
    box_coords,
    box_clip,
    box_valid,
    labels,
):
    row = lax.axis_index("row")
    group = lax.axis_index("clip")
    row_size = lax.axis_size("row")
    clip_size = lax.axis_size("clip")
    core = row % 2
    chip = row // 2
    chips = row_size // 2
    clips, frames, rows_local, cols, channels = clip_input.shape
    mid = temporal.shape[2]
    width = short_weight.shape[1]
    classes = class_weight.shape[1]
    cells = clips * frames * cols
    boxes = box_coords.shape[0]
    box_local = labels.shape[0]
    slots_local = bank_feats.shape[1]
    score_scale = 1.0 / math.sqrt(width)
    part = mid // clip_size

    feats = bank_feats.reshape(clips * slots_local, channels)
    memory_own = mm(feats, bank_weight).astype(BF16).reshape(clips, slots_local, width)
    memory = lax.all_gather(memory_own, "row", axis=1, tiled=True).reshape(-1, width)

    source = clip_input.reshape(cells, channels)
    halves = source.reshape(cells, chips, 2, channels // row_size)
    keep = lax.dynamic_index_in_dim(halves, core, 2, False).reshape(cells, channels // 2)
    send = lax.dynamic_index_in_dim(halves, 1 - core, 2, False).reshape(cells, channels // 2)
    pair_input = jnp.concatenate([keep, swap(send, "row", 1)], axis=0)
    wide_input = [pair_input] + [swap(pair_input, "clip", s) for s in range(1, clip_size)]

    framed = jnp.pad(
        clip_input.reshape(clips, frames, cols, channels), ((0, 0), (1, 1), (0, 0), (0, 0))
    )
    temporal_sum = None
    for offset in range(3):
        term = mm(framed[:, offset : offset + frames].reshape(cells, channels), temporal[offset])
        temporal_sum = term if temporal_sum is None else temporal_sum + term
    temporal_arg = temporal_sum * mid_gain[0] + mid_shift[0]
    temporal_out = jax.nn.silu(temporal_arg).astype(BF16)

    def halo(values):
        ends = row_size - 1
        above = lax.ppermute(values, "row", [(i, i + 1) for i in range(ends)])
        below = lax.ppermute(values, "row", [(i + 1, i) for i in range(ends)])
        return above, values, below

    def windows(values):
        padded = jnp.pad(
            values.reshape(clips, frames, cols, -1), ((0, 0), (0, 0), (1, 1), (0, 0))
        )
        return [padded[:, :, j : j + cols].reshape(cells, -1) for j in range(3)]

    plane_rows = halo(temporal_out)
    plane_sum = None
    for i in (1, 0, 2):
        term = mm(
            jnp.concatenate(windows(plane_rows[i]), axis=1), spatial[i].reshape(3 * mid, mid)
        )
        plane_sum = term if plane_sum is None else plane_sum + term
    plane_arg = plane_sum * mid_gain[1] + mid_shift[1]
    plane_out = jax.nn.silu(plane_arg).astype(BF16)
    expand_sum = mm(plane_out, expand)
    final_arg = expand_sum * out_gain + out_shift + source.astype(F32)
    pooled = jnp.mean(
        jax.nn.silu(final_arg).reshape(clips, frames, cols, channels), axis=1
    ).astype(BF16)
    pooled = pooled.reshape(clips * cols, channels)

    def half_lanes(values, which):
        split = values.reshape(values.shape[0], chips, 2, values.shape[1] // row_size)
        return lax.dynamic_index_in_dim(split, which, 2, False).reshape(
            values.shape[0], values.shape[1] // 2
        )

    stacked_rows = jnp.concatenate(plane_rows, axis=0)
    pair_rows = jnp.stack(
        [
            half_lanes(stacked_rows, core),
            swap(half_lanes(stacked_rows, 1 - core), "row", 1),
        ]
    )
    pair_plane = jnp.concatenate([plane_out, swap(plane_out, "row", 1)], axis=0)

    clip_group = box_clip - group * clips
    weights = box_weights(
        box_coords, clip_group, row * rows_local, rows_local, rows_local * row_size, clips, cols
    ).reshape(boxes, clips * cols)
    partial_low = mm(weights, pooled).astype(BF16)
    joint_weight = jnp.concatenate([short_weight, class_weight[:channels]], axis=1)
    joint_width = -(-(width + classes) // LANES) * LANES
    joint_weight = jnp.pad(joint_weight, ((0, 0), (0, joint_width - width - classes)))
    projected = mm(partial_low, joint_weight).reshape(2, boxes // 2, joint_width)
    mine = lax.dynamic_index_in_dim(projected, core, 0, False)
    other = lax.dynamic_index_in_dim(projected, 1 - core, 0, False)
    half_sum = mine + swap(other.astype(BF16), "row", 1).astype(F32)
    facts = jnp.concatenate([labels.astype(BF16), box_valid.astype(BF16)[:, None]], axis=1)
    facts = jnp.pad(facts, ((0, 0), (0, joint_width - facts.shape[1])))
    payload = jnp.concatenate([half_sum.astype(BF16), facts], axis=0)
    heard = [payload] + [swap(payload, "row", 2 * s) for s in range(1, chips)]
    half_total = tree_sum([item[: boxes // 2].astype(F32) for item in heard])
    facts_heard = jnp.stack([item[boxes // 2 :] for item in heard])
    facts_other = swap(facts_heard, "row", 1)
    half_other = swap(half_total, "row", 1)
    total = jnp.where(
        core == 0,
        jnp.concatenate([half_total, half_other], axis=0),
        jnp.concatenate([half_other, half_total], axis=0),
    )
    both = jnp.where(
        core == 0,
        jnp.stack([facts_heard, facts_other], axis=1),
        jnp.stack([facts_other, facts_heard], axis=1),
    )
    in_order = []
    for place in range(chips):
        chosen = both[0]
        for shift in range(1, chips):
            chosen = jnp.where(chip == (place ^ shift), both[shift], chosen)
        in_order.append(chosen)
    facts_all = jnp.concatenate(in_order, axis=0).reshape(boxes, joint_width).astype(F32)
    labels_all = facts_all[:, :classes]
    valid_all = facts_all[:, classes : classes + 1]

    own_short = channels // row_size
    cat = channels + width
    own_class = cat // row_size
    partial_wide = jnp.pad(partial_low, ((0, 0), (0, width)))
    column_pieces = jnp.concatenate(
        [
            partial_low.reshape(boxes, row_size, own_short),
            partial_wide.reshape(boxes, row_size, own_class),
        ],
        axis=2,
    )
    columns = lax.psum_scatter(
        column_pieces.transpose(1, 0, 2), "row", scatter_dimension=0, tiled=False
    )
    short_columns = columns[:, :own_short]
    class_columns = columns[:, own_short:]

    live = (bank_mask == 1).reshape(-1)
    slot_clip = jnp.repeat(
        jnp.arange(clips, dtype=jnp.int32),
        slots_local * row_size,
        total_repeat_length=clips * slots_local * row_size,
    )
    allowed = (clip_group[:, None] == slot_clip[None, :]) & live[None, :]
    stream = total[:, :width]
    stored = []
    for n in range(2):
        stream, kept = block_forward(
            stream, block_weight[n], norm_gain[n], norm_shift[n], memory, allowed, score_scale
        )
        stored.append(kept)
    stream_low = stream.astype(BF16)
    logits = total[:, width : width + classes] + mm(stream_low, class_weight[channels:])
    scores_all = jax.nn.sigmoid(logits)
    scores = lax.dynamic_slice_in_dim(scores_all, row * box_local, box_local, 0)
    back_logits = ((scores_all - labels_all) * valid_all / (clips * clip_size)).astype(BF16)
    back_stream = mm_nt(back_logits, class_weight[channels:])
    block_parts = [None, None]
    norm_parts = [None, None]
    back_memory = None
    member_own = (
        clip_group[:, None, None] == jnp.arange(clips, dtype=jnp.int32)[None, :, None]
    )

    def own_slots(values):
        grid = values.reshape(boxes, clips, slots_local * row_size)
        return lax.dynamic_slice_in_dim(grid, row * slots_local, slots_local, 2).reshape(
            boxes, clips * slots_local
        )

    for n in (1, 0):
        back_stream, lefts, rights, gain_grad, shift_grad, back_raw, back_mixed = block_backward(
            back_stream, stored[n], block_weight[n], norm_gain[n], memory, score_scale
        )
        grads = []
        for left, right in zip(lefts, rights):
            own = lax.dynamic_slice_in_dim(left, row * (width // row_size), width // row_size, 1)
            grads.append(mm_tn(own, right))
        block_parts[n] = jnp.concatenate(grads, axis=0)
        norm_parts[n] = (gain_grad, shift_grad)
        term = mm_tn(own_slots(back_raw), stored[n][2]) + mm_tn(
            own_slots(stored[n][3].astype(BF16)), back_mixed
        )
        back_memory = term if back_memory is None else back_memory + term
    back_low = back_stream.astype(BF16)
    back_boxes = mm_nt(back_logits, class_weight[:channels]) + mm_nt(back_low, short_weight)
    back_box_low = back_boxes.astype(BF16)
    back_pooled = mm_tn(weights, back_box_low).reshape(clips, 1, cols, channels)

    back_final = (
        back_pooled
        / frames
        * silu_slope(final_arg).reshape(clips, frames, cols, channels)
    ).reshape(cells, channels)
    out_gain_part = jnp.sum(back_final * expand_sum, axis=0)
    out_shift_part = jnp.sum(back_final, axis=0)
    back_expand = (back_final * out_gain).astype(BF16)
    back_plane_arg = mm_nt(back_expand, expand) * silu_slope(plane_arg)
    plane_gain_part = jnp.sum(back_plane_arg * plane_sum, axis=0)
    plane_shift_part = jnp.sum(back_plane_arg, axis=0)
    back_plane = (back_plane_arg * mid_gain[1]).astype(BF16)

    back_rows = halo(back_plane)
    back_temporal_out = None
    for i in (1, 0, 2):
        patch = jnp.concatenate(windows(back_rows[2 - i])[::-1], axis=1)
        term = dot(
            patch.reshape(cells, 3, mid), spatial[i], (((1, 2)), ((0, 2)))
        )
        back_temporal_out = term if back_temporal_out is None else back_temporal_out + term
    back_temporal_arg = back_temporal_out * silu_slope(temporal_arg)
    temporal_gain_part = jnp.sum(back_temporal_arg * temporal_sum, axis=0)
    temporal_shift_part = jnp.sum(back_temporal_arg, axis=0)
    back_temporal = (back_temporal_arg * mid_gain[0]).astype(BF16)

    first_facts = jnp.stack([temporal_gain_part, temporal_shift_part]).astype(BF16)
    fact_rows = -(-2 * mid // part // 16) * 16
    first_facts = pad_rows(first_facts.reshape(-1, part), fact_rows)

    def temporal_piece(place):
        block = lax.dynamic_slice_in_dim(back_temporal, place * part, part, 1)
        return jnp.concatenate([block, first_facts], axis=0)

    got = exchange(temporal_piece, "clip", 1, clip_size, group)
    got_own = jnp.stack(got)
    got_other = swap(got_own, "row", 1)
    temporal_partial = None
    for s in range(clip_size):
        pair = jnp.concatenate([got_own[s, :cells], got_other[s, :cells]], axis=0)
        pair = jnp.pad(
            pair.reshape(2 * clips, frames, cols, part), ((0, 0), (1, 1), (0, 0), (0, 0))
        )
        shifted = jnp.concatenate(
            [pair[:, 2 - k : 2 - k + frames].reshape(2 * cells, part) for k in range(3)], axis=1
        )
        term = mm_tn(wide_input[s], shifted)
        temporal_partial = term if temporal_partial is None else temporal_partial + term
    first_sum = tree_sum(
        [got_own[s, cells:].astype(F32) + got_other[s, cells:].astype(F32) for s in range(clip_size)]
    ).astype(BF16)
    own_rows = channels // row_size
    temporal_low = temporal_partial.astype(BF16).reshape(chips, own_rows, 3, part)

    def temporal_rows(place):
        block = lax.dynamic_index_in_dim(temporal_low, place, 0, False)
        block = jnp.concatenate([block[:, k] for k in range(3)], axis=0)
        return jnp.concatenate([block, first_sum], axis=0)

    temporal_got = tree_sum(
        [item.astype(F32) for item in exchange(temporal_rows, "row", 2, chips, chip)]
    )
    first_total = temporal_got[3 * own_rows :].reshape(-1)[: 2 * mid].reshape(2, mid)
    temporal_own = temporal_got[: 3 * own_rows].astype(BF16)

    padded_back = jnp.pad(
        back_temporal.reshape(clips, frames, cols, mid), ((0, 0), (1, 1), (0, 0), (0, 0))
    )
    input_grad = back_final
    for k in range(3):
        input_grad = input_grad + mm_nt(
            padded_back[:, 2 - k : 2 - k + frames].reshape(cells, mid), temporal[k]
        )
    input_grad = input_grad.reshape(clip_input.shape)

    short_part = mm_tn(short_columns, back_low)
    class_cols = row * own_class + jnp.arange(own_class, dtype=jnp.int32)
    stream_cols = lax.dynamic_slice_in_dim(
        jnp.pad(stream_low, ((0, 0), (channels, 0))), row * own_class, own_class, 1
    )
    joined_columns = jnp.where(class_cols[None, :] < channels, class_columns, stream_cols)
    class_part = mm_tn(joined_columns, back_logits)
    class_part = jnp.pad(class_part, ((0, 0), (0, -(-classes // part) * part - classes)))
    class_shape = class_part.shape
    class_part = class_part.reshape(-1, part)
    own_norm = width // row_size
    norm_stack = jnp.stack(
        [norm_parts[0][0], norm_parts[1][0], norm_parts[0][1], norm_parts[1][1]]
    )
    norm_own = lax.dynamic_slice_in_dim(norm_stack, row * own_norm, own_norm, 1)
    norm_rows = -(-4 * own_norm // part)
    norm_flat = jnp.pad(norm_own.reshape(-1), (0, norm_rows * part - 4 * own_norm))
    norm_flat = pad_rows(norm_flat.reshape(norm_rows, part), -(-norm_rows // 16) * 16)
    expand_send = half_lanes(back_expand, 1 - core)
    pair_expand = jnp.concatenate(
        [half_lanes(back_expand, core), swap(expand_send, "row", 1)], axis=0
    )
    expand_partial = mm_tn(pair_expand, pair_plane)
    wide_part = jnp.concatenate(
        [expand_partial, block_parts[0], block_parts[1], short_part], axis=0
    ).astype(BF16)
    shared = jnp.concatenate([class_part, norm_flat], axis=0).astype(BF16)

    def box_piece(place):
        block = lax.dynamic_slice_in_dim(wide_part, place * part, part, 1)
        return jnp.concatenate([block, shared], axis=0)

    box_got = tree_sum(
        [item.astype(F32) for item in exchange(box_piece, "clip", 1, clip_size, group)]
    )
    expand_rows = channels // 2
    wide_rows = wide_part.shape[0]
    expand_low = box_got[:expand_rows].astype(BF16).reshape(chips, own_rows, part)

    def expand_piece(place):
        return lax.dynamic_index_in_dim(expand_low, place, 0, False)

    expand_own = tree_sum(
        [item.astype(F32) for item in exchange(expand_piece, "row", 2, chips, chip)]
    ).astype(BF16)
    box_own = jnp.concatenate(
        [expand_own, box_got[expand_rows:wide_rows].astype(BF16)], axis=0
    )
    box_full = join_lanes(
        [box_own] + [swap(box_own, "clip", s) for s in range(1, clip_size)], group
    )
    class_grad = box_got[wide_rows : wide_rows + class_part.shape[0]].reshape(class_shape)
    class_grad = class_grad[:, :classes]
    norm_got = box_got[wide_rows + class_part.shape[0] :].reshape(-1)[: 4 * own_norm]
    norm_got = norm_got.reshape(4, own_norm)

    bank_part = mm_tn(feats, back_memory.astype(BF16))
    bank_rows = lax.psum_scatter(
        bank_part.astype(BF16), "row", scatter_dimension=0, tiled=True
    )
    second_facts = jnp.concatenate(
        [
            out_gain_part.reshape(-1, mid),
            out_shift_part.reshape(-1, mid),
            plane_gain_part[None],
            plane_shift_part[None],
        ],
        axis=0,
    )
    fact_count = second_facts.shape[0]
    second_facts = pad_rows(second_facts.astype(BF16), -(-fact_count // 16) * 16)
    plane_payload = jnp.concatenate([back_plane, second_facts], axis=0)
    plane_other = swap(plane_payload, "row", 1)
    second_sum = (
        second_facts.astype(F32) + plane_other[cells:].astype(F32)
    ).astype(BF16).reshape(-1, part)
    spatial_parts = []
    row_blocks = pair_rows.reshape(2, 3, cells, mid // 2)
    plane_pair = jnp.concatenate([back_plane, plane_other[:cells]], axis=0)
    for i in range(3):
        wide = jnp.concatenate(
            [
                jnp.concatenate(windows(row_blocks[0, i]), axis=1),
                jnp.concatenate(windows(row_blocks[1, i]), axis=1),
            ],
            axis=0,
        )
        spatial_parts.append(mm_tn(wide, plane_pair))
    spatial_partial = jnp.concatenate(spatial_parts, axis=0).astype(BF16)

    def spatial_piece(place):
        block = lax.dynamic_slice_in_dim(spatial_partial, place * part, part, 1)
        bank_block = lax.dynamic_slice_in_dim(bank_rows, place * part, part, 1)
        return jnp.concatenate([block, bank_block, second_sum], axis=0)

    spatial_got = tree_sum(
        [item.astype(F32) for item in exchange(spatial_piece, "clip", 1, clip_size, group)]
    )
    spatial_count = spatial_partial.shape[0]
    own_mid = mid // row_size
    bank_own = spatial_got[spatial_count : spatial_count + own_rows].astype(BF16)
    second_low = spatial_got[spatial_count + own_rows :].astype(BF16)
    spatial_low = spatial_got[:spatial_count].astype(BF16).reshape(9, chips, own_mid, part)

    def spatial_rows_piece(place):
        block = lax.dynamic_index_in_dim(spatial_low, place, 1, False).reshape(-1, part)
        return jnp.concatenate([block, second_low], axis=0)

    spatial_own = tree_sum(
        [item.astype(F32) for item in exchange(spatial_rows_piece, "row", 2, chips, chip)]
    )
    second_total = spatial_own[9 * own_mid :].reshape(-1, mid)
    last_own = jnp.concatenate(
        [spatial_own[: 9 * own_mid].astype(BF16), bank_own], axis=0
    )
    last_full = join_lanes(
        [last_own] + [swap(last_own, "clip", s) for s in range(1, clip_size)], group
    )
    temporal_full = join_lanes(
        [temporal_own] + [swap(temporal_own, "clip", s) for s in range(1, clip_size)], group
    )

    temporal_grad = temporal_full.reshape(3, own_rows, mid)
    spatial_grad = last_full[: 9 * own_mid].reshape(3, 3, own_mid, mid)
    bank_grad = last_full[9 * own_mid :]
    expand_grad = box_full[:own_rows].T
    block_grad = box_full[own_rows : own_rows + 8 * own_mid].reshape(2, 4, own_mid, width)
    short_grad = box_full[own_rows + 8 * own_mid :]
    wide_count = channels // mid
    out_gain_all = second_total[:wide_count].reshape(-1)
    out_shift_all = second_total[wide_count : 2 * wide_count].reshape(-1)
    out_gain_grad = lax.dynamic_slice_in_dim(out_gain_all, row * own_rows, own_rows, 0)
    out_shift_grad = lax.dynamic_slice_in_dim(out_shift_all, row * own_rows, own_rows, 0)
    gain_all = jnp.stack([first_total[0], second_total[2 * wide_count]])
    shift_all = jnp.stack([first_total[1], second_total[2 * wide_count + 1]])
    mid_gain_grad = lax.dynamic_slice_in_dim(gain_all, row * own_mid, own_mid, 1)
    mid_shift_grad = lax.dynamic_slice_in_dim(shift_all, row * own_mid, own_mid, 1)
    return (
        scores,
        input_grad,
        temporal_grad,
        spatial_grad,
        expand_grad,
        mid_gain_grad,
        mid_shift_grad,
        out_gain_grad,
        out_shift_grad,
        short_grad,
        bank_grad,
        block_grad,
        norm_got[:2],
        norm_got[2:],
        class_grad,
    )


def solution(mesh):
    whole = P()
    in_specs = (
        (P("clip", None, "row", None, None),)
        + (whole,) * 13
        + (
            P("clip", "row", None),
            P("clip", None),
            P("clip", None),
            P("clip"),
            P(("clip", "row")),
            P(("clip", "row"), None),
        )
    )
    out_specs = (
        P(("clip", "row"), None),
        P("clip", None, "row", None, None),
        P(None, "row", None),
        P(None, None, "row", None),
        P(None, "row"),
        P(None, "row"),
        P(None, "row"),
        P("row"),
        P("row"),
        P("row", None),
        P("row", None),
        P(None, None, "row", None),
        P(None, "row"),
        P(None, "row"),
        P("row", None),
    )
    return jax.shard_map(body, mesh=mesh, in_specs=in_specs, out_specs=out_specs, check_vma=False)
```

```python
import math

import jax
import jax.numpy as jnp
from jax import lax
from jax.experimental import pallas as pl
from jax.experimental.pallas import tpu as pltpu
from jax.sharding import PartitionSpec as P

SAMPLES = 14
LANES = 128
EPSILON = 1e-05
F32 = jnp.float32
BF16 = jnp.bfloat16


def dot(left, right, dims):
    return lax.dot_general(left, right, (dims, ((), ())), preferred_element_type=F32)


def mm(left, right):
    return dot(left, right, ((1,), (0,)))


def mm_nt(left, right):
    return dot(left, right, ((1,), (1,)))


def mm_tn(left, right):
    return dot(left, right, ((0,), (0,)))


def swap(values, axis, mask):
    count = lax.axis_size(axis)
    return lax.ppermute(values, axis, [(i, i ^ mask) for i in range(count)])


def tree_sum(parts):
    while len(parts) > 1:
        parts = [parts[i] + parts[i + 1] for i in range(0, len(parts), 2)]
    return parts[0]


def exchange(piece_of, axis, step, count, place):
    got = [piece_of(place)]
    for shift in range(1, count):
        got.append(swap(piece_of(place ^ shift), axis, shift * step))
    return got


def join_lanes(parts, place):
    count = len(parts)
    blocks = []
    for block in range(count):
        chosen = parts[0]
        for shift in range(1, count):
            chosen = jnp.where(place == (block ^ shift), parts[shift], chosen)
        blocks.append(chosen)
    return jnp.concatenate(blocks, axis=-1).astype(F32)


def pad_rows(values, rows):
    return jnp.pad(values, ((0, rows - values.shape[0]), (0, 0)))


def axis_weights(low_edge, high_edge, cell_count, first_cell, span_count):
    samples = (jnp.arange(SAMPLES, dtype=F32) + 0.5) / SAMPLES
    start_pos = low_edge.astype(F32) * 0.25
    extent = (high_edge - low_edge).astype(F32) * 0.25
    points = start_pos[:, None] + extent[:, None] * samples[None, :]
    points = jnp.clip(points - 0.5, 0.0, cell_count - 1.0)
    centers = (first_cell + jnp.arange(span_count, dtype=jnp.int32)).astype(F32)
    tents = jnp.maximum(0.0, 1.0 - jnp.abs(points[:, :, None] - centers[None, None, :]))
    return jnp.mean(tents, axis=1)


def box_weights(coords, clip_local, first_row, row_count, rows_total, clip_count, col_count):
    along_rows = axis_weights(coords[:, 0], coords[:, 1], rows_total, first_row, row_count)
    along_cols = axis_weights(coords[:, 2], coords[:, 3], col_count, 0, col_count)
    member = (clip_local[:, None] == jnp.arange(clip_count, dtype=jnp.int32)[None, :]).astype(F32)
    product = along_rows[:, None, :, None] * along_cols[:, None, None, :] * member[:, :, None, None]
    return product.astype(BF16)


def silu_slope(value_in):
    gate = jax.nn.sigmoid(value_in)
    return gate * (1.0 + value_in * (1.0 - gate))


VMEM = pl.BlockSpec(memory_space=pltpu.VMEM)
SMEM = pl.BlockSpec(memory_space=pltpu.SMEM)
MIB = 1024 * 1024


def shape_of(shape, dtype):
    return jax.ShapeDtypeStruct(shape, dtype)


def run(kernel, outs, ins, grid=(), in_specs=None, out_specs=None, scratch=(), mib=24, flops=0):
    moved = sum(math.prod(v.shape) * v.dtype.itemsize for v in (*ins, *outs))
    return pl.pallas_call(
        kernel,
        grid=grid,
        out_shape=tuple(outs),
        in_specs=in_specs or [VMEM] * len(ins),
        out_specs=tuple(out_specs or [VMEM] * len(outs)),
        scratch_shapes=list(scratch),
        compiler_params=pltpu.CompilerParams(vmem_limit_bytes=mib * MIB),
        cost_estimate=pl.CostEstimate(flops=flops, bytes_accessed=moved, transcendentals=0),
    )(*ins)


def frame_shift(values, clips, step):
    grid = values.reshape(clips, -1, values.shape[1])
    rows = grid.shape[1]
    zeros = jnp.zeros((clips, abs(step), values.shape[1]), values.dtype)
    if step > 0:
        moved = jnp.concatenate([zeros, grid[:, : rows - step]], axis=1)
    else:
        moved = jnp.concatenate([grid[:, -step:], zeros], axis=1)
    return moved.reshape(values.shape)


def col_shift(values, cols, step):
    col = lax.broadcasted_iota(jnp.int32, (values.shape[0], 1), 0) % cols
    edge = 0 if step > 0 else cols - 1
    rows = values.shape[0]
    return jnp.where(col == edge, 0.0, pltpu.roll(values, step % rows, 0))


def split_halves(core, values, keep_ref, send_ref, lanes):
    for block in range(values.shape[1] // (2 * lanes)):
        first = values[:, 2 * block * lanes : (2 * block + 1) * lanes]
        second = values[:, (2 * block + 1) * lanes : (2 * block + 2) * lanes]
        place = slice(block * lanes, (block + 1) * lanes)

        @pl.when(core == 0)
        def _():
            keep_ref[:, place] = first
            send_ref[:, place] = second

        @pl.when(core != 0)
        def _():
            keep_ref[:, place] = second
            send_ref[:, place] = first


def temporal_kernel(clips, cols, lanes, pos, x, w, gain, shift, keep, send, total, out):
    step = pl.program_id(0)
    values = x[...]
    split_halves(pos[0], values, keep, send, lanes)
    term = mm(values, w[1])
    term = term + frame_shift(mm(values, w[0]), clips, cols)
    term = term + frame_shift(mm(values, w[2]), clips, -cols)

    @pl.when(step == 0)
    def _():
        total[...] = term

    @pl.when(step > 0)
    def _():
        total[...] += term

    @pl.when(step == pl.num_programs(0) - 1)
    def _():
        arg = total[...] * gain[...] + shift[...]
        out[...] = (arg * jax.nn.sigmoid(arg)).astype(BF16)


def plane_rows_sum(rows, weights, cols):
    sides = []
    for j in range(3):
        term = None
        for values, kernel in zip(rows, weights):
            part = mm(values, kernel[j])
            term = part if term is None else term + part
        sides.append(term)
    return sides[1] + col_shift(sides[0], cols, 1) + col_shift(sides[2], cols, -1)


def plane_own_kernel(cols, own, w, out):
    out[...] = plane_rows_sum([own[...]], [w[1]], cols)


def plane_kernel(
    clips, frames, cols, above, below, w, part, gain, shift, expand, x, og, os, total, out, pooled
):
    @pl.when(pl.program_id(0) == 0)
    def _():
        whole = part[...] + plane_rows_sum([above[...], below[...]], [w[0], w[2]], cols)
        total[...] = whole
        arg = whole * gain[...] + shift[...]
        out[...] = (arg * jax.nn.sigmoid(arg)).astype(BF16)

    arg = mm(out[...], expand[...]) * og[...] + os[...] + x[...].astype(F32)
    active = arg * jax.nn.sigmoid(arg)
    summed = jnp.sum(active.reshape(clips, frames, cols, -1), axis=1)
    pooled[...] = (summed / frames).reshape(clips * cols, -1).astype(BF16)


def project_kernel(pos, weights, pooled, short, classes, mine, other, low, scratch):
    half = mine.shape[0]
    width = short.shape[1]
    values = mm(weights[...], pooled[...]).astype(BF16)
    low[...] = values
    scratch[:, :width] = mm(values, short[...])
    scratch[:, width:] = mm(values, classes[...])
    mine[...] = scratch[pl.ds(pos[0] * half, half), :]
    other[...] = scratch[pl.ds((1 - pos[0]) * half, half), :].astype(BF16)


def box_kernel(
    chips,
    classes,
    clip_total,
    pos,
    own,
    other,
    memory,
    tag,
    clip_of,
    weights,
    gain,
    shift,
    class_stream,
    class_box,
    short,
    roi,
    scores,
    back_pooled,
    lefts,
    rights,
    keys,
    mixes,
    stats,
    last_low,
    first_low,
    back_logits_ref,
    norms,
    total,
    facts,
    attention_ref,
):
    half = own.shape[0] // 2
    each = half // chips
    core = pos[0]
    total[pl.ds(core * half, half), :] = own[:half, :]
    total[pl.ds((1 - core) * half, half), :] = other[:half, :]
    for place in range(chips):
        rows = slice(half + place * each, half + (place + 1) * each)
        facts[pl.ds((2 * place + core) * each, each), :] = own[rows, :LANES]
        facts[pl.ds((2 * place + 1 - core) * each, each), :] = other[rows, :LANES]
    width = memory.shape[1]
    scale = 1.0 / math.sqrt(width)
    allowed = clip_of[...] == tag[...]
    stream = total[:, :width]
    kept = []
    for n in range(2):
        stream_low = stream.astype(BF16)
        query = mm(stream_low, weights[n, 0]).astype(BF16)
        query_key = mm_nt(query, weights[n, 1]).astype(BF16)
        raw = mm_nt(query_key, memory[...])
        masked = jnp.where(allowed, raw * scale, -jnp.inf)
        peak = jnp.max(masked, axis=1, keepdims=True)
        exponent = jnp.exp(masked - peak)
        whole = jnp.sum(exponent, axis=1, keepdims=True)
        attention = exponent * (1.0 / whole)
        attention_ref[n] = attention
        mixed = mm(attention.astype(BF16), memory[...]).astype(BF16)
        attended = mm(mixed, weights[n, 2])
        centred = attended - jnp.mean(attended, axis=1, keepdims=True)
        inverse = lax.rsqrt(jnp.mean(centred * centred, axis=1, keepdims=True) + EPSILON)
        hatted = centred * inverse
        normed = hatted * gain[n : n + 1, :] + shift[n : n + 1, :]
        hidden = (normed * jax.nn.sigmoid(normed)).astype(BF16)
        stream = stream + mm(hidden, weights[n, 3])
        lefts[4 * n] = stream_low
        lefts[4 * n + 2] = mixed
        lefts[4 * n + 3] = hidden
        rights[4 * n + 1] = query
        keys[n] = query_key
        kept.append((peak + jnp.log(whole), hatted, inverse, normed))
    stream_low = stream.astype(BF16)
    last_low[...] = stream_low
    logits = total[:, width:] + mm(stream_low, class_stream[...])
    chance = jax.nn.sigmoid(logits)
    scores[...] = chance
    lane = lax.broadcasted_iota(jnp.int32, chance.shape, 1)
    valid = facts[:, classes : classes + 1]
    back_logits = jnp.where(lane < classes, (chance - facts[...]) * valid / clip_total, 0.0)
    back_logits = back_logits.astype(BF16)
    back_logits_ref[...] = back_logits
    back_stream = mm_nt(back_logits, class_stream[...])
    inners = [None, None]
    for n in (1, 0):
        log_sum, hatted, inverse, normed = kept[n]
        back_branch = back_stream.astype(BF16)
        back_normed = mm_nt(back_branch, weights[n, 3]) * silu_slope(normed)
        norms[n : n + 1, :] = jnp.sum(back_normed * hatted, axis=0, keepdims=True)
        norms[n + 2 : n + 3, :] = jnp.sum(back_normed, axis=0, keepdims=True)
        back_hat = back_normed * gain[n : n + 1, :]
        back_attended = inverse * (
            back_hat
            - jnp.mean(back_hat, axis=1, keepdims=True)
            - hatted * jnp.mean(back_hat * hatted, axis=1, keepdims=True)
        )
        back_att_low = back_attended.astype(BF16)
        back_mixed = mm_nt(back_att_low, weights[n, 2]).astype(BF16)
        attention = attention_ref[n]
        back_attention = mm_nt(back_mixed, memory[...])
        inner = jnp.sum(attention * back_attention, axis=1, keepdims=True)
        back_raw = (attention * (back_attention - inner) * scale).astype(BF16)
        back_key_mix = mm(back_raw, memory[...]).astype(BF16)
        back_query = mm(back_key_mix, weights[n, 1]).astype(BF16)
        back_stream = back_stream + mm_nt(back_query, weights[n, 0])
        lefts[4 * n + 1] = back_key_mix
        rights[4 * n] = back_query
        rights[4 * n + 2] = back_att_low
        rights[4 * n + 3] = back_branch
        mixes[n] = back_mixed
        inners[n] = inner
    lane = lax.broadcasted_iota(jnp.int32, stats.shape, 1)
    stats[...] = jnp.where(
        lane == 0,
        kept[0][0],
        jnp.where(lane == 1, kept[1][0], jnp.where(lane == 2, inners[0], inners[1])),
    )
    back_low = back_stream.astype(BF16)
    first_low[...] = back_low
    back_boxes = mm_nt(back_logits, class_box[...]) + mm_nt(back_low, short[...])
    back_pooled[...] = mm(roi[...], back_boxes.astype(BF16))


def box_grad_kernel(
    lefts, rights, keys, mixes, stats, memory, tag, clip_of, feats, pick, block, bank
):
    width = memory.shape[1]
    scale = 1.0 / math.sqrt(width)
    allowed = clip_of[...] == tag[...]
    back_memory = None
    for n in range(2):
        raw = mm_nt(keys[n], memory[...])
        attention = jnp.where(allowed, jnp.exp(raw * scale - stats[:, n : n + 1]), 0.0)
        back_attention = mm_nt(mixes[n], memory[...])
        back_raw = (attention * (back_attention - stats[:, n + 2 : n + 3]) * scale).astype(BF16)
        term = mm_tn(back_raw, keys[n]) + mm_tn(attention.astype(BF16), mixes[n])
        back_memory = term if back_memory is None else back_memory + term
    bank[...] = mm_tn(feats[...], back_memory.astype(BF16)).astype(BF16)
    own = pick.shape[1]
    for item in range(8):
        columns = mm(lefts[item], pick[...]).astype(BF16)
        block[item * own : (item + 1) * own, :] = mm_tn(columns, rights[item]).astype(BF16)


def back_plane_kernel(
    clips,
    frames,
    cols,
    lanes,
    pos,
    back_pooled,
    x,
    plane_out,
    expand,
    og,
    os,
    plane_sum,
    gain,
    shift,
    back_final,
    keep,
    send,
    back_plane,
    facts,
    acc,
    rows,
):
    step = pl.program_id(0)
    steps = pl.num_programs(0)
    cells = x.shape[0]

    @pl.when(step == 0)
    def _():
        rows[...] = jnp.zeros_like(rows)

    expand_sum = mm(plane_out[...], expand[...])
    slope = silu_slope(expand_sum * og[...] + os[...] + x[...].astype(F32))
    pooled = back_pooled[...].reshape(clips, 1, cols, -1) * (1.0 / frames)
    final = (pooled * slope.reshape(clips, frames, cols, -1)).reshape(cells, -1)
    back_final[...] = final
    rows[pl.ds(step, 1), :] = jnp.sum(final * expand_sum, axis=0, keepdims=True)
    rows[pl.ds(steps + step, 1), :] = jnp.sum(final, axis=0, keepdims=True)
    low = (final * og[...]).astype(BF16)
    split_halves(pos[0], low, keep, send, lanes)
    term = mm_nt(low, expand[...])

    @pl.when(step == 0)
    def _():
        acc[...] = term

    @pl.when(step > 0)
    def _():
        acc[...] += term

    @pl.when(step == steps - 1)
    def _():
        back_arg = acc[...] * silu_slope(plane_sum[...] * gain[...] + shift[...])
        rows[pl.ds(2 * steps, 1), :] = jnp.sum(back_arg * plane_sum[...], axis=0, keepdims=True)
        rows[pl.ds(2 * steps + 1, 1), :] = jnp.sum(back_arg, axis=0, keepdims=True)
        back_plane[...] = (back_arg * gain[...]).astype(BF16)
        facts[...] = rows[...].astype(BF16)


def back_temporal_kernel(cols, above, own, below, w, temporal_sum, gain, shift, out, facts):
    sides = []
    for j in range(3):
        term = mm_nt(below[...], w[0, j]) + mm_nt(own[...], w[1, j]) + mm_nt(above[...], w[2, j])
        sides.append(term)
    back_out = sides[1] + col_shift(sides[0], cols, -1) + col_shift(sides[2], cols, 1)
    back_arg = back_out * silu_slope(temporal_sum[...] * gain[...] + shift[...])
    facts[...] = jnp.zeros_like(facts)
    facts[0:1, :] = jnp.sum(back_arg * temporal_sum[...], axis=0, keepdims=True)
    facts[1:2, :] = jnp.sum(back_arg, axis=0, keepdims=True)
    out[...] = (back_arg * gain[...]).astype(BF16)


def input_kernel(clips, cols, back, w, final, out):
    values = back[...]
    total = final[...] + mm_nt(values, w[1])
    total = total + frame_shift(mm_nt(values, w[0]), clips, -cols)
    out[...] = total + frame_shift(mm_nt(values, w[2]), clips, cols)


def body(
    clip_input,
    temporal,
    spatial,
    expand,
    mid_gain,
    mid_shift,
    out_gain,
    out_shift,
    short_weight,
    bank_weight,
    block_weight,
    norm_gain,
    norm_shift,
    class_weight,
    bank_feats,
    bank_mask,
    box_coords,
    box_clip,
    box_valid,
    labels,
):
    row = lax.axis_index("row")
    group = lax.axis_index("clip")
    row_size = lax.axis_size("row")
    clip_size = lax.axis_size("clip")
    core = row % 2
    chip = row // 2
    chips = row_size // 2
    clips, frames, rows_local, cols, channels = clip_input.shape
    mid = temporal.shape[2]
    width = short_weight.shape[1]
    classes = class_weight.shape[1]
    cells = clips * frames * cols
    boxes = box_coords.shape[0]
    box_local = labels.shape[0]
    slots_local = bank_feats.shape[1]
    part = mid // clip_size
    steps = channels // mid
    lanes = channels // row_size
    place = jnp.stack([core]).astype(jnp.int32)
    gain_first, gain_second = mid_gain[0:1], mid_gain[1:2]
    shift_first, shift_second = mid_shift[0:1], mid_shift[1:2]
    og, os = out_gain[None], out_shift[None]

    feats = bank_feats.reshape(clips * slots_local, channels)
    memory_own = mm(feats, bank_weight).astype(BF16)
    source, memory_own = lax.optimization_barrier((clip_input.reshape(cells, channels), memory_own))
    memory = lax.all_gather(
        memory_own.reshape(clips, slots_local, width), "row", axis=1, tiled=True
    ).reshape(-1, width)

    def fixed(*shape):
        return pl.BlockSpec(shape, lambda i: (0,) * len(shape))

    def across(height, lane_count):
        return pl.BlockSpec((height, lane_count), lambda i: (0, i))

    half_shape = shape_of((cells, channels // 2), BF16)
    kept_input, sent_input, temporal_sum, temporal_out = run(
        lambda *refs: temporal_kernel(clips, cols, lanes, *refs),
        [half_shape, half_shape, shape_of((cells, mid), F32), shape_of((cells, mid), BF16)],
        [place, source, temporal, gain_first, shift_first],
        grid=(steps,),
        in_specs=[
            SMEM,
            across(cells, mid),
            pl.BlockSpec((3, mid, mid), lambda i: (0, i, 0)),
            fixed(1, mid),
            fixed(1, mid),
        ],
        out_specs=[
            across(cells, mid // 2),
            across(cells, mid // 2),
            fixed(cells, mid),
            fixed(cells, mid),
        ],
        mib=24,
        flops=6 * cells * channels * mid,
    )

    def halo(values):
        ends = row_size - 1
        above = lax.ppermute(values, "row", [(i, i + 1) for i in range(ends)])
        below = lax.ppermute(values, "row", [(i + 1, i) for i in range(ends)])
        return above, below

    above_row, below_row = halo(temporal_out)

    pair_input = jnp.concatenate([kept_input, swap(sent_input, "row", 1)], axis=0)

    def joint_swap(values, even_mask, odd_mask):
        pairs = []
        for c in range(clip_size):
            for r in range(row_size):
                mask = odd_mask if r % 2 else even_mask
                pairs.append((c * row_size + r, (c ^ mask) * row_size + r))
        return lax.ppermute(values, ("clip", "row"), pairs)

    crossed = clip_size == 4
    masks = [(s, s) for s in range(clip_size)]
    if crossed:
        masks = [(0, 0), (1, 2), (2, 1), (3, 3)]
        first = joint_swap(pair_input, 1, 2)
        pair_again, first = lax.optimization_barrier((pair_input, first))
        second = joint_swap(pair_again, 2, 1)
        first, second = lax.optimization_barrier((first, second))
        third = joint_swap(first, 2, 1)
        wide_input = [pair_again, first, second, third]
    else:
        wide_input = [pair_input] + [swap(pair_input, "clip", s) for s in range(1, clip_size)]

    (plane_part,) = run(
        lambda *refs: plane_own_kernel(cols, *refs),
        [shape_of((cells, mid), F32)],
        [temporal_out, spatial],
        grid=(1,),
        in_specs=[fixed(cells, mid), fixed(3, 3, mid, mid)],
        out_specs=[fixed(cells, mid)],
        mib=24,
        flops=6 * cells * mid * mid,
    )
    plane_sum, plane_out, pooled = run(
        lambda *refs: plane_kernel(clips, frames, cols, *refs),
        [
            shape_of((cells, mid), F32),
            shape_of((cells, mid), BF16),
            shape_of((clips * cols, channels), BF16),
        ],
        [
            above_row,
            below_row,
            spatial,
            plane_part,
            gain_second,
            shift_second,
            expand,
            source,
            og,
            os,
        ],
        grid=(steps,),
        in_specs=[
            fixed(cells, mid),
            fixed(cells, mid),
            fixed(3, 3, mid, mid),
            fixed(cells, mid),
            fixed(1, mid),
            fixed(1, mid),
            across(mid, mid),
            across(cells, mid),
            across(1, mid),
            across(1, mid),
        ],
        out_specs=[fixed(cells, mid), fixed(cells, mid), across(clips * cols, mid)],
        mib=32,
        flops=12 * cells * mid * mid + 2 * cells * mid * channels,
    )

    clip_group = box_clip - group * clips
    weights = box_weights(
        box_coords, clip_group, row * rows_local, rows_local, rows_local * row_size, clips, cols
    ).reshape(boxes, clips * cols)
    class_box = jnp.pad(class_weight[:channels], ((0, 0), (0, LANES - classes)))
    class_stream = jnp.pad(class_weight[channels:], ((0, 0), (0, LANES - classes)))
    half = boxes // 2
    joint = width + LANES
    mine, other, partial_low = run(
        project_kernel,
        [shape_of((half, joint), F32), shape_of((half, joint), BF16), shape_of((boxes, channels), BF16)],
        [place, weights, pooled, short_weight, class_box],
        in_specs=[SMEM] + [VMEM] * 4,
        scratch=[pltpu.VMEM((boxes, joint), F32)],
        mib=24,
        flops=2 * boxes * channels * joint,
    )
    facts = jnp.concatenate([labels.astype(BF16), box_valid.astype(BF16)[:, None]], axis=1)
    facts = jnp.pad(facts, ((0, 0), (0, joint - facts.shape[1])))
    half_sum = mine + swap(other, "row", 1).astype(F32)
    payload = jnp.concatenate([half_sum.astype(BF16), facts], axis=0)
    heard = [payload] + [swap(payload, "row", 2 * s) for s in range(1, chips)]
    half_total = tree_sum([item[:half].astype(F32) for item in heard])
    in_order = []
    for target in range(chips):
        chosen = heard[0][half:]
        for shift in range(1, chips):
            chosen = jnp.where(chip == (target ^ shift), heard[shift][half:], chosen)
        in_order.append(chosen.astype(F32))
    totals_own = jnp.concatenate([half_total] + in_order, axis=0)
    totals_other = swap(totals_own, "row", 1)

    own_short = channels // row_size
    cat = channels + width
    own_class = cat // row_size
    partial_wide = jnp.pad(partial_low, ((0, 0), (0, width)))
    column_pieces = jnp.stack(
        [
            jnp.concatenate(
                [
                    partial_low[:, r * own_short : (r + 1) * own_short],
                    partial_wide[:, r * own_class : (r + 1) * own_class],
                ],
                axis=1,
            )
            for r in range(row_size)
        ]
    )
    columns = lax.psum_scatter(column_pieces, "row", scatter_dimension=0, tiled=False)
    short_columns = columns[:, :own_short]
    class_columns = columns[:, own_short:]

    live = bank_mask == 1
    tags = jnp.where(live, jnp.arange(clips, dtype=jnp.int32)[:, None], -1)
    tags_own = lax.dynamic_slice_in_dim(tags, row * slots_local, slots_local, 1).reshape(1, -1)
    tags = tags.reshape(1, -1)
    clip_column = clip_group[:, None]
    slots = tags.shape[1]
    stream_shape = (boxes, width)
    (
        scores_all,
        back_pooled,
        lefts,
        rights,
        keys,
        mixes,
        stats,
        last_low,
        first_low,
        back_logits,
        norms,
    ) = run(
        lambda *refs: box_kernel(chips, classes, float(clips * clip_size), *refs),
        [
            shape_of((boxes, LANES), F32),
            shape_of((clips * cols, channels), F32),
            shape_of((8, *stream_shape), BF16),
            shape_of((8, *stream_shape), BF16),
            shape_of((2, *stream_shape), BF16),
            shape_of((2, *stream_shape), BF16),
            shape_of((boxes, LANES), F32),
            shape_of(stream_shape, BF16),
            shape_of(stream_shape, BF16),
            shape_of((boxes, LANES), BF16),
            shape_of((4, width), F32),
        ],
        [
            place,
            totals_own,
            totals_other,
            memory,
            tags,
            clip_column,
            block_weight,
            norm_gain,
            norm_shift,
            class_stream,
            class_box,
            short_weight,
            weights.T,
        ],
        in_specs=[SMEM] + [VMEM] * 12,
        scratch=[
            pltpu.VMEM((boxes, joint), F32),
            pltpu.VMEM((boxes, LANES), F32),
            pltpu.VMEM((2, boxes, slots), F32),
        ],
        mib=56,
        flops=16 * boxes * slots * width + 32 * boxes * width * width,
    )
    scores = lax.dynamic_slice_in_dim(scores_all, row * box_local, box_local, 0)[:, :classes]

    fact_rows = -(-(2 * steps + 2) // 16) * 16
    back_final, kept_expand, sent_expand, back_plane, second_facts = run(
        lambda *refs: back_plane_kernel(clips, frames, cols, lanes, *refs),
        [
            shape_of((cells, channels), F32),
            half_shape,
            half_shape,
            shape_of((cells, mid), BF16),
            shape_of((fact_rows, mid), BF16),
        ],
        [
            place,
            back_pooled,
            source,
            plane_out,
            expand,
            og,
            os,
            plane_sum,
            gain_second,
            shift_second,
        ],
        grid=(steps,),
        in_specs=[
            SMEM,
            across(clips * cols, mid),
            across(cells, mid),
            fixed(cells, mid),
            across(mid, mid),
            across(1, mid),
            across(1, mid),
            fixed(cells, mid),
            fixed(1, mid),
            fixed(1, mid),
        ],
        out_specs=[
            across(cells, mid),
            across(cells, mid // 2),
            across(cells, mid // 2),
            fixed(cells, mid),
            fixed(fact_rows, mid),
        ],
        scratch=[pltpu.VMEM((cells, mid), F32), pltpu.VMEM((fact_rows, mid), F32)],
        mib=32,
        flops=4 * cells * mid * channels,
    )

    back_above, back_below = halo(back_plane)
    back_temporal, first_facts = run(
        lambda *refs: back_temporal_kernel(cols, *refs),
        [shape_of((cells, mid), BF16), shape_of((8, mid), F32)],
        [
            back_above,
            back_plane,
            back_below,
            spatial,
            temporal_sum,
            gain_first,
            shift_first,
        ],
        mib=32,
        flops=18 * cells * mid * mid,
    )

    first_rows = -(-2 * mid // part // 16) * 16
    first_facts = pad_rows(first_facts[:2].astype(BF16).reshape(-1, part), first_rows)

    def temporal_piece(target):
        block = lax.dynamic_slice_in_dim(back_temporal, target * part, part, 1)
        return jnp.concatenate([block, first_facts], axis=0)

    got = [temporal_piece(group)]
    for even_mask, odd_mask in masks[1:]:
        mask = jnp.where(core == 0, even_mask, odd_mask)
        got.append(joint_swap(temporal_piece(group ^ mask), even_mask, odd_mask))
    got_own = jnp.stack(got)
    got_other = swap(got_own, "row", 1)
    other_order = [masks.index((b, a)) for a, b in masks]
    temporal_partial = None
    for s in range(clip_size):
        pair = jnp.concatenate([got_own[s, :cells], got_other[other_order[s], :cells]], axis=0)
        pair = jnp.pad(
            pair.reshape(2 * clips, frames, cols, part), ((0, 0), (1, 1), (0, 0), (0, 0))
        )
        shifted = jnp.concatenate(
            [pair[:, 2 - k : 2 - k + frames].reshape(2 * cells, part) for k in range(3)], axis=1
        )
        term = mm_tn(wide_input[s], shifted)
        temporal_partial = term if temporal_partial is None else temporal_partial + term
    first_sum = tree_sum(
        [
            got_own[s, cells:].astype(F32) + got_other[other_order[s], cells:].astype(F32)
            for s in range(clip_size)
        ]
    ).astype(BF16)
    own_rows = channels // row_size
    temporal_low = temporal_partial.astype(BF16).reshape(chips, own_rows, 3, part)

    def temporal_rows(target):
        block = lax.dynamic_index_in_dim(temporal_low, target, 0, False)
        block = jnp.concatenate([block[:, k] for k in range(3)], axis=0)
        return jnp.concatenate([block, first_sum], axis=0)

    temporal_got = tree_sum(
        [item.astype(F32) for item in exchange(temporal_rows, "row", 2, chips, chip)]
    )
    first_total = temporal_got[3 * own_rows :].reshape(-1)[: 2 * mid].reshape(2, mid)
    temporal_own = temporal_got[: 3 * own_rows].astype(BF16)

    (input_grad,) = run(
        lambda *refs: input_kernel(clips, cols, *refs),
        [shape_of((cells, channels), F32)],
        [back_temporal, temporal, back_final],
        grid=(steps,),
        in_specs=[
            fixed(cells, mid),
            pl.BlockSpec((3, mid, mid), lambda i: (0, i, 0)),
            across(cells, mid),
        ],
        out_specs=[across(cells, mid)],
        mib=24,
        flops=6 * cells * channels * mid,
    )
    input_grad = input_grad.reshape(clip_input.shape)

    own_mid = width // row_size
    pick = (
        jnp.arange(width, dtype=jnp.int32)[:, None]
        == row * own_mid + jnp.arange(own_mid, dtype=jnp.int32)[None, :]
    ).astype(BF16)
    block_part, bank_part = run(
        box_grad_kernel,
        [shape_of((8 * own_mid, width), BF16), shape_of((channels, width), BF16)],
        [
            lefts,
            rights,
            keys,
            mixes,
            stats,
            memory_own,
            tags_own,
            clip_column,
            feats,
            pick,
        ],
        mib=32,
        flops=16 * boxes * width * clips * slots_local + 2 * clips * slots_local * width * channels,
    )
    short_part = mm_tn(short_columns, first_low)
    class_cols = row * own_class + jnp.arange(own_class, dtype=jnp.int32)
    stream_cols = lax.dynamic_slice_in_dim(
        jnp.pad(last_low, ((0, 0), (channels, 0))), row * own_class, own_class, 1
    )
    joined_columns = jnp.where(class_cols[None, :] < channels, class_columns, stream_cols)
    class_part = mm_tn(joined_columns, back_logits)
    class_part = jnp.pad(class_part, ((0, 0), (0, -(-LANES // part) * part - LANES)))
    class_shape = class_part.shape
    class_part = class_part.reshape(-1, part)
    norm_own = lax.dynamic_slice_in_dim(norms, row * own_mid, own_mid, 1)
    norm_rows = -(-4 * own_mid // part)
    norm_flat = jnp.pad(norm_own.reshape(-1), (0, norm_rows * part - 4 * own_mid))
    norm_flat = pad_rows(norm_flat.reshape(norm_rows, part), -(-norm_rows // 16) * 16)
    pair_expand = jnp.concatenate([kept_expand, swap(sent_expand, "row", 1)], axis=0)
    pair_plane = jnp.concatenate([plane_out, swap(plane_out, "row", 1)], axis=0)
    expand_partial = mm_tn(pair_expand, pair_plane)
    wide_part = jnp.concatenate(
        [expand_partial.astype(BF16), block_part, short_part.astype(BF16)], axis=0
    )
    shared = jnp.concatenate([class_part, norm_flat], axis=0).astype(BF16)

    def box_piece(target):
        block = lax.dynamic_slice_in_dim(wide_part, target * part, part, 1)
        return jnp.concatenate([block, shared], axis=0)

    box_got = tree_sum(
        [item.astype(F32) for item in exchange(box_piece, "clip", 1, clip_size, group)]
    )
    expand_rows = channels // 2
    wide_rows = wide_part.shape[0]
    expand_low = box_got[:expand_rows].astype(BF16).reshape(chips, own_rows, part)
    class_grad = box_got[wide_rows : wide_rows + class_part.shape[0]].reshape(class_shape)
    class_grad = class_grad[:, :classes]
    norm_got = box_got[wide_rows + class_part.shape[0] :].reshape(-1)[: 4 * own_mid]
    norm_got = norm_got.reshape(4, own_mid)

    bank_rows = lax.psum_scatter(bank_part, "row", scatter_dimension=0, tiled=True)

    def half_lanes(values, which):
        pieces = [values[:, k * own_mid : (k + 1) * own_mid] for k in range(row_size)]
        low = jnp.concatenate(pieces[0::2], axis=1)
        high = jnp.concatenate(pieces[1::2], axis=1)
        return jnp.where(which == 0, low, high)

    stacked_rows = jnp.concatenate([above_row, temporal_out, below_row], axis=0)
    kept_rows = half_lanes(stacked_rows, core)
    other_rows = swap(half_lanes(stacked_rows, 1 - core), "row", 1)
    plane_payload = jnp.concatenate([back_plane, second_facts], axis=0)
    plane_other = swap(plane_payload, "row", 1)
    second_sum = (second_facts.astype(F32) + plane_other[cells:].astype(F32)).astype(BF16)
    second_sum = second_sum.reshape(-1, part)
    plane_pair = jnp.concatenate([back_plane, plane_other[:cells]], axis=0)
    padded_plane = jnp.pad(
        plane_pair.reshape(2 * clips * frames, cols, mid), ((0, 0), (1, 1), (0, 0))
    )
    shifted_plane = jnp.concatenate(
        [padded_plane[:, 2 - j : 2 - j + cols].reshape(2 * cells, mid) for j in range(3)], axis=1
    )
    pair_rows = jnp.concatenate(
        [
            jnp.concatenate(
                [kept_rows[i * cells : (i + 1) * cells], other_rows[i * cells : (i + 1) * cells]],
                axis=0,
            )
            for i in range(3)
        ],
        axis=1,
    )
    spatial_partial = mm_tn(pair_rows, shifted_plane).astype(BF16)
    half_mid = mid // 2

    def spatial_piece(target):
        blocks = [
            lax.dynamic_slice(
                spatial_partial, (i * half_mid, j * mid + target * part), (half_mid, part)
            )
            for i in range(3)
            for j in range(3)
        ]
        bank_block = lax.dynamic_slice_in_dim(bank_rows, target * part, part, 1)
        return jnp.concatenate(blocks + [bank_block, second_sum], axis=0)

    spatial_got = tree_sum(
        [item.astype(F32) for item in exchange(spatial_piece, "clip", 1, clip_size, group)]
    )
    spatial_count = 9 * half_mid
    bank_own = spatial_got[spatial_count : spatial_count + own_rows].astype(BF16)
    second_low = spatial_got[spatial_count + own_rows :].astype(BF16)
    spatial_low = spatial_got[:spatial_count].astype(BF16).reshape(9, chips, own_mid, part)

    def chip_piece(target):
        block = lax.dynamic_index_in_dim(spatial_low, target, 1, False).reshape(-1, part)
        expand_block = lax.dynamic_index_in_dim(expand_low, target, 0, False)
        return jnp.concatenate([block, expand_block, second_low], axis=0)

    chip_got = tree_sum(
        [item.astype(F32) for item in exchange(chip_piece, "row", 2, chips, chip)]
    )
    second_total = chip_got[9 * own_mid + own_rows :].reshape(-1, mid)
    last_own = jnp.concatenate(
        [
            chip_got[: 9 * own_mid + own_rows].astype(BF16),
            bank_own,
            box_got[expand_rows:wide_rows].astype(BF16),
        ],
        axis=0,
    )
    last_full = join_lanes(
        [last_own] + [swap(last_own, "clip", s) for s in range(1, clip_size)], group
    )
    temporal_full = join_lanes(
        [temporal_own] + [swap(temporal_own, "clip", s) for s in range(1, clip_size)], group
    )

    counts = [9 * own_mid, own_rows, own_rows, 8 * own_mid, own_rows]
    ends = [sum(counts[: k + 1]) for k in range(len(counts))]
    pieces = [last_full[end - count : end] for count, end in zip(counts, ends)]
    temporal_grad = temporal_full.reshape(3, own_rows, mid)
    spatial_grad = pieces[0].reshape(3, 3, own_mid, mid)
    expand_grad = pieces[1].T
    bank_grad = pieces[2]
    block_grad = pieces[3].reshape(2, 4, own_mid, width)
    short_grad = pieces[4]
    out_gain_all = second_total[:steps].reshape(-1)
    out_shift_all = second_total[steps : 2 * steps].reshape(-1)
    out_gain_grad = lax.dynamic_slice_in_dim(out_gain_all, row * own_rows, own_rows, 0)
    out_shift_grad = lax.dynamic_slice_in_dim(out_shift_all, row * own_rows, own_rows, 0)
    gain_all = jnp.stack([first_total[0], second_total[2 * steps]])
    shift_all = jnp.stack([first_total[1], second_total[2 * steps + 1]])
    mid_gain_grad = lax.dynamic_slice_in_dim(gain_all, row * own_mid, own_mid, 1)
    mid_shift_grad = lax.dynamic_slice_in_dim(shift_all, row * own_mid, own_mid, 1)
    return (
        scores,
        input_grad,
        temporal_grad,
        spatial_grad,
        expand_grad,
        mid_gain_grad,
        mid_shift_grad,
        out_gain_grad,
        out_shift_grad,
        short_grad,
        bank_grad,
        block_grad,
        norm_got[:2],
        norm_got[2:],
        class_grad,
    )


def solution(mesh):
    whole = P()
    in_specs = (
        (P("clip", None, "row", None, None),)
        + (whole,) * 13
        + (
            P("clip", "row", None),
            P("clip", None),
            P("clip", None),
            P("clip"),
            P(("clip", "row")),
            P(("clip", "row"), None),
        )
    )
    out_specs = (
        P(("clip", "row"), None),
        P("clip", None, "row", None, None),
        P(None, "row", None),
        P(None, None, "row", None),
        P(None, "row"),
        P(None, "row"),
        P(None, "row"),
        P("row"),
        P("row"),
        P("row", None),
        P("row", None),
        P(None, None, "row", None),
        P(None, "row"),
        P(None, "row"),
        P("row", None),
    )
    return jax.shard_map(body, mesh=mesh, in_specs=in_specs, out_specs=out_specs, check_vma=False)
```

```python
import math

import jax
import jax.numpy as jnp
from jax import lax
from jax.experimental import pallas as pl
from jax.experimental.pallas import tpu as pltpu
from jax.sharding import PartitionSpec as P

SAMPLES = 14
LANES = 128
EPSILON = 1e-05
F32 = jnp.float32
BF16 = jnp.bfloat16


def dot(left, right, dims):
    return lax.dot_general(left, right, (dims, ((), ())), preferred_element_type=F32)


def mm(left, right):
    return dot(left, right, ((1,), (0,)))


def mm_nt(left, right):
    return dot(left, right, ((1,), (1,)))


def mm_tn(left, right):
    return dot(left, right, ((0,), (0,)))


def swap(values, axis, mask):
    count = lax.axis_size(axis)
    return lax.ppermute(values, axis, [(i, i ^ mask) for i in range(count)])


def tree_sum(parts):
    while len(parts) > 1:
        parts = [parts[i] + parts[i + 1] for i in range(0, len(parts), 2)]
    return parts[0]


def step_masks(count):
    even = [1 << t for t in range(count.bit_length() - 1)]
    odd = list(even)
    for t in range(0, len(odd) - 1, 2):
        odd[t], odd[t + 1] = odd[t + 1], odd[t]
    return even, odd


def joint_swap(values, even_mask, odd_mask):
    clip_size = lax.axis_size("clip")
    row_size = lax.axis_size("row")
    pairs = []
    for c in range(clip_size):
        for r in range(row_size):
            mask = odd_mask if r % 2 else even_mask
            pairs.append((c * row_size + r, (c ^ mask) * row_size + r))
    return lax.ppermute(values, ("clip", "row"), pairs)


def place_of(code, group, core):
    even, odd = step_masks(lax.axis_size("clip"))
    first = sum(m for t, m in enumerate(even) if code >> t & 1)
    second = sum(m for t, m in enumerate(odd) if code >> t & 1)
    return group ^ (first if first == second else jnp.where(core == 0, first, second))


def give(held, t):
    return jnp.concatenate([held[code].astype(BF16) for code in held if code >> t & 1], axis=0)


def take(held, t, got):
    high = [code for code in held if code >> t & 1]
    rows = got.shape[0] // len(high)
    return {
        code ^ (1 << t): held[code ^ (1 << t)].astype(F32)
        + got[n * rows : (n + 1) * rows].astype(F32)
        for n, code in enumerate(high)
    }


def bits(count):
    return count.bit_length() - 1


def pad_rows(values, rows):
    return jnp.pad(values, ((0, rows - values.shape[0]), (0, 0)))


def axis_weights(low_edge, high_edge, cell_count, first_cell, span_count):
    samples = (jnp.arange(SAMPLES, dtype=F32) + 0.5) / SAMPLES
    start_pos = low_edge.astype(F32) * 0.25
    extent = (high_edge - low_edge).astype(F32) * 0.25
    points = start_pos[:, None] + extent[:, None] * samples[None, :]
    points = jnp.clip(points - 0.5, 0.0, cell_count - 1.0)
    centers = (first_cell + jnp.arange(span_count, dtype=jnp.int32)).astype(F32)
    tents = jnp.maximum(0.0, 1.0 - jnp.abs(points[:, :, None] - centers[None, None, :]))
    return jnp.mean(tents, axis=1)


def box_weights(coords, clip_local, first_row, row_count, rows_total, clip_count, col_count):
    along_rows = axis_weights(coords[:, 0], coords[:, 1], rows_total, first_row, row_count)
    along_cols = axis_weights(coords[:, 2], coords[:, 3], col_count, 0, col_count)
    member = (clip_local[:, None] == jnp.arange(clip_count, dtype=jnp.int32)[None, :]).astype(F32)
    product = along_rows[:, None, :, None] * along_cols[:, None, None, :] * member[:, :, None, None]
    return product.astype(BF16)


def silu_slope(value_in):
    gate = jax.nn.sigmoid(value_in)
    return gate * (1.0 + value_in * (1.0 - gate))


VMEM = pl.BlockSpec(memory_space=pltpu.VMEM)
SMEM = pl.BlockSpec(memory_space=pltpu.SMEM)
MIB = 1024 * 1024
MIB_DEFAULT = 58


def shape_of(shape, dtype):
    return jax.ShapeDtypeStruct(shape, dtype)


def run(kernel, outs, ins, grid=(), in_specs=None, out_specs=None, scratch=(), mib=MIB_DEFAULT):
    return pl.pallas_call(
        kernel,
        grid=grid,
        out_shape=tuple(outs),
        in_specs=in_specs or [VMEM] * len(ins),
        out_specs=tuple(out_specs or [VMEM] * len(outs)),
        scratch_shapes=list(scratch),
        compiler_params=pltpu.CompilerParams(vmem_limit_bytes=mib * MIB),
        cost_estimate=pl.CostEstimate(flops=0, bytes_accessed=0, transcendentals=0),
    )(*ins)


def frame_shift(values, clips, step):
    grid = values.reshape(clips, -1, values.shape[1])
    rows = grid.shape[1]
    zeros = jnp.zeros((clips, abs(step), values.shape[1]), values.dtype)
    if step > 0:
        moved = jnp.concatenate([zeros, grid[:, : rows - step]], axis=1)
    else:
        moved = jnp.concatenate([grid[:, -step:], zeros], axis=1)
    return moved.reshape(values.shape)


def col_shift(values, cols, step):
    col = lax.broadcasted_iota(jnp.int32, (values.shape[0], 1), 0) % cols
    edge = 0 if step > 0 else cols - 1
    rows = values.shape[0]
    return jnp.where(col == edge, 0.0, pltpu.roll(values, step % rows, 0))


def temporal_kernel(clips, cols, x, w, gain, shift, total, out):
    step = pl.program_id(0)
    values = x[...]
    term = mm(values, w[1])
    term = term + frame_shift(mm(values, w[0]), clips, cols)
    term = term + frame_shift(mm(values, w[2]), clips, -cols)

    @pl.when(step == 0)
    def _():
        total[...] = term

    @pl.when(step > 0)
    def _():
        total[...] += term

    @pl.when(step == pl.num_programs(0) - 1)
    def _():
        arg = total[...] * gain[0:1, :] + shift[0:1, :]
        out[...] = (arg * jax.nn.sigmoid(arg)).astype(BF16)


def plane_rows_sum(rows, weights, cols):
    sides = []
    for j in range(3):
        term = None
        for values, kernel in zip(rows, weights):
            part = mm(values, kernel[j])
            term = part if term is None else term + part
        sides.append(term)
    return sides[1] + col_shift(sides[0], cols, 1) + col_shift(sides[2], cols, -1)


def plane_own_kernel(cols, own, w, out):
    out[...] = plane_rows_sum([own[...]], [w[0]], cols)


def plane_kernel(
    clips,
    frames,
    cols,
    pos,
    above,
    below,
    first,
    last,
    part,
    gain,
    shift,
    expand,
    x,
    og,
    os,
    weights,
    short,
    classes,
    total,
    out,
    low,
    mine,
    other,
    projected,
):
    step = pl.program_id(0)

    @pl.when(step == 0)
    def _():
        whole = part[...] + plane_rows_sum([above[...], below[...]], [first[0], last[0]], cols)
        total[...] = whole
        arg = whole * gain[1:2, :] + shift[1:2, :]
        out[...] = (arg * jax.nn.sigmoid(arg)).astype(BF16)
        projected[...] = jnp.zeros_like(projected)

    arg = mm(out[...], expand[...]) * og[...] + os[...] + x[...].astype(F32)
    active = arg * jax.nn.sigmoid(arg)
    summed = jnp.sum(active.reshape(clips, frames, cols, -1), axis=1)
    pooled = (summed / frames).reshape(clips * cols, -1).astype(BF16)
    values = mm(weights[...], pooled).astype(BF16)
    lanes = low.shape[2]
    for r in range(low.shape[0]):
        low[r] = values[:, r * lanes : (r + 1) * lanes]
    width = short.shape[1]
    projected[:, :width] += mm(values, short[...])
    projected[:, width:] += mm_nt(values, classes[...])

    @pl.when(step == pl.num_programs(0) - 1)
    def _():
        half = mine.shape[0]
        mine[...] = projected[pl.ds(pos[0] * half, half), :]
        other[...] = projected[pl.ds((1 - pos[0]) * half, half), :].astype(BF16)


def slope_kernel(frames, plane_out, expand, x, og, os, sums, slope):
    expand_sum = mm(plane_out[...], expand[...])
    sums[...] = expand_sum.astype(BF16)
    slope[...] = silu_slope(expand_sum * og[...] + os[...] + x[...].astype(F32)) * (1.0 / frames)


def total_kernel(order, pos, part, got, *refs):
    facts, out = refs[:-1], refs[-1]
    rows = part.shape[0]
    side = pos[1] % 2
    out[pl.ds(side * rows, rows), :] = part[...]
    out[pl.ds((1 - side) * rows, rows), :] = got[:rows, :].astype(F32)
    each = facts[0].shape[0]
    near = len(facts)
    for n, code in enumerate(order):
        start = 2 * rows + code * each
        if n < near:
            out[start : start + each, :] = facts[n][...].astype(F32)
        else:
            other = rows + (n - near) * each
            out[start : start + each, :] = got[other : other + each, :].astype(F32)


def box_kernel(
    chips,
    classes,
    clip_total,
    pos,
    own,
    other,
    memory,
    bias,
    clip_of,
    weights,
    gain,
    shift,
    class_stream,
    class_box,
    short,
    roi,
    scores,
    back_pooled,
    lefts,
    rights,
    keys,
    mixes,
    stats,
    last_low,
    first_low,
    back_logits_ref,
    norms,
    total,
    facts,
    attention_ref,
):
    half = total.shape[0] // 2
    each = half // chips // 2
    core, chip = pos[0], pos[1]
    total[pl.ds(core * half, half), :] = own[:half, :]
    total[pl.ds((1 - core) * half, half), :] = other[:half, :]
    for s in range(chips):
        rows = slice(half + s * each, half + (s + 1) * each)
        base = 4 * (chip ^ s)
        for part in range(2):
            lanes = slice(part * LANES, (part + 1) * LANES)
            facts[pl.ds((base + 2 * core + part) * each, each), :] = own[rows, lanes]
            facts[pl.ds((base + 2 * (1 - core) + part) * each, each), :] = other[rows, lanes]
    width = memory.shape[1]
    scale = 1.0 / math.sqrt(width)
    clips, slots = bias.shape
    clip_rows = clip_of[...]

    def select(values):
        chosen = values[:, :slots]
        for c in range(1, clips):
            chosen = jnp.where(clip_rows == c, values[:, c * slots : (c + 1) * slots], chosen)
        return chosen

    def spread(values):
        return jnp.concatenate(
            [jnp.where(clip_rows == c, values, 0.0).astype(BF16) for c in range(clips)], axis=1
        )

    dead = jnp.broadcast_to(bias[0:1, :], (clip_rows.shape[0], slots))
    for c in range(1, clips):
        dead = jnp.where(clip_rows == c, bias[c : c + 1, :], dead)
    stream = total[:, :width]
    kept = []
    for n in range(2):
        stream_low = stream.astype(BF16)
        query = mm(stream_low, weights[n, 0]).astype(BF16)
        query_key = mm_nt(query, weights[n, 1]).astype(BF16)
        masked = select(mm_nt(query_key, memory[...])) * scale + dead
        peak = jnp.max(masked, axis=1, keepdims=True)
        exponent = jnp.exp(masked - peak)
        whole = jnp.sum(exponent, axis=1, keepdims=True)
        attention = exponent * (1.0 / whole)
        attention_ref[n] = attention
        mixed = mm(spread(attention), memory[...]).astype(BF16)
        attended = mm(mixed, weights[n, 2])
        centred = attended - jnp.mean(attended, axis=1, keepdims=True)
        inverse = lax.rsqrt(jnp.mean(centred * centred, axis=1, keepdims=True) + EPSILON)
        hatted = centred * inverse
        normed = hatted * gain[n : n + 1, :] + shift[n : n + 1, :]
        hidden = (normed * jax.nn.sigmoid(normed)).astype(BF16)
        stream = stream + mm(hidden, weights[n, 3])
        lefts[4 * n] = stream_low
        lefts[4 * n + 2] = mixed
        lefts[4 * n + 3] = hidden
        rights[4 * n + 1] = query
        keys[n] = query_key
        kept.append((peak + jnp.log(whole), hatted, inverse, normed))
    stream_low = stream.astype(BF16)
    last_low[...] = stream_low
    logits = total[:, width:] + mm_nt(stream_low, class_stream[...])
    chance = jax.nn.sigmoid(logits)
    scores[...] = chance
    lane = lax.broadcasted_iota(jnp.int32, chance.shape, 1)
    valid = facts[:, classes : classes + 1]
    back_logits = jnp.where(lane < classes, (chance - facts[...]) * valid / clip_total, 0.0)
    back_logits = back_logits.astype(BF16)
    back_logits_ref[...] = back_logits
    back_stream = mm(back_logits, class_stream[...])
    inners = [None, None]
    for n in (1, 0):
        log_sum, hatted, inverse, normed = kept[n]
        back_branch = back_stream.astype(BF16)
        back_normed = mm_nt(back_branch, weights[n, 3]) * silu_slope(normed)
        norms[n : n + 1, :] = jnp.sum(back_normed * hatted, axis=0, keepdims=True)
        norms[n + 2 : n + 3, :] = jnp.sum(back_normed, axis=0, keepdims=True)
        back_hat = back_normed * gain[n : n + 1, :]
        back_attended = inverse * (
            back_hat
            - jnp.mean(back_hat, axis=1, keepdims=True)
            - hatted * jnp.mean(back_hat * hatted, axis=1, keepdims=True)
        )
        back_att_low = back_attended.astype(BF16)
        back_mixed = mm_nt(back_att_low, weights[n, 2]).astype(BF16)
        attention = attention_ref[n]
        back_attention = select(mm_nt(back_mixed, memory[...]))
        inner = jnp.sum(attention * back_attention, axis=1, keepdims=True)
        back_raw = attention * (back_attention - inner) * scale
        back_key_mix = mm(spread(back_raw), memory[...]).astype(BF16)
        back_query = mm(back_key_mix, weights[n, 1]).astype(BF16)
        back_stream = back_stream + mm_nt(back_query, weights[n, 0])
        lefts[4 * n + 1] = back_key_mix
        rights[4 * n] = back_query
        rights[4 * n + 2] = back_att_low
        rights[4 * n + 3] = back_branch
        mixes[n] = back_mixed
        inners[n] = inner
    lane = lax.broadcasted_iota(jnp.int32, stats.shape, 1)
    stats[...] = jnp.where(
        lane == 0,
        kept[0][0],
        jnp.where(lane == 1, kept[1][0], jnp.where(lane == 2, inners[0], inners[1])),
    )
    back_low = back_stream.astype(BF16)
    first_low[...] = back_low
    back_boxes = mm(back_logits, class_box[...]) + mm_nt(back_low, short[...])
    back_pooled[...] = mm(roi[...], back_boxes.astype(BF16))


def box_grad_kernel(
    pos,
    lefts,
    rights,
    keys,
    mixes,
    stats,
    memory,
    tag,
    clip_of,
    feats,
    pick,
    norms,
    low,
    back_logits,
    last_low,
    block,
    wide,
    rows,
):
    width = memory.shape[1]
    scale = 1.0 / math.sqrt(width)
    allowed = clip_of[...] == tag[...]
    back_memory = None
    for n in range(2):
        raw = mm_nt(keys[n], memory[...])
        attention = jnp.where(allowed, jnp.exp(raw * scale - stats[:, n : n + 1]), 0.0)
        back_attention = mm_nt(mixes[n], memory[...])
        back_raw = (attention * (back_attention - stats[:, n + 2 : n + 3]) * scale).astype(BF16)
        term = mm_tn(back_raw, keys[n]) + mm_tn(attention.astype(BF16), mixes[n])
        back_memory = term if back_memory is None else back_memory + term
    count, boxes, lanes = low.shape
    fine = rows.shape[0] // count // (width // LANES)
    span = fine + lanes
    low_memory = back_memory.astype(BF16)
    fine = rows.shape[0] // count // (width // LANES)
    span = fine + lanes
    for r in range(count):
        values = mm_tn(feats[:, r * lanes : (r + 1) * lanes], low_memory)
        wide[r, fine:, :] = values.astype(BF16)
    own = pick.shape[1]
    for item in range(8):
        columns = mm(lefts[item], pick[...]).astype(BF16)
        block[item * own : (item + 1) * own, :] = mm_tn(columns, rights[item]).astype(BF16)
    block[8 * own :, :] = jnp.zeros((block.shape[0] - 8 * own, width), BF16)
    block[8 * own : 8 * own + norms.shape[0], :] = norms[...].astype(BF16)
    for r in range(count):
        rows[r * lanes : (r + 1) * lanes, :] = mm_tn(low[r], back_logits[...])
    box = lax.broadcasted_iota(jnp.int32, (boxes, 1), 0)
    mine = (box // (boxes // count)) == 2 * pos[1] + pos[0]
    own_logits = jnp.where(mine, back_logits[...].astype(F32), 0.0).astype(BF16)
    rows[count * lanes :, :] = mm_tn(last_low[...], own_logits)
    blocks = width // LANES
    for r in range(count):
        for q in range(blocks):
            start = (r * blocks + q) * fine
            wide[r, :fine, q * LANES : (q + 1) * LANES] = rows[start : start + fine, :].astype(BF16)


def weight_kernel(cols, count, pos, back_expand, plane_out, above, own, below, back_plane, keep, send):
    width = plane_out.shape[1]
    lanes = back_expand.shape[1] // count
    rows = width // count

    def put(start, first, second):
        place = slice(start, start + first.shape[0])

        @pl.when(pos[0] == 0)
        def _():
            keep[place, :] = first.astype(BF16)
            send[place, :] = second.astype(BF16)

        @pl.when(pos[0] != 0)
        def _():
            keep[place, :] = second.astype(BF16)
            send[place, :] = first.astype(BF16)

    each = lanes + 9 * rows
    for chip in range(count // 2):
        block = mm_tn(back_expand[:, 2 * chip * lanes : 2 * (chip + 1) * lanes], plane_out[...])
        put(chip * each, block[:lanes], block[lanes:])
    whole = back_plane[...].astype(F32)
    moved = jnp.concatenate(
        [
            col_shift(whole, cols, -1).astype(BF16),
            back_plane[...],
            col_shift(whole, cols, 1).astype(BF16),
        ],
        axis=1,
    )
    for i, source in enumerate((above, own, below)):
        block = mm_tn(source[...], moved)
        for j in range(3):
            for chip in range(count // 2):
                start = chip * each + lanes + (3 * i + j) * rows
                top = 2 * chip * rows
                columns = slice(j * width, (j + 1) * width)
                put(
                    start,
                    block[top : top + rows, columns],
                    block[top + rows : top + 2 * rows, columns],
                )


def temporal_grad_kernel(clips, cols, count, lanes, pos, *refs):
    sources, pieces = refs[: -3 - count], refs[-3 - count : -3]
    keep, send, moved = refs[-3:]
    step = pl.program_id(0)
    cells, wide = sources[0].shape
    part = pieces[0].shape[1]

    @pl.when(step == 0)
    def _():
        facts = None
        for s, piece in enumerate(pieces):
            values = piece[:cells, :]
            shifts = (frame_shift(values, clips, -cols), values, frame_shift(values, clips, cols))
            for k in range(3):
                moved[k * part : (k + 1) * part, s * cells : (s + 1) * cells] = shifts[k].T
            term = piece[cells:, :].astype(F32)
            facts = term if facts is None else facts + term
        low = facts.astype(BF16)
        each = 3 * lanes + low.shape[0]
        for end in range(each, keep.shape[0] + 1, each):
            keep[end - low.shape[0] : end, :] = low
            send[end - low.shape[0] : end, :] = low

    total, start = None, 0
    for source in sources:
        end = start + source.shape[0]
        term = mm(moved[:, start:end], source[...])
        total = term if total is None else total + term
        start = end
    blocks = wide // (2 * lanes)
    each = 3 * lanes + pieces[0].shape[0] - cells
    for block in range(blocks):
        for k in range(3):
            turned = total[k * part : (k + 1) * part, 2 * block * lanes : 2 * (block + 1) * lanes].T
            start = pl.multiple_of(step * (blocks * each), 16) + block * each + k * lanes
            first = turned[:lanes].astype(BF16)
            second = turned[lanes:].astype(BF16)

            @pl.when(pos[0] == 0)
            def _():
                keep[pl.ds(start, lanes), :] = first
                send[pl.ds(start, lanes), :] = second

            @pl.when(pos[0] != 0)
            def _():
                keep[pl.ds(start, lanes), :] = second
                send[pl.ds(start, lanes), :] = first


def back_plane_kernel(
    clips,
    frames,
    cols,
    back_pooled,
    slope,
    sums,
    expand,
    og,
    plane_sum,
    gain,
    shift,
    back_final,
    back_expand,
    back_plane,
    facts,
    acc,
    rows,
):
    step = pl.program_id(0)
    steps = pl.num_programs(0)
    cells, lanes = slope.shape

    @pl.when(step == 0)
    def _():
        rows[...] = jnp.zeros_like(rows)

    pooled = back_pooled[...].reshape(clips, 1, cols, lanes)
    final = (pooled * slope[...].reshape(clips, frames, cols, lanes)).reshape(cells, lanes)
    back_final[...] = final
    rows[pl.ds(step, 1), :] = jnp.sum(final * sums[...].astype(F32), axis=0, keepdims=True)
    rows[pl.ds(steps + step, 1), :] = jnp.sum(final, axis=0, keepdims=True)
    low = (final * og[...]).astype(BF16)
    back_expand[...] = low
    term = mm_nt(low, expand[...])

    @pl.when(step == 0)
    def _():
        acc[...] = term

    @pl.when(step > 0)
    def _():
        acc[...] += term

    @pl.when(step == steps - 1)
    def _():
        back_arg = acc[...] * silu_slope(plane_sum[...] * gain[1:2, :] + shift[1:2, :])
        rows[pl.ds(2 * steps, 1), :] = jnp.sum(back_arg * plane_sum[...], axis=0, keepdims=True)
        rows[pl.ds(2 * steps + 1, 1), :] = jnp.sum(back_arg, axis=0, keepdims=True)
        back_plane[...] = (back_arg * gain[1:2, :]).astype(BF16)
        facts[...] = rows[...].astype(BF16)


def back_temporal_kernel(
    cols, pos, above, own, below, w, temporal_sum, gain, shift, late, out, facts, *pieces
):
    sides = []
    for j in range(3):
        term = mm_nt(below[...], w[0, j]) + mm_nt(own[...], w[1, j]) + mm_nt(above[...], w[2, j])
        sides.append(term)
    back_out = sides[1] + col_shift(sides[0], cols, -1) + col_shift(sides[2], cols, 1)
    back_arg = back_out * silu_slope(temporal_sum[...] * gain[0:1, :] + shift[0:1, :])
    cells, width = out.shape
    facts[...] = late[...].astype(F32)
    facts[facts.shape[0] - 2 : facts.shape[0] - 1, :] = jnp.sum(
        back_arg * temporal_sum[...], axis=0, keepdims=True
    )
    facts[facts.shape[0] - 1 :, :] = jnp.sum(back_arg, axis=0, keepdims=True)
    out[...] = (back_arg * gain[0:1, :]).astype(BF16)
    for s, piece in enumerate(pieces):
        start = pl.multiple_of(pos[2 + s] * LANES, LANES)
        piece[:cells, :] = out[:, pl.ds(start, LANES)]
        rows = facts.shape[0]
        for q in range(width // LANES):
            piece[cells + q * rows : cells + (q + 1) * rows, :] = facts[
                :, q * LANES : (q + 1) * LANES
            ].astype(BF16)


def input_kernel(clips, cols, back, w, final, out):
    values = back[...]
    total = final[...] + mm_nt(values, w[1])
    total = total + frame_shift(mm_nt(values, w[0]), clips, -cols)
    out[...] = total + frame_shift(mm_nt(values, w[2]), clips, cols)


def lanes_kernel(counts, forms, pos, *refs):
    outs, whole = refs[-1 - len(counts) : -1], refs[-1]
    rows = whole.shape[0]
    index = 0
    for ref in refs[: -1 - len(counts)]:
        for n in range(ref.shape[0] // rows):
            start = pl.multiple_of(pos[index] * LANES, LANES)
            whole[:, pl.ds(start, LANES)] = ref[n * rows : (n + 1) * rows, :]
            index += 1
    start = 0
    for count, form, out in zip(counts, forms, outs):
        piece = whole[start : start + count, :].astype(F32)
        start += count
        if form == 0:
            out[...] = piece
        elif form == 1:
            out[...] = piece.T
        else:
            for q in range(whole.shape[1] // LANES):
                first = q * LANES
                out[q * count : (q + 1) * count, :] = piece[:, first : first + out.shape[1]]


class Halving:
    def __init__(self, held, steps, send, step=0):
        self.held, self.steps, self.send = held, steps, send
        self.step, self.got = step, None

    def advance(self, hold):
        if self.got is not None:
            self.held = take(self.held, self.step - 1, self.got)
            self.got = None
        if self.step < self.steps:
            buffer, hold = lax.optimization_barrier((give(self.held, self.step), hold))
            self.got = self.send(self.step, buffer)
            self.step += 1
        return hold

    def finish(self):
        while self.got is not None:
            self.advance(())
        return self.held[0]


class Doubling:
    def __init__(self, own, steps, send):
        self.parts, self.steps, self.send = [own], steps, send
        self.step, self.got = 0, None

    def advance(self, hold):
        if self.got is not None:
            self.parts.append(self.got)
            self.got = None
        if self.step < self.steps:
            buffer = self.parts[0] if self.step == 0 else jnp.concatenate(self.parts, axis=0)
            buffer, hold = lax.optimization_barrier((buffer, hold))
            self.got = self.send(self.step, buffer)
            self.step += 1
        return hold

    def finish(self):
        while self.got is not None:
            self.advance(())
        return self.parts


def window(values, chains):
    chains = [chain for chain in chains if chain.got is not None]
    tied = lax.optimization_barrier((tuple(values), tuple(chain.got for chain in chains)))
    for chain, got in zip(chains, tied[1]):
        chain.got = got
    return tied[0]


def join_lanes(parts, places):
    rows = parts[0].shape[0]
    blocks = [part[n * rows : (n + 1) * rows] for part in parts for n in range(part.shape[0] // rows)]
    joined = []
    for target in range(len(blocks)):
        chosen = blocks[0]
        for code in range(1, len(blocks)):
            chosen = jnp.where(places[code] == target, blocks[code], chosen)
        joined.append(chosen)
    return jnp.concatenate(joined, axis=-1).astype(F32)


def body(
    clip_input,
    temporal,
    spatial,
    expand,
    mid_gain,
    mid_shift,
    out_gain,
    out_shift,
    short_weight,
    bank_weight,
    block_weight,
    norm_gain,
    norm_shift,
    class_weight,
    bank_feats,
    bank_mask,
    box_coords,
    box_clip,
    box_valid,
    labels,
):
    row = lax.axis_index("row")
    group = lax.axis_index("clip")
    row_size = lax.axis_size("row")
    clip_size = lax.axis_size("clip")
    core = row % 2
    chip = row // 2
    chips = row_size // 2
    clips, frames, rows_local, cols, channels = clip_input.shape
    mid = temporal.shape[2]
    width = short_weight.shape[1]
    classes = class_weight.shape[1]
    cells = clips * frames * cols
    boxes = box_coords.shape[0]
    box_local = labels.shape[0]
    slots_local = bank_feats.shape[1]
    part = mid // clip_size
    steps = channels // mid
    lanes = channels // row_size
    crossed = clip_size == 4
    masks = [(s, s) for s in range(clip_size)]
    if crossed:
        masks = [(0, 0), (1, 2), (2, 1), (3, 3)]
    targets = [group ^ jnp.where(core == 0, first, second) for first, second in masks]
    place = jnp.stack([core, chip, *targets]).astype(jnp.int32)
    og, os = out_gain[None], out_shift[None]

    tie = lax.optimization_barrier
    source = clip_input.reshape(cells, channels)

    eighth = cells // 8
    wide_input = [source]
    if not crossed:
        wide_input += [swap(source, "clip", s) for s in range(1, clip_size)]

    def source_rows(start, count, after):
        values, _ = tie((source, after))
        return values[start * eighth : (start + count) * eighth]

    def kernel_row(i):
        return pl.BlockSpec((1, 3, mid, mid), lambda _: (i, 0, 0, 0))

    def fixed(*shape):
        return pl.BlockSpec(shape, lambda i: (0,) * len(shape))

    def across(height, lane_count):
        return pl.BlockSpec((height, lane_count), lambda i: (0, i))

    temporal_sum, temporal_out = run(
        lambda *refs: temporal_kernel(clips, cols, *refs),
        [shape_of((cells, mid), F32), shape_of((cells, mid), BF16)],
        [source, temporal, mid_gain, mid_shift],
        grid=(steps,),
        in_specs=[
            across(cells, mid),
            pl.BlockSpec((3, mid, mid), lambda i: (0, i, 0)),
            fixed(2, mid),
            fixed(2, mid),
        ],
        out_specs=[fixed(cells, mid), fixed(cells, mid)],
    )

    def halo(values):
        ends = row_size - 1
        above = lax.ppermute(values, "row", [(i, i + 1) for i in range(ends)])
        below = lax.ppermute(values, "row", [(i + 1, i) for i in range(ends)])
        return above, below

    above_row, below_row = halo(temporal_out)

    if crossed:
        first_a = joint_swap(source_rows(0, 3, temporal_out), 1, 2)
    feats, box_coords, temporal_out = tie(
        (bank_feats.reshape(clips * slots_local, channels), box_coords, temporal_out)
    )
    memory_own = mm(feats, bank_weight).astype(BF16)
    clip_group = box_clip - group * clips
    weights = box_weights(
        box_coords, clip_group, row * rows_local, rows_local, rows_local * row_size, clips, cols
    ).reshape(boxes, clips * cols)
    class_rows = jnp.pad(class_weight.T, ((0, LANES - classes), (0, 0)))

    (plane_part,) = run(
        lambda *refs: plane_own_kernel(cols, *refs),
        [shape_of((cells, mid), F32)],
        [temporal_out, spatial],
        grid=(1,),
        in_specs=[fixed(cells, mid), kernel_row(1)],
        out_specs=[fixed(cells, mid)],
    )
    tied = (above_row, below_row, plane_part, weights, class_rows, memory_own)
    if crossed:
        *tied, first_a = tie((*tied, first_a))
    else:
        tied = tie(tied)
    above_row, below_row, plane_part, weights, class_rows, memory_own = tied
    if crossed:
        first_b = joint_swap(source_rows(3, 4, above_row), 1, 2)
    memory = lax.all_gather(
        memory_own.reshape(clips, slots_local, width), "row", axis=1, tiled=True
    ).reshape(-1, width)
    half = boxes // 2
    joint = width + LANES
    plane_sum, plane_out, partial_low, mine, other = run(
        lambda *refs: plane_kernel(clips, frames, cols, *refs),
        [
            shape_of((cells, mid), F32),
            shape_of((cells, mid), BF16),
            shape_of((row_size, boxes, lanes), BF16),
            shape_of((half, joint), F32),
            shape_of((half, joint), BF16),
        ],
        [
            place,
            above_row,
            below_row,
            spatial,
            spatial,
            plane_part,
            mid_gain,
            mid_shift,
            expand,
            source,
            og,
            os,
            weights,
            short_weight,
            class_rows,
        ],
        grid=(steps,),
        in_specs=[
            SMEM,
            fixed(cells, mid),
            fixed(cells, mid),
            kernel_row(0),
            kernel_row(2),
            fixed(cells, mid),
            fixed(2, mid),
            fixed(2, mid),
            across(mid, mid),
            across(cells, mid),
            across(1, mid),
            across(1, mid),
            fixed(boxes, clips * cols),
            pl.BlockSpec((mid, width), lambda i: (i, 0)),
            across(LANES, mid),
        ],
        out_specs=[
            fixed(cells, mid),
            fixed(cells, mid),
            pl.BlockSpec((mid // lanes, boxes, lanes), lambda i: (i, 0, 0)),
            fixed(half, joint),
            fixed(half, joint),
        ],
        scratch=[pltpu.VMEM((boxes, joint), F32)],
    )

    if crossed:
        mine, other, plane_out, first_b = tie((mine, other, plane_out, first_b))
        first_c = joint_swap(source_rows(7, 1, mine), 1, 2)
        second_a = joint_swap(source_rows(0, 2, mine), 2, 1)
    facts = jnp.concatenate([labels.astype(BF16), box_valid.astype(BF16)[:, None]], axis=1)
    facts = jnp.pad(facts, ((0, 0), (0, LANES - facts.shape[1])))
    facts = jnp.concatenate([facts[: box_local // 2], facts[box_local // 2 :]], axis=1)
    facts = jnp.pad(facts, ((0, 0), (0, joint - 2 * LANES)))
    half_sum = mine + swap(other, "row", 1).astype(F32)
    quarter = half // 2
    side = chip % 2
    got = swap(
        lax.dynamic_slice_in_dim(half_sum, (1 - side) * quarter, quarter, 0).astype(BF16), "row", 2
    )
    plane_late, _ = tie((plane_out, half_sum))
    expand_sums, slope = run(
        lambda *refs: slope_kernel(frames, *refs),
        [shape_of((cells, channels), BF16), shape_of((cells, channels), F32)],
        [plane_late, expand, source, og, os],
        grid=(steps,),
        in_specs=[
            fixed(cells, mid),
            across(mid, mid),
            across(cells, mid),
            across(1, mid),
            across(1, mid),
        ],
        out_specs=[across(cells, mid)] * 2,
    )
    if crossed:
        got, slope, first_c, second_a = tie((got, slope, first_c, second_a))
    else:
        got, slope = tie((got, slope))
    part_sum = lax.dynamic_slice_in_dim(half_sum, side * quarter, quarter, 0) + got.astype(F32)
    label_rows, codes = [facts], [0]
    for t in range(1, bits(chips)):
        payload = jnp.concatenate([part_sum.astype(BF16)] + label_rows, axis=0)
        got = swap(payload, "row", 2 << t)
        part_sum = part_sum + got[:quarter].astype(F32)
        each = facts.shape[0]
        label_rows = label_rows + [
            got[quarter + n * each : quarter + (n + 1) * each] for n in range(len(codes))
        ]
        codes = codes + [code ^ (1 << t) for code in codes]
    got = swap(jnp.concatenate([part_sum.astype(BF16)] + label_rows, axis=0), "row", 2)
    live = bank_mask == 1
    tags = jnp.where(live, jnp.arange(clips, dtype=jnp.int32)[:, None], -1)
    tags_own = lax.dynamic_slice_in_dim(tags, row * slots_local, slots_local, 1).reshape(1, -1)
    bias = jnp.where(live, 0.0, -jnp.inf).astype(F32)
    clip_column = clip_group[:, None]
    class_box, class_stream = class_rows[:, :channels], class_rows[:, channels:]
    got, memory, bias, clip_column, class_box, class_stream = tie(
        (got, memory, bias, clip_column, class_box, class_stream)
    )
    (totals_own,) = run(
        lambda *refs: total_kernel(codes + [code ^ 1 for code in codes], *refs),
        [shape_of((half + chips * facts.shape[0], joint), F32)],
        [place, part_sum, got, *label_rows],
        in_specs=[SMEM] + [VMEM] * (2 + len(label_rows)),
    )
    totals_other = swap(totals_own, "row", 1)
    if crossed:
        second_b = joint_swap(source_rows(2, 6, totals_own), 2, 1)

    partial_low, totals_other = tie((partial_low, totals_other))
    short_columns = lax.psum_scatter(partial_low, "row", scatter_dimension=0, tiled=False)

    slots = bias.shape[1]
    stream_shape = (boxes, width)
    (
        scores_all,
        back_pooled,
        lefts,
        rights,
        keys,
        mixes,
        stats,
        last_low,
        first_low,
        back_logits,
        norms,
    ) = run(
        lambda *refs: box_kernel(chips, classes, float(clips * clip_size), *refs),
        [
            shape_of((boxes, LANES), F32),
            shape_of((clips * cols, channels), F32),
            shape_of((8, *stream_shape), BF16),
            shape_of((8, *stream_shape), BF16),
            shape_of((2, *stream_shape), BF16),
            shape_of((2, *stream_shape), BF16),
            shape_of((boxes, LANES), F32),
            shape_of(stream_shape, BF16),
            shape_of(stream_shape, BF16),
            shape_of((boxes, LANES), BF16),
            shape_of((4, width), F32),
        ],
        [
            place,
            totals_own,
            totals_other,
            memory,
            bias,
            clip_column,
            block_weight,
            norm_gain,
            norm_shift,
            class_stream,
            class_box,
            short_weight,
            weights.T,
        ],
        in_specs=[SMEM] + [VMEM] * 12,
        scratch=[
            pltpu.VMEM((boxes, joint), F32),
            pltpu.VMEM((boxes, LANES), F32),
            pltpu.VMEM((2, boxes, slots), F32),
        ],
    )
    scores = lax.dynamic_slice_in_dim(scores_all, row * box_local, box_local, 0)[:, :classes]

    if crossed:
        back_pooled, second_b = tie((back_pooled, second_b))
        first_late, _ = tie((first_a, back_pooled))
        third_a = joint_swap(first_late, 2, 1)

    fact_rows = -(-(2 * steps + 2) // 16) * 16
    back_final, back_expand, back_plane, second_facts = run(
        lambda *refs: back_plane_kernel(clips, frames, cols, *refs),
        [
            shape_of((cells, channels), F32),
            shape_of((cells, channels), BF16),
            shape_of((cells, mid), BF16),
            shape_of((fact_rows, mid), BF16),
        ],
        [
            back_pooled,
            slope,
            expand_sums,
            expand,
            og,
            plane_sum,
            mid_gain,
            mid_shift,
        ],
        grid=(steps,),
        in_specs=[
            across(clips * cols, mid),
            across(cells, mid),
            across(cells, mid),
            across(mid, mid),
            across(1, mid),
            fixed(cells, mid),
            fixed(2, mid),
            fixed(2, mid),
        ],
        out_specs=[
            across(cells, mid),
            across(cells, mid),
            fixed(cells, mid),
            fixed(fact_rows, mid),
        ],
        scratch=[pltpu.VMEM((cells, mid), F32), pltpu.VMEM((fact_rows, mid), F32)],
    )

    if crossed:
        back_plane, back_final, back_expand, second_facts, third_a = tie(
            (back_plane, back_final, back_expand, second_facts, third_a)
        )
        first_late, _ = tie((first_b, back_plane))
        third_b = joint_swap(first_late, 2, 1)
    back_above, back_below = halo(back_plane)

    fact_count = second_facts.shape[0]
    own_mid = mid // row_size
    own_rows = channels // row_size

    weight_rows = own_rows + 9 * own_mid
    kept_weight, sent_weight = run(
        lambda *refs: weight_kernel(cols, row_size, *refs),
        [shape_of((chips * weight_rows, mid), BF16)] * 2,
        [
            place,
            back_expand,
            plane_out,
            above_row,
            temporal_out,
            below_row,
            back_plane,
        ],
        in_specs=[SMEM] + [VMEM] * 6,
    )
    tied = (back_above, back_below, kept_weight, sent_weight, short_columns)
    if crossed:
        *tied, third_b = tie((*tied, third_b))
        first_late, _ = tie((first_c, sent_weight))
        third_c = joint_swap(first_late, 2, 1)
        wide_input += [first_a, first_b, first_c, second_a, second_b, third_a, third_b, third_c]
    else:
        tied = tie(tied)
    back_above, back_below, kept_weight, sent_weight, short_columns = tied
    got_weight = swap(sent_weight, "row", 1)

    even, odd = step_masks(clip_size)
    places = [place_of(code, group, core) for code in range(clip_size)]

    def clip_step(t, values):
        return joint_swap(values, even[t], odd[t])

    def chip_step(t, values):
        return swap(values, "row", 2 << t)

    def lane_block(values, target):
        return lax.dynamic_slice_in_dim(values, target * part, part, 1)

    def chip_rows(target, *values):
        each = values[0].shape[0] // chips
        rows = [lax.dynamic_slice_in_dim(item, target * each, each, 0) for item in values]
        if len(rows) == 1:
            return rows[0]
        return tree_sum([item.astype(F32) for item in rows]).astype(BF16)

    def over_chips(*values):
        return Halving(
            {code: chip_rows(chip ^ code, *values) for code in range(chips)}, bits(chips), chip_step
        )

    def over_clips(piece):
        return Halving(
            {code: piece(places[code]) for code in range(clip_size)}, bits(clip_size), clip_step
        )

    pick = (
        jnp.arange(width, dtype=jnp.int32)[:, None]
        == row * own_mid + jnp.arange(own_mid, dtype=jnp.int32)[None, :]
    ).astype(BF16)
    class_fine = (channels + width) // row_size * LANES // width
    lefts, _ = tie((lefts, sent_weight))
    block_part, wide_part = run(
        box_grad_kernel,
        [
            shape_of((8 * own_mid + 16, width), BF16),
            shape_of((row_size, class_fine + own_rows, width), BF16),
        ],
        [
            place,
            lefts,
            rights,
            keys,
            mixes,
            stats,
            memory_own,
            tags_own,
            clip_column,
            feats,
            pick,
            norms,
            partial_low,
            back_logits,
            last_low,
        ],
        in_specs=[SMEM] + [VMEM] * 14,
        scratch=[pltpu.VMEM((channels + width, LANES), F32)],
    )
    short_part = mm_tn(short_columns, first_low).astype(BF16)
    tied = (got_weight, block_part, short_part, wide_part)
    if crossed:
        *tied, third_c = tie((*tied, third_c))
        wide_input[-1] = third_c
    else:
        tied = tie(tied)
    got_weight, block_part, short_part, wide_part = tied
    wide_own = lax.psum_scatter(wide_part, "row", scatter_dimension=0, tiled=False)

    held = {
        code: (
            lane_block(kept_weight, target).astype(F32) + lane_block(got_weight, target).astype(F32)
        ).astype(BF16)
        for code, target in enumerate(places)
    }
    high = [code for code in range(clip_size) if code & 1]
    late, early = high[: len(high) // 2], high[len(high) // 2 :]
    buffers, back_above = tie((tuple(held[code] for code in early), back_above))
    first_step = {code: clip_step(0, values) for code, values in zip(early, buffers)}

    direct = part == LANES
    piece_rows = fact_rows * (mid // part)
    back_temporal, facts_own, *pieces = run(
        lambda *refs: back_temporal_kernel(cols, *refs),
        [shape_of((cells, mid), BF16), shape_of((fact_rows, mid), F32)]
        + [shape_of((cells + piece_rows, part), BF16)] * (clip_size if direct else 0),
        [
            place,
            back_above,
            back_plane,
            back_below,
            spatial,
            temporal_sum,
            mid_gain,
            mid_shift,
            second_facts,
        ],
        in_specs=[SMEM] + [VMEM] * 8,
    )
    if not direct:
        facts_flat = jnp.concatenate(
            [facts_own[:, q * part : (q + 1) * part] for q in range(mid // part)], axis=0
        ).astype(BF16)
        pieces = [
            jnp.concatenate(
                [lax.dynamic_slice_in_dim(back_temporal, target * part, part, 1), facts_flat], axis=0
            )
            for target in targets
        ]
    back_temporal, first_step, pieces = tie((back_temporal, first_step, tuple(pieces)))

    got = pieces[:1] + tuple(
        joint_swap(piece, *step_mask) for piece, step_mask in zip(pieces[1:], masks[1:])
    )
    (input_grad,) = run(
        lambda *refs: input_kernel(clips, cols, *refs),
        [shape_of((cells, channels), F32)],
        [back_temporal, temporal, back_final],
        grid=(steps,),
        in_specs=[
            fixed(cells, mid),
            pl.BlockSpec((3, mid, mid), lambda i: (0, i, 0)),
            across(cells, mid),
        ],
        out_specs=[across(cells, mid)],
    )
    got, input_grad = tie((got, input_grad))
    input_grad = input_grad.reshape(clip_input.shape)

    buffers, got = tie((tuple(held[code] for code in late), got))
    first_step.update({code: clip_step(0, values) for code, values in zip(late, buffers)})
    temporal_rows = chips * (3 * own_rows + piece_rows)
    kept_temporal, sent_temporal = run(
        lambda *refs: temporal_grad_kernel(clips, cols, clip_size, lanes, *refs),
        [shape_of((temporal_rows, part), BF16)] * 2,
        [place, *wide_input, *got],
        grid=(steps,),
        in_specs=[SMEM]
        + [across(item.shape[0], mid) for item in wide_input]
        + [fixed(cells + piece_rows, part)] * clip_size,
        out_specs=[fixed(temporal_rows, part)] * 2,
        scratch=[pltpu.VMEM((3 * part, clip_size * cells), BF16)],
    )
    tied = tie((kept_temporal, sent_temporal, first_step))
    kept_temporal, sent_temporal, first_step = tied
    got_temporal = swap(sent_temporal, "row", 1)
    sums_weight = Halving(
        {
            code ^ 1: held[code ^ 1].astype(F32) + values.astype(F32)
            for code, values in first_step.items()
        },
        bits(clip_size),
        clip_step,
        step=1,
    )
    got_temporal = sums_weight.advance(got_temporal)
    sums_temporal = over_chips(kept_temporal, got_temporal)
    wide_own = sums_temporal.advance(wide_own)

    box_wide = [wide_own, block_part, short_part]
    sums_box = over_clips(
        lambda target: jnp.concatenate([lane_block(item, target) for item in box_wide], axis=0)
    )
    sums_weight.got = sums_box.advance(sums_weight.got)
    sums_chip = over_chips(sums_weight.finish().astype(BF16))
    sums_temporal.got = sums_chip.advance(sums_temporal.got)
    sums_box.got = sums_temporal.advance(sums_box.got)
    sums_temporal.got = sums_box.advance(sums_temporal.got)
    temporal_got = sums_temporal.finish()
    own_temporal = 3 * own_rows
    facts_total = temporal_got[own_temporal:].reshape(mid // part, fact_rows, part)
    facts_total = jnp.concatenate([facts_total[q] for q in range(mid // part)], axis=1)
    temporal_got, sums_box.got = tie((temporal_got, sums_box.got))
    box_own = sums_box.finish().astype(BF16)
    all_first = Doubling(
        jnp.concatenate([temporal_got[:own_temporal].astype(BF16), box_own], axis=0),
        bits(clip_size),
        clip_step,
    )
    sums_chip.got = all_first.advance(sums_chip.got)
    all_first.got = sums_chip.advance(all_first.got)
    sums_chip.got = all_first.advance(sums_chip.got)
    weight_own = sums_chip.finish().astype(BF16)
    all_last = Doubling(weight_own, bits(clip_size), clip_step)
    all_first.got = all_last.advance(all_first.got)
    firsts = all_first.finish()
    all_last.advance(())
    lasts = all_last.finish()

    class_count = class_fine * width // LANES
    first_counts = [own_temporal, class_fine, own_rows, 8 * own_mid, 16, own_rows]
    first_shapes = [(own_temporal, mid), (class_count, classes), (own_rows, width)]
    first_shapes += [(8 * own_mid, width), (16, width), (own_rows, width)]
    last_counts = [own_rows, 9 * own_mid]
    last_shapes = [(mid, own_rows), (9 * own_mid, mid)]

    def assemble(parts, counts, shapes, forms):
        if direct:
            return run(
                lambda *refs: lanes_kernel(counts, forms, *refs),
                [shape_of(shape, F32) for shape in shapes],
                [jnp.stack([jnp.asarray(p, jnp.int32) for p in places]), *parts],
                in_specs=[SMEM] + [VMEM] * len(parts),
                scratch=[pltpu.VMEM((sum(counts), width), BF16)],
            )
        whole = join_lanes(parts, places)
        ends = [sum(counts[: k + 1]) for k in range(len(counts))]
        outs = []
        for count, end, shape, form in zip(counts, ends, shapes, forms):
            piece = whole[end - count : end]
            if form == 1:
                piece = piece.T
            if form == 2:
                piece = jnp.concatenate(
                    [piece[:, q * LANES : q * LANES + shape[1]] for q in range(width // LANES)],
                    axis=0,
                )
            outs.append(piece)
        return outs

    temporal_grad, class_grad, bank_grad, block_grad, norm_got, short_grad = assemble(
        firsts, first_counts, first_shapes, (0, 2, 0, 0, 0, 0)
    )
    expand_grad, spatial_grad = assemble(lasts, last_counts, last_shapes, (1, 0))
    temporal_grad = temporal_grad.reshape(3, own_rows, mid)
    spatial_grad = spatial_grad.reshape(3, 3, own_mid, mid)
    block_grad = block_grad.reshape(2, 4, own_mid, width)
    norm_got = lax.dynamic_slice_in_dim(norm_got[:4], row * own_mid, own_mid, 1)
    out_gain_all = facts_total[:steps].reshape(-1)
    out_shift_all = facts_total[steps : 2 * steps].reshape(-1)
    out_gain_grad = lax.dynamic_slice_in_dim(out_gain_all, row * own_rows, own_rows, 0)
    out_shift_grad = lax.dynamic_slice_in_dim(out_shift_all, row * own_rows, own_rows, 0)
    gain_all = jnp.stack([facts_total[fact_rows - 2], facts_total[2 * steps]])
    shift_all = jnp.stack([facts_total[fact_rows - 1], facts_total[2 * steps + 1]])
    mid_gain_grad = lax.dynamic_slice_in_dim(gain_all, row * own_mid, own_mid, 1)
    mid_shift_grad = lax.dynamic_slice_in_dim(shift_all, row * own_mid, own_mid, 1)
    return (
        scores,
        input_grad,
        temporal_grad,
        spatial_grad,
        expand_grad,
        mid_gain_grad,
        mid_shift_grad,
        out_gain_grad,
        out_shift_grad,
        short_grad,
        bank_grad,
        block_grad,
        norm_got[:2],
        norm_got[2:],
        class_grad,
    )


def solution(mesh):
    whole = P()
    in_specs = (
        (P("clip", None, "row", None, None),)
        + (whole,) * 13
        + (
            P("clip", "row", None),
            P("clip", None),
            P("clip", None),
            P("clip"),
            P(("clip", "row")),
            P(("clip", "row"), None),
        )
    )
    out_specs = (
        P(("clip", "row"), None),
        P("clip", None, "row", None, None),
        P(None, "row", None),
        P(None, None, "row", None),
        P(None, "row"),
        P(None, "row"),
        P(None, "row"),
        P("row"),
        P("row"),
        P("row", None),
        P("row", None),
        P(None, None, "row", None),
        P(None, "row"),
        P(None, "row"),
        P("row", None),
    )
    return jax.shard_map(body, mesh=mesh, in_specs=in_specs, out_specs=out_specs, check_vma=False)
```

```python
import math

import jax
import jax.numpy as jnp
from jax import lax
from jax.experimental import pallas as pl
from jax.experimental.pallas import tpu as pltpu
from jax.sharding import PartitionSpec as P

SAMPLES = 14
LANES = 128
SUBLANES = 8
EPSILON = 1e-05
F32 = jnp.float32
BF16 = jnp.bfloat16


def dot(left, right, dims):
    return lax.dot_general(left, right, (dims, ((), ())), preferred_element_type=F32)


def mm(left, right):
    return dot(left, right, ((1,), (0,)))


def mm_nt(left, right):
    return dot(left, right, ((1,), (1,)))


def mm_tn(left, right):
    return dot(left, right, ((0,), (0,)))


def swap(values, axis, mask):
    count = lax.axis_size(axis)
    return lax.ppermute(values, axis, [(i, i ^ mask) for i in range(count)])


def tree_sum(parts):
    while len(parts) > 1:
        parts = [parts[i] + parts[i + 1] for i in range(0, len(parts), 2)]
    return parts[0]


def step_masks(count):
    even = [1 << t for t in range(count.bit_length() - 1)]
    odd = list(even)
    for t in range(0, len(odd) - 1, 2):
        odd[t], odd[t + 1] = odd[t + 1], odd[t]
    return even, odd


def joint_swap(values, even_mask, odd_mask):
    clip_size = lax.axis_size("clip")
    row_size = lax.axis_size("row")
    pairs = []
    for c in range(clip_size):
        for r in range(row_size):
            mask = odd_mask if r % 2 else even_mask
            pairs.append((c * row_size + r, (c ^ mask) * row_size + r))
    return lax.ppermute(values, ("clip", "row"), pairs)


def place_of(code, group, core):
    even, odd = step_masks(lax.axis_size("clip"))
    first = sum(m for t, m in enumerate(even) if code >> t & 1)
    second = sum(m for t, m in enumerate(odd) if code >> t & 1)
    return group ^ (first if first == second else jnp.where(core == 0, first, second))


def give(held, t):
    return jnp.concatenate([held[code].astype(BF16) for code in held if code >> t & 1], axis=0)


def take(held, t, got):
    low = [code for code in held if not code >> t & 1]
    rows = got.shape[0] // len(low)
    return {
        code: held[code].astype(F32) + got[n * rows : (n + 1) * rows].astype(F32)
        for n, code in enumerate(low)
    }


def bits(count):
    return count.bit_length() - 1


def pad_rows(values, rows):
    return jnp.pad(values, ((0, rows - values.shape[0]), (0, 0)))


def axis_weights(low_edge, high_edge, cell_count, first_cell, span_count):
    samples = (jnp.arange(SAMPLES, dtype=F32) + 0.5) / SAMPLES
    start_pos = low_edge.astype(F32) * 0.25
    extent = (high_edge - low_edge).astype(F32) * 0.25
    points = start_pos[:, None] + extent[:, None] * samples[None, :]
    points = jnp.clip(points - 0.5, 0.0, cell_count - 1.0)
    centers = (first_cell + jnp.arange(span_count, dtype=jnp.int32)).astype(F32)
    tents = jnp.maximum(0.0, 1.0 - jnp.abs(points[:, :, None] - centers[None, None, :]))
    return jnp.mean(tents, axis=1)


def box_weights(coords, clip_local, first_row, row_count, rows_total, clip_count, col_count):
    along_rows = axis_weights(coords[:, 0], coords[:, 1], rows_total, first_row, row_count)
    along_cols = axis_weights(coords[:, 2], coords[:, 3], col_count, 0, col_count)
    member = (clip_local[:, None] == jnp.arange(clip_count, dtype=jnp.int32)[None, :]).astype(F32)
    product = along_rows[:, None, :, None] * along_cols[:, None, None, :] * member[:, :, None, None]
    return product.astype(BF16)


def silu_slope(value_in):
    gate = jax.nn.sigmoid(value_in)
    return gate * (1.0 + value_in * (1.0 - gate))


VMEM = pl.BlockSpec(memory_space=pltpu.VMEM)
SMEM = pl.BlockSpec(memory_space=pltpu.SMEM)
MIB = 1024 * 1024
MIB_DEFAULT = 58


ANY = pl.BlockSpec(memory_space=pl.ANY)


class Loads:
    def __init__(self, pairs, sems):
        self.copies = [
            pltpu.make_async_copy(source, target, sems.at[n])
            for n, (source, target) in enumerate(pairs)
        ]
        self.done = 0
        for copy in self.copies:
            copy.start()

    def wait(self, count):
        while self.done < count:
            self.copies[self.done].wait()
            self.done += 1


def shape_of(shape, dtype):
    return jax.ShapeDtypeStruct(shape, dtype)


def run(kernel, outs, ins, grid=(), in_specs=None, out_specs=None, scratch=(), mib=MIB_DEFAULT):
    return pl.pallas_call(
        kernel,
        grid=grid,
        out_shape=tuple(outs),
        in_specs=in_specs or [VMEM] * len(ins),
        out_specs=tuple(out_specs or [VMEM] * len(outs)),
        scratch_shapes=list(scratch),
        compiler_params=pltpu.CompilerParams(vmem_limit_bytes=mib * MIB),
        cost_estimate=pl.CostEstimate(flops=0, bytes_accessed=0, transcendentals=0),
    )(*ins)


def frame_shift(values, clips, step):
    grid = values.reshape(clips, -1, values.shape[1])
    rows = grid.shape[1]
    zeros = jnp.zeros((clips, abs(step), values.shape[1]), values.dtype)
    if step > 0:
        moved = jnp.concatenate([zeros, grid[:, : rows - step]], axis=1)
    else:
        moved = jnp.concatenate([grid[:, -step:], zeros], axis=1)
    return moved.reshape(values.shape)


def col_shift(values, cols, step):
    col = lax.broadcasted_iota(jnp.int32, (values.shape[0], 1), 0) % cols
    edge = 0 if step > 0 else cols - 1
    rows = values.shape[0]
    return jnp.where(col == edge, 0.0, pltpu.roll(values, step % rows, 0))


def temporal_kernel(clips, cols, starts, x, w, gain, shift, total, out, *pieces):
    step = pl.program_id(0)
    values = x[...]
    for start, piece in zip(starts, pieces):
        piece[...] = x[start : start + piece.shape[0], :]
    term = mm(frame_shift(values, clips, cols), w[0]) + mm(values, w[1])
    term = term + mm(frame_shift(values, clips, -cols), w[2])

    @pl.when(step == 0)
    def _():
        total[...] = term

    @pl.when(step > 0)
    def _():
        total[...] += term

    @pl.when(step == pl.num_programs(0) - 1)
    def _():
        arg = total[...] * gain[0:1, :] + shift[0:1, :]
        out[...] = (arg * jax.nn.sigmoid(arg)).astype(BF16)


def plane_rows_sum(rows, weights, cols):
    sides = []
    for j in range(3):
        term = None
        for values, kernel in zip(rows, weights):
            part = mm(values, kernel[j])
            term = part if term is None else term + part
        sides.append(term)
    return sides[1] + col_shift(sides[0], cols, 1) + col_shift(sides[2], cols, -1)


def plane_own_kernel(cols, own, w, out):
    out[...] = plane_rows_sum([own[...]], [w[0]], cols)


def plane_kernel(
    clips,
    frames,
    cols,
    pos,
    above,
    below,
    first,
    last,
    part,
    gain,
    shift,
    expand,
    x,
    og,
    os,
    weights,
    short,
    classes,
    total,
    out,
    low,
    mine,
    other,
    projected,
):
    step = pl.program_id(0)

    @pl.when(step == 0)
    def _():
        whole = part[...] + plane_rows_sum([above[...], below[...]], [first[0], last[0]], cols)
        total[...] = whole
        arg = whole * gain[1:2, :] + shift[1:2, :]
        out[...] = (arg * jax.nn.sigmoid(arg)).astype(BF16)
        projected[...] = jnp.zeros_like(projected)

    arg = mm(out[...], expand[...]) * og[...] + os[...] + x[...].astype(F32)
    active = arg * jax.nn.sigmoid(arg)
    summed = jnp.sum(active.reshape(clips, frames, cols, -1), axis=1)
    pooled = (summed / frames).reshape(clips * cols, -1).astype(BF16)
    values = mm_tn(weights[...], pooled).astype(BF16)
    lanes = low.shape[2]
    for r in range(low.shape[0]):
        low[r] = values[:, r * lanes : (r + 1) * lanes]
    width = short.shape[1]
    count = classes.shape[0]
    projected[:, :width] += mm(values, short[...])
    projected[:, width : width + count] += mm_nt(values, classes[...])

    @pl.when(step == pl.num_programs(0) - 1)
    def _():
        half = mine.shape[0]
        mine[...] = projected[pl.ds(pos[0] * half, half), :]
        other[...] = projected[pl.ds((1 - pos[0]) * half, half), :].astype(BF16)


def slope_kernel(frames, plane_out, expand, x, og, os, sums, slope):
    expand_sum = mm(plane_out[...], expand[...])
    sums[...] = expand_sum.astype(BF16)
    arg = expand_sum * og[...] + os[...] + x[...].astype(F32)
    slope[...] = (silu_slope(arg) * (1.0 / frames)).astype(BF16)


def total_kernel(order, pos, part, got, *refs):
    facts, out = refs[:-1], refs[-1]
    rows = part.shape[0]
    side = pos[1] % 2
    out[pl.ds(side * rows, rows), :] = part[...]
    out[pl.ds((1 - side) * rows, rows), :] = got[:rows, :].astype(F32)
    each = facts[0].shape[0]
    near = len(facts)
    for n, code in enumerate(order):
        start = 2 * rows + code * each
        if n < near:
            out[start : start + each, :] = facts[n][...].astype(F32)
        else:
            other = rows + (n - near) * each
            out[start : start + each, :] = got[other : other + each, :].astype(F32)


def box_kernel(
    chips,
    classes,
    clip_total,
    pos,
    own,
    other,
    bias,
    gain,
    shift,
    memory_far,
    weights_far,
    class_far,
    short_far,
    roi_far,
    scores,
    back_pooled,
    lefts,
    rights,
    keys,
    mixes,
    stats,
    last_low,
    first_low,
    back_logits_ref,
    norms,
    total,
    facts,
    attention_ref,
    memory,
    weights,
    class_rows,
    short,
    roi,
    sems,
):
    loads = Loads(
        [(weights_far.at[0, 0], weights.at[0, 0]), (weights_far.at[0, 1], weights.at[0, 1])]
        + [(memory_far, memory)]
        + [(weights_far.at[0, k], weights.at[0, k]) for k in (2, 3)]
        + [(weights_far.at[1], weights.at[1]), (class_far, class_rows)]
        + [(short_far, short), (roi_far, roi)],
        sems,
    )
    half = total.shape[0] // 2
    each = half // chips // 2
    core, chip = pos[0], pos[1]
    total[pl.ds(core * half, half), :] = own[:half, :]
    total[pl.ds((1 - core) * half, half), :] = other[:half, :]
    for s in range(chips):
        rows = slice(half + s * each, half + (s + 1) * each)
        base = 4 * (chip ^ s)
        for part in range(2):
            lanes = slice(part * LANES, (part + 1) * LANES)
            facts[pl.ds((base + 2 * core + part) * each, each), :] = own[rows, lanes]
            facts[pl.ds((base + 2 * (1 - core) + part) * each, each), :] = other[rows, lanes]
    width = memory.shape[1]
    scale = 1.0 / math.sqrt(width)
    clips, slots = bias.shape
    clip_rows = facts[:, classes + 1 : classes + 2].astype(jnp.int32)

    def select(values):
        chosen = values[:, :slots]
        for c in range(1, clips):
            chosen = jnp.where(clip_rows == c, values[:, c * slots : (c + 1) * slots], chosen)
        return chosen

    def spread(values):
        return jnp.concatenate(
            [jnp.where(clip_rows == c, values, 0.0).astype(BF16) for c in range(clips)], axis=1
        )

    dead = jnp.broadcast_to(bias[0:1, :], (clip_rows.shape[0], slots))
    for c in range(1, clips):
        dead = jnp.where(clip_rows == c, bias[c : c + 1, :], dead)
    stream = total[:, :width]
    kept = []
    for n in range(2):
        stream_low = stream.astype(BF16)
        loads.wait(1 if n == 0 else 6)
        query = mm(stream_low, weights[n, 0]).astype(BF16)
        loads.wait(2)
        query_key = mm_nt(query, weights[n, 1]).astype(BF16)
        loads.wait(3)
        masked = select(mm_nt(query_key, memory[...])) * scale + dead
        peak = jnp.max(masked, axis=1, keepdims=True)
        exponent = jnp.exp(masked - peak)
        whole = jnp.sum(exponent, axis=1, keepdims=True)
        attention = exponent * (1.0 / whole)
        attention_ref[n] = attention
        mixed = mm(spread(attention), memory[...]).astype(BF16)
        loads.wait(5)
        attended = mm(mixed, weights[n, 2])
        centred = attended - jnp.mean(attended, axis=1, keepdims=True)
        inverse = lax.rsqrt(jnp.mean(centred * centred, axis=1, keepdims=True) + EPSILON)
        hatted = centred * inverse
        normed = hatted * gain[n : n + 1, :] + shift[n : n + 1, :]
        hidden = (normed * jax.nn.sigmoid(normed)).astype(BF16)
        stream = stream + mm(hidden, weights[n, 3])
        lefts[4 * n] = stream_low
        lefts[4 * n + 2] = mixed
        lefts[4 * n + 3] = hidden
        rights[4 * n + 1] = query
        keys[n] = query_key
        kept.append((peak + jnp.log(whole), hatted, inverse, normed))
    stream_low = stream.astype(BF16)
    last_low[...] = stream_low
    loads.wait(7)
    split = class_rows.shape[1] - width
    logits = total[:, width : width + classes] + mm_nt(stream_low, class_rows[:, split:])
    chance = jax.nn.sigmoid(logits)
    scores[...] = chance
    valid = facts[:, classes : classes + 1]
    back_logits = (chance - facts[:, :classes]) * valid / clip_total
    back_logits = back_logits.astype(BF16)
    back_logits_ref[...] = back_logits
    back_stream = mm(back_logits, class_rows[:, split:])
    inners = [None, None]
    for n in (1, 0):
        log_sum, hatted, inverse, normed = kept[n]
        back_branch = back_stream.astype(BF16)
        back_normed = mm_nt(back_branch, weights[n, 3]) * silu_slope(normed)
        norms[n : n + 1, :] = jnp.sum(back_normed * hatted, axis=0, keepdims=True)
        norms[n + 2 : n + 3, :] = jnp.sum(back_normed, axis=0, keepdims=True)
        back_hat = back_normed * gain[n : n + 1, :]
        back_attended = inverse * (
            back_hat
            - jnp.mean(back_hat, axis=1, keepdims=True)
            - hatted * jnp.mean(back_hat * hatted, axis=1, keepdims=True)
        )
        back_att_low = back_attended.astype(BF16)
        back_mixed = mm_nt(back_att_low, weights[n, 2]).astype(BF16)
        attention = attention_ref[n]
        back_attention = select(mm_nt(back_mixed, memory[...]))
        inner = jnp.sum(attention * back_attention, axis=1, keepdims=True)
        back_raw = attention * (back_attention - inner) * scale
        back_key_mix = mm(spread(back_raw), memory[...]).astype(BF16)
        back_query = mm(back_key_mix, weights[n, 1]).astype(BF16)
        back_stream = back_stream + mm_nt(back_query, weights[n, 0])
        lefts[4 * n + 1] = back_key_mix
        rights[4 * n] = back_query
        rights[4 * n + 2] = back_att_low
        rights[4 * n + 3] = back_branch
        mixes[n] = back_mixed
        inners[n] = inner
    lane = lax.broadcasted_iota(jnp.int32, stats.shape, 1)
    stats[...] = jnp.where(
        lane == 0,
        kept[0][0],
        jnp.where(
            lane == 1,
            kept[1][0],
            jnp.where(
                lane == 2,
                inners[0],
                jnp.where(lane == 3, inners[1], facts[:, classes + 1 : classes + 2]),
            ),
        ),
    )
    back_low = back_stream.astype(BF16)
    first_low[...] = back_low
    loads.wait(9)
    back_boxes = mm(back_logits, class_rows[:, :split]) + mm_nt(back_low, short[...])
    back_pooled[...] = mm(roi[...], back_boxes.astype(BF16))


def bank_kernel(
    pos, keys, mixes, stats, memory, tag, feats, low, back_logits, last_low, wide, rows
):
    width = memory.shape[1]
    scale = 1.0 / math.sqrt(width)
    allowed = stats[:, 4:5].astype(jnp.int32) == tag[...]
    back_memory = None
    for n in range(2):
        raw = mm_nt(keys[n], memory[...])
        attention = jnp.where(allowed, jnp.exp(raw * scale - stats[:, n : n + 1]), 0.0)
        back_attention = mm_nt(mixes[n], memory[...])
        back_raw = (attention * (back_attention - stats[:, n + 2 : n + 3]) * scale).astype(BF16)
        term = mm_tn(back_raw, keys[n]) + mm_tn(attention.astype(BF16), mixes[n])
        back_memory = term if back_memory is None else back_memory + term
    count, boxes, lanes = low.shape
    low_memory = back_memory.astype(BF16)
    fine = rows.shape[0] // count // (width // LANES)
    for r in range(count):
        values = mm_tn(feats[:, r * lanes : (r + 1) * lanes], low_memory)
        wide[r, fine:, :] = values.astype(BF16)
    classes = back_logits.shape[1]
    rows[...] = jnp.zeros_like(rows)
    for r in range(count):
        rows[r * lanes : (r + 1) * lanes, :classes] = mm_tn(low[r], back_logits[...])
    box = lax.broadcasted_iota(jnp.int32, (boxes, 1), 0)
    mine = (box // (boxes // count)) == 2 * pos[1] + pos[0]
    own_logits = jnp.where(mine, back_logits[...].astype(F32), 0.0).astype(BF16)
    rows[count * lanes :, :classes] = mm_tn(last_low[...], own_logits)
    blocks = width // LANES
    for r in range(count):
        for q in range(blocks):
            start = (r * blocks + q) * fine
            wide[r, :fine, q * LANES : (q + 1) * LANES] = rows[start : start + fine, :].astype(BF16)


def block_kernel(lefts, rights, pick, norms, block):
    own = pick.shape[1]
    for item in range(8):
        columns = mm(lefts[item], pick[...]).astype(BF16)
        block[item * own : (item + 1) * own, :] = mm_tn(columns, rights[item]).astype(BF16)
    block[8 * own :, :] = jnp.zeros((block.shape[0] - 8 * own, block.shape[1]), BF16)
    for n in range(2):
        start = 8 * own + n * 2 * SUBLANES
        block[start : start + 2, :] = norms[2 * n : 2 * n + 2, :].astype(BF16)


def weight_kernel(cols, count, pos, back_expand, plane_out, above, own, below, back_plane, keep, send):
    width = plane_out.shape[1]
    lanes = back_expand.shape[1] // count
    rows = width // count

    def put(start, first, second):
        place = slice(start, start + first.shape[0])

        @pl.when(pos[0] == 0)
        def _():
            keep[place, :] = first.astype(BF16)
            send[place, :] = second.astype(BF16)

        @pl.when(pos[0] != 0)
        def _():
            keep[place, :] = second.astype(BF16)
            send[place, :] = first.astype(BF16)

    each = lanes + 9 * rows
    for chip in range(count // 2):
        block = mm_tn(back_expand[:, 2 * chip * lanes : 2 * (chip + 1) * lanes], plane_out[...])
        put(chip * each, block[:lanes], block[lanes:])
    whole = back_plane[...].astype(F32)
    moved = jnp.concatenate(
        [
            col_shift(whole, cols, -1).astype(BF16),
            back_plane[...],
            col_shift(whole, cols, 1).astype(BF16),
        ],
        axis=1,
    )
    for i, source in enumerate((above, own, below)):
        block = mm_tn(source[...], moved)
        for j in range(3):
            for chip in range(count // 2):
                start = chip * each + lanes + (3 * i + j) * rows
                top = 2 * chip * rows
                columns = slice(j * width, (j + 1) * width)
                put(
                    start,
                    block[top : top + rows, columns],
                    block[top + rows : top + 2 * rows, columns],
                )


def temporal_grad_kernel(clips, cols, count, lanes, pos, *refs):
    sources, pieces = refs[: -3 - count], refs[-3 - count : -3]
    keep, send, moved = refs[-3:]
    step = pl.program_id(0)
    cells, wide = sources[0].shape
    part = pieces[0].shape[1]

    @pl.when(step == 0)
    def _():
        facts = None
        for s, piece in enumerate(pieces):
            values = piece[:cells, :]
            shifts = (frame_shift(values, clips, -cols), values, frame_shift(values, clips, cols))
            for k in range(3):
                moved[k * part : (k + 1) * part, s * cells : (s + 1) * cells] = shifts[k].T
            term = piece[cells:, :].astype(F32)
            facts = term if facts is None else facts + term
        low = facts.astype(BF16)
        each = 3 * lanes + low.shape[0]
        for end in range(each, keep.shape[0] + 1, each):
            keep[end - low.shape[0] : end, :] = low
            send[end - low.shape[0] : end, :] = low

    total, start = None, 0
    for source in sources:
        end = start + source.shape[0]
        term = mm(moved[:, start:end], source[...])
        total = term if total is None else total + term
        start = end
    blocks = wide // (2 * lanes)
    each = 3 * lanes + pieces[0].shape[0] - cells
    for block in range(blocks):
        for k in range(3):
            turned = total[k * part : (k + 1) * part, 2 * block * lanes : 2 * (block + 1) * lanes].T
            start = pl.multiple_of(step * (blocks * each), 16) + block * each + k * lanes
            first = turned[:lanes].astype(BF16)
            second = turned[lanes:].astype(BF16)

            @pl.when(pos[0] == 0)
            def _():
                keep[pl.ds(start, lanes), :] = first
                send[pl.ds(start, lanes), :] = second

            @pl.when(pos[0] != 0)
            def _():
                keep[pl.ds(start, lanes), :] = second
                send[pl.ds(start, lanes), :] = first


def back_plane_kernel(
    clips,
    frames,
    cols,
    back_pooled,
    slope,
    sums,
    expand,
    og,
    plane_sum,
    gain,
    shift,
    back_expand,
    back_plane,
    facts,
    acc,
    rows,
):
    step = pl.program_id(0)
    steps = pl.num_programs(0)
    cells, lanes = slope.shape

    @pl.when(step == 0)
    def _():
        rows[...] = jnp.zeros_like(rows)

    pooled = back_pooled[...].reshape(clips, 1, cols, lanes)
    final = (pooled * slope[...].astype(F32).reshape(clips, frames, cols, lanes)).reshape(cells, lanes)
    rows[pl.ds(step, 1), :] = jnp.sum(final * sums[...].astype(F32), axis=0, keepdims=True)
    rows[pl.ds(steps + step, 1), :] = jnp.sum(final, axis=0, keepdims=True)
    low = (final * og[...]).astype(BF16)
    back_expand[...] = low
    term = mm_nt(low, expand[...])

    @pl.when(step == 0)
    def _():
        acc[...] = term

    @pl.when(step > 0)
    def _():
        acc[...] += term

    @pl.when(step == steps - 1)
    def _():
        back_arg = acc[...] * silu_slope(plane_sum[...] * gain[1:2, :] + shift[1:2, :])
        rows[pl.ds(2 * steps, 1), :] = jnp.sum(back_arg * plane_sum[...], axis=0, keepdims=True)
        rows[pl.ds(2 * steps + 1, 1), :] = jnp.sum(back_arg, axis=0, keepdims=True)
        back_plane[...] = (back_arg * gain[1:2, :]).astype(BF16)
        facts[...] = rows[...].astype(BF16)


def back_temporal_kernel(
    cols, pos, above, own, below, w, temporal_sum, gain, shift, late, out, facts, *pieces
):
    sides = []
    for j in range(3):
        term = mm_nt(below[...], w[0, j]) + mm_nt(own[...], w[1, j]) + mm_nt(above[...], w[2, j])
        sides.append(term)
    back_out = sides[1] + col_shift(sides[0], cols, -1) + col_shift(sides[2], cols, 1)
    back_arg = back_out * silu_slope(temporal_sum[...] * gain[0:1, :] + shift[0:1, :])
    cells, width = out.shape
    facts[...] = late[...].astype(F32)
    facts[facts.shape[0] - 2 : facts.shape[0] - 1, :] = jnp.sum(
        back_arg * temporal_sum[...], axis=0, keepdims=True
    )
    facts[facts.shape[0] - 1 :, :] = jnp.sum(back_arg, axis=0, keepdims=True)
    out[...] = (back_arg * gain[0:1, :]).astype(BF16)
    for s, piece in enumerate(pieces):
        start = pl.multiple_of(pos[2 + s] * LANES, LANES)
        piece[:cells, :] = out[:, pl.ds(start, LANES)]
        rows = facts.shape[0]
        for q in range(width // LANES):
            piece[cells + q * rows : cells + (q + 1) * rows, :] = facts[
                :, q * LANES : (q + 1) * LANES
            ].astype(BF16)


def input_kernel(clips, frames, cols, back, w, back_pooled, slope, out):
    values = back[...]
    cells, lanes = slope.shape
    pooled = back_pooled[...].reshape(clips, 1, cols, lanes)
    total = (pooled * slope[...].astype(F32).reshape(clips, frames, cols, lanes)).reshape(cells, lanes)
    total = total + mm_nt(values, w[1]) + mm_nt(frame_shift(values, clips, -cols), w[0])
    out[...] = total + mm_nt(frame_shift(values, clips, cols), w[2])


def lanes_kernel(counts, forms, pos, *refs):
    outs, whole = refs[-1 - len(counts) : -1], refs[-1]
    rows = whole.shape[0]
    index = 0
    for ref in refs[: -1 - len(counts)]:
        for n in range(ref.shape[0] // rows):
            start = pl.multiple_of(pos[index] * LANES, LANES)
            whole[:, pl.ds(start, LANES)] = ref[n * rows : (n + 1) * rows, :]
            index += 1
    start = 0
    for count, form, out in zip(counts, forms, outs):
        piece = whole[start : start + count, :].astype(F32)
        start += count
        if form == 0:
            out[...] = piece
        elif form == 1:
            out[...] = piece.T
        elif form == 2:
            for q in range(whole.shape[1] // LANES):
                first = q * LANES
                out[:, q * count : (q + 1) * count] = piece[:, first : first + out.shape[0]].T
        else:
            own = out.shape[1]
            shift = whole.shape[1] - pos[pos.shape[0] - 1] * own
            moved = pltpu.roll(piece[: 2 * SUBLANES, :], shift, 1)
            out[...] = moved[: out.shape[0], :own]


def blocks_kernel(codes, pos, *refs):
    sources, outs = refs[: -len(codes)], refs[-len(codes) :]
    for group, out in zip(codes, outs):
        row = 0
        for code in group:
            start = pl.multiple_of(pos[code] * LANES, LANES)
            for source in sources:
                count = source.shape[0]
                out[row : row + count, :] = source[:, pl.ds(start, LANES)]
                row += count


class Halving:
    def __init__(self, held, steps, send, step=0, first=None):
        self.held, self.steps, self.send = held, steps, send
        self.step, self.got, self.first = step, None, first

    def advance(self, hold):
        if self.got is not None:
            self.held = take(self.held, self.step - 1, self.got)
            self.got = None
        if self.step < self.steps:
            buffer = give(self.held, self.step) if self.first is None else self.first
            self.first = None
            buffer, hold = lax.optimization_barrier((buffer, hold))
            self.got = self.send(self.step, buffer)
            self.step += 1
        return hold

    def finish(self):
        while self.got is not None:
            self.advance(())
        return self.held[0]


class Doubling:
    def __init__(self, own, steps, send):
        self.parts, self.steps, self.send = [own], steps, send
        self.step, self.got = 0, None

    def advance(self, hold):
        if self.got is not None:
            self.parts.append(self.got)
            self.got = None
        if self.step < self.steps:
            buffer = self.parts[0] if self.step == 0 else jnp.concatenate(self.parts, axis=0)
            buffer, hold = lax.optimization_barrier((buffer, hold))
            self.got = self.send(self.step, buffer)
            self.step += 1
        return hold

    def finish(self):
        while self.got is not None:
            self.advance(())
        return self.parts


def window(values, chains):
    chains = [chain for chain in chains if chain.got is not None]
    tied = lax.optimization_barrier((tuple(values), tuple(chain.got for chain in chains)))
    for chain, got in zip(chains, tied[1]):
        chain.got = got
    return tied[0]


def join_lanes(parts, places):
    rows = parts[0].shape[0]
    blocks = [part[n * rows : (n + 1) * rows] for part in parts for n in range(part.shape[0] // rows)]
    joined = []
    for target in range(len(blocks)):
        chosen = blocks[0]
        for code in range(1, len(blocks)):
            chosen = jnp.where(places[code] == target, blocks[code], chosen)
        joined.append(chosen)
    return jnp.concatenate(joined, axis=-1).astype(F32)


def body(
    clip_input,
    temporal,
    spatial,
    expand,
    mid_gain,
    mid_shift,
    out_gain,
    out_shift,
    short_weight,
    bank_weight,
    block_weight,
    norm_gain,
    norm_shift,
    class_weight,
    bank_feats,
    bank_mask,
    box_coords,
    box_clip,
    box_valid,
    labels,
):
    row = lax.axis_index("row")
    group = lax.axis_index("clip")
    row_size = lax.axis_size("row")
    clip_size = lax.axis_size("clip")
    core = row % 2
    chip = row // 2
    chips = row_size // 2
    clips, frames, rows_local, cols, channels = clip_input.shape
    mid = temporal.shape[2]
    width = short_weight.shape[1]
    classes = class_weight.shape[1]
    cells = clips * frames * cols
    boxes = box_coords.shape[0]
    box_local = labels.shape[0]
    slots_local = bank_feats.shape[1]
    part = mid // clip_size
    steps = channels // mid
    lanes = channels // row_size
    crossed = clip_size == 4
    masks = [(s, s) for s in range(clip_size)]
    if crossed:
        masks = [(0, 0), (1, 2), (2, 1), (3, 3)]
    targets = [group ^ jnp.where(core == 0, first, second) for first, second in masks]
    place = jnp.stack([core, chip, *targets]).astype(jnp.int32)
    og, os = out_gain[None], out_shift[None]

    tie = lax.optimization_barrier
    source = clip_input.reshape(cells, channels)

    wide_input = [source]
    if not crossed:
        wide_input += [swap(source, "clip", s) for s in range(1, clip_size)]

    def passed(values, after, even_mask, odd_mask):
        values, _ = tie((values, after))
        return joint_swap(values, even_mask, odd_mask)

    def kernel_row(i):
        return pl.BlockSpec((1, 3, mid, mid), lambda _: (i, 0, 0, 0))

    def fixed(*shape):
        return pl.BlockSpec(shape, lambda i: (0,) * len(shape))

    def across(height, lane_count):
        return pl.BlockSpec((height, lane_count), lambda i: (0, i))

    eighth = cells // 8
    cuts = [(0, 2), (2, 4), (6, 2), (0, 1), (1, 6), (7, 1)] if crossed else []
    temporal_sum, temporal_out, *cut_rows = run(
        lambda *refs: temporal_kernel(clips, cols, [start * eighth for start, _ in cuts], *refs),
        [shape_of((cells, mid), F32), shape_of((cells, mid), BF16)]
        + [shape_of((count * eighth, channels), BF16) for _, count in cuts],
        [source, temporal, mid_gain, mid_shift],
        grid=(steps,),
        in_specs=[
            across(cells, mid),
            pl.BlockSpec((3, mid, mid), lambda i: (0, i, 0)),
            fixed(2, mid),
            fixed(2, mid),
        ],
        out_specs=[fixed(cells, mid), fixed(cells, mid)]
        + [across(count * eighth, mid) for _, count in cuts],
    )

    def halo(values):
        ends = row_size - 1
        above = lax.ppermute(values, "row", [(i, i + 1) for i in range(ends)])
        below = lax.ppermute(values, "row", [(i + 1, i) for i in range(ends)])
        return above, below

    above_row, below_row = halo(temporal_out)

    if crossed:
        first_a = joint_swap(cut_rows[0], 1, 2)
    feats, box_coords, temporal_out = tie(
        (bank_feats.reshape(clips * slots_local, channels), box_coords, temporal_out)
    )
    memory_own = mm(feats, bank_weight).astype(BF16)
    clip_group = box_clip - group * clips
    weights = box_weights(
        box_coords, clip_group, row * rows_local, rows_local, rows_local * row_size, clips, cols
    ).reshape(boxes, clips * cols).T
    class_rows = class_weight.T

    (plane_part,) = run(
        lambda *refs: plane_own_kernel(cols, *refs),
        [shape_of((cells, mid), F32)],
        [temporal_out, spatial],
        grid=(1,),
        in_specs=[fixed(cells, mid), kernel_row(1)],
        out_specs=[fixed(cells, mid)],
    )
    above_row, below_row, memory_own, plane_part = tie(
        (above_row, below_row, memory_own, plane_part)
    )
    memory = lax.all_gather(
        memory_own.reshape(clips, slots_local, width), "row", axis=1, tiled=True
    ).reshape(-1, width)
    tied = (above_row, below_row, plane_part, weights, class_rows)
    if crossed:
        *tied, first_a = tie((*tied, first_a))
    else:
        tied = tie(tied)
    above_row, below_row, plane_part, weights, class_rows = tied
    if crossed:
        first_b = passed(cut_rows[1], above_row, 1, 2)
    half = boxes // 2
    joint = width + LANES
    plane_sum, plane_out, partial_low, mine, other = run(
        lambda *refs: plane_kernel(clips, frames, cols, *refs),
        [
            shape_of((cells, mid), F32),
            shape_of((cells, mid), BF16),
            shape_of((row_size, boxes, lanes), BF16),
            shape_of((half, joint), F32),
            shape_of((half, joint), BF16),
        ],
        [
            place,
            above_row,
            below_row,
            spatial,
            spatial,
            plane_part,
            mid_gain,
            mid_shift,
            expand,
            source,
            og,
            os,
            weights,
            short_weight,
            class_rows,
        ],
        grid=(steps,),
        in_specs=[
            SMEM,
            fixed(cells, mid),
            fixed(cells, mid),
            kernel_row(0),
            kernel_row(2),
            fixed(cells, mid),
            fixed(2, mid),
            fixed(2, mid),
            across(mid, mid),
            across(cells, mid),
            across(1, mid),
            across(1, mid),
            fixed(clips * cols, boxes),
            pl.BlockSpec((mid, width), lambda i: (i, 0)),
            across(classes, mid),
        ],
        out_specs=[
            fixed(cells, mid),
            fixed(cells, mid),
            pl.BlockSpec((mid // lanes, boxes, lanes), lambda i: (i, 0, 0)),
            fixed(half, joint),
            fixed(half, joint),
        ],
        scratch=[pltpu.VMEM((boxes, joint), F32)],
    )

    if crossed:
        mine, other, plane_out, first_b = tie((mine, other, plane_out, first_b))
        first_c = passed(cut_rows[2], mine, 1, 2)
        second_a = passed(cut_rows[3], mine, 2, 1)
    clip_own = lax.dynamic_slice_in_dim(clip_group, row * box_local, box_local, 0)
    facts = jnp.concatenate(
        [labels.astype(BF16), box_valid.astype(BF16)[:, None], clip_own.astype(BF16)[:, None]], axis=1
    )
    facts = jnp.pad(facts, ((0, 0), (0, LANES - facts.shape[1])))
    facts = jnp.concatenate([facts[: box_local // 2], facts[box_local // 2 :]], axis=1)
    facts = jnp.pad(facts, ((0, 0), (0, joint - 2 * LANES)))
    half_sum = mine + swap(other, "row", 1).astype(F32)
    quarter = half // 2
    side = chip % 2
    got = swap(
        lax.dynamic_slice_in_dim(half_sum, (1 - side) * quarter, quarter, 0).astype(BF16), "row", 2
    )
    plane_late, _ = tie((plane_out, half_sum))
    expand_sums, slope = run(
        lambda *refs: slope_kernel(frames, *refs),
        [shape_of((cells, channels), BF16), shape_of((cells, channels), BF16)],
        [plane_late, expand, source, og, os],
        grid=(steps,),
        in_specs=[
            fixed(cells, mid),
            across(mid, mid),
            across(cells, mid),
            across(1, mid),
            across(1, mid),
        ],
        out_specs=[across(cells, mid)] * 2,
    )
    if crossed:
        got, slope, first_c, second_a = tie((got, slope, first_c, second_a))
    else:
        got, slope = tie((got, slope))
    part_sum = lax.dynamic_slice_in_dim(half_sum, side * quarter, quarter, 0) + got.astype(F32)
    label_rows, codes = [facts], [0]
    for t in range(1, bits(chips)):
        payload = jnp.concatenate([part_sum.astype(BF16)] + label_rows, axis=0)
        got = swap(payload, "row", 2 << t)
        part_sum = part_sum + got[:quarter].astype(F32)
        each = facts.shape[0]
        label_rows = label_rows + [
            got[quarter + n * each : quarter + (n + 1) * each] for n in range(len(codes))
        ]
        codes = codes + [code ^ (1 << t) for code in codes]
    got = swap(jnp.concatenate([part_sum.astype(BF16)] + label_rows, axis=0), "row", 2)
    live = bank_mask == 1
    tags = jnp.where(live, jnp.arange(clips, dtype=jnp.int32)[:, None], -1)
    tags_own = lax.dynamic_slice_in_dim(tags, row * slots_local, slots_local, 1).reshape(1, -1)
    bias = jnp.where(live, 0.0, -jnp.inf).astype(F32)
    got, memory, bias = tie((got, memory, bias))
    (totals_own,) = run(
        lambda *refs: total_kernel(codes + [code ^ 1 for code in codes], *refs),
        [shape_of((half + chips * facts.shape[0], joint), F32)],
        [place, part_sum, got, *label_rows],
        in_specs=[SMEM] + [VMEM] * (2 + len(label_rows)),
    )
    totals_other = swap(totals_own, "row", 1)
    if crossed:
        second_b = passed(cut_rows[4], totals_own, 2, 1)

    partial_low, totals_other = tie((partial_low, totals_other))
    short_columns = lax.psum_scatter(partial_low, "row", scatter_dimension=0, tiled=False)

    slots = bias.shape[1]
    stream_shape = (boxes, width)
    (
        scores_all,
        back_pooled,
        lefts,
        rights,
        keys,
        mixes,
        stats,
        last_low,
        first_low,
        back_logits,
        norms,
    ) = run(
        lambda *refs: box_kernel(chips, classes, float(clips * clip_size), *refs),
        [
            shape_of((boxes, classes), F32),
            shape_of((clips * cols, channels), F32),
            shape_of((8, *stream_shape), BF16),
            shape_of((8, *stream_shape), BF16),
            shape_of((2, *stream_shape), BF16),
            shape_of((2, *stream_shape), BF16),
            shape_of((boxes, LANES), F32),
            shape_of(stream_shape, BF16),
            shape_of(stream_shape, BF16),
            shape_of((boxes, classes), BF16),
            shape_of((4, width), F32),
        ],
        [
            place,
            totals_own,
            totals_other,
            bias,
            norm_gain,
            norm_shift,
            memory,
            block_weight,
            class_rows,
            short_weight,
            weights,
        ],
        in_specs=[SMEM] + [VMEM] * 5 + [ANY] * 5,
        scratch=[
            pltpu.VMEM((boxes, joint), F32),
            pltpu.VMEM((boxes, LANES), F32),
            pltpu.VMEM((2, boxes, slots), F32),
            pltpu.VMEM(memory.shape, BF16),
            pltpu.VMEM(block_weight.shape, BF16),
            pltpu.VMEM(class_rows.shape, BF16),
            pltpu.VMEM(short_weight.shape, BF16),
            pltpu.VMEM(weights.shape, BF16),
            pltpu.SemaphoreType.DMA((9,)),
        ],
    )
    scores = lax.dynamic_slice_in_dim(scores_all, row * box_local, box_local, 0)

    if crossed:
        back_pooled, second_b = tie((back_pooled, second_b))
        third_a = passed(first_a, back_pooled, 2, 1)

    fact_rows = -(-(2 * steps + 2) // 16) * 16
    back_expand, back_plane, second_facts = run(
        lambda *refs: back_plane_kernel(clips, frames, cols, *refs),
        [
            shape_of((cells, channels), BF16),
            shape_of((cells, mid), BF16),
            shape_of((fact_rows, mid), BF16),
        ],
        [
            back_pooled,
            slope,
            expand_sums,
            expand,
            og,
            plane_sum,
            mid_gain,
            mid_shift,
        ],
        grid=(steps,),
        in_specs=[
            across(clips * cols, mid),
            across(cells, mid),
            across(cells, mid),
            across(mid, mid),
            across(1, mid),
            fixed(cells, mid),
            fixed(2, mid),
            fixed(2, mid),
        ],
        out_specs=[
            across(cells, mid),
            fixed(cells, mid),
            fixed(fact_rows, mid),
        ],
        scratch=[pltpu.VMEM((cells, mid), F32), pltpu.VMEM((fact_rows, mid), F32)],
    )

    if crossed:
        back_plane, back_expand, second_facts, third_a = tie(
            (back_plane, back_expand, second_facts, third_a)
        )
        second_c = passed(cut_rows[5], back_plane, 2, 1)
        third_b = passed(first_b, back_plane, 2, 1)
    back_above, back_below = halo(back_plane)

    fact_count = second_facts.shape[0]
    own_mid = mid // row_size
    own_rows = channels // row_size

    weight_rows = own_rows + 9 * own_mid
    kept_weight, sent_weight = run(
        lambda *refs: weight_kernel(cols, row_size, *refs),
        [shape_of((chips * weight_rows, mid), BF16)] * 2,
        [
            place,
            back_expand,
            plane_out,
            above_row,
            temporal_out,
            below_row,
            back_plane,
        ],
        in_specs=[SMEM] + [VMEM] * 6,
    )
    tied = (back_above, back_below, kept_weight, sent_weight, short_columns)
    if crossed:
        *tied, second_c, third_b = tie((*tied, second_c, third_b))
        third_c = passed(first_c, sent_weight, 2, 1)
        wide_input += [first_a, first_b, first_c, second_a, second_b, second_c]
        wide_input += [third_a, third_b, third_c]
    else:
        tied = tie(tied)
    back_above, back_below, kept_weight, sent_weight, short_columns = tied
    got_weight = swap(sent_weight, "row", 1)

    even, odd = step_masks(clip_size)
    places = [place_of(code, group, core) for code in range(clip_size)]
    block_places = jnp.stack([jnp.asarray(item, jnp.int32) for item in places])

    def clip_step(t, values):
        return joint_swap(values, even[t], odd[t])

    def chip_step(t, values):
        return swap(values, "row", 2 << t)

    def lane_block(values, target):
        return lax.dynamic_slice_in_dim(values, target * part, part, 1)

    def chip_rows(target, *values):
        each = values[0].shape[0] // chips
        rows = [lax.dynamic_slice_in_dim(item, target * each, each, 0) for item in values]
        if len(rows) == 1:
            return rows[0]
        return tree_sum([item.astype(F32) for item in rows]).astype(BF16)

    def over_chips(*values):
        return Halving(
            {code: chip_rows(chip ^ code, *values) for code in range(chips)}, bits(chips), chip_step
        )

    def over_clips(piece):
        return Halving(
            {code: piece(places[code]) for code in range(clip_size)}, bits(clip_size), clip_step
        )

    class_fine = (channels + width) // row_size * LANES // width
    keys, _ = tie((keys, sent_weight))
    (wide_part,) = run(
        bank_kernel,
        [shape_of((row_size, class_fine + own_rows, width), BF16)],
        [
            place,
            keys,
            mixes,
            stats,
            memory_own,
            tags_own,
            feats,
            partial_low,
            back_logits,
            last_low,
        ],
        in_specs=[SMEM] + [VMEM] * 9,
        scratch=[pltpu.VMEM((channels + width, LANES), F32)],
    )
    if crossed:
        got_weight, wide_part, third_c = tie((got_weight, wide_part, third_c))
        wide_input[-3:] = [third_a, third_b, third_c]
    else:
        got_weight, wide_part = tie((got_weight, wide_part))
    wide_own = lax.psum_scatter(wide_part, "row", scatter_dimension=0, tiled=False)

    held = {
        code: (
            lane_block(kept_weight, target).astype(F32) + lane_block(got_weight, target).astype(F32)
        ).astype(BF16)
        for code, target in enumerate(places)
    }
    high = [code for code in range(clip_size) if code & 1]
    late, early = high[: len(high) // 2], high[len(high) // 2 :]
    buffers, back_above = tie((tuple(held[code] for code in early), back_above))
    first_step = {code: clip_step(0, values) for code, values in zip(early, buffers)}

    direct = part == LANES
    piece_rows = fact_rows * (mid // part)
    back_temporal, facts_own, *pieces = run(
        lambda *refs: back_temporal_kernel(cols, *refs),
        [shape_of((cells, mid), BF16), shape_of((fact_rows, mid), F32)]
        + [shape_of((cells + piece_rows, part), BF16)] * (clip_size if direct else 0),
        [
            place,
            back_above,
            back_plane,
            back_below,
            spatial,
            temporal_sum,
            mid_gain,
            mid_shift,
            second_facts,
        ],
        in_specs=[SMEM] + [VMEM] * 8,
    )
    if not direct:
        facts_flat = jnp.concatenate(
            [facts_own[:, q * part : (q + 1) * part] for q in range(mid // part)], axis=0
        ).astype(BF16)
        pieces = [
            jnp.concatenate(
                [lax.dynamic_slice_in_dim(back_temporal, target * part, part, 1), facts_flat], axis=0
            )
            for target in targets
        ]
    back_temporal, first_step, pieces = tie((back_temporal, first_step, tuple(pieces)))

    got = pieces[:1] + tuple(
        joint_swap(piece, *step_mask) for piece, step_mask in zip(pieces[1:], masks[1:])
    )
    pick = (
        jnp.arange(width, dtype=jnp.int32)[:, None]
        == row * own_mid + jnp.arange(own_mid, dtype=jnp.int32)[None, :]
    ).astype(BF16)
    lefts, _ = tie((lefts, back_temporal))
    (block_part,) = run(
        block_kernel,
        [shape_of((8 * own_mid + 32, width), BF16)],
        [lefts, rights, pick, norms],
    )
    short_part = mm_tn(short_columns, first_low).astype(BF16)
    got, block_part, short_part = tie((got, block_part, short_part))

    buffers, got = tie((tuple(held[code] for code in late), got))
    first_step.update({code: clip_step(0, values) for code, values in zip(late, buffers)})
    temporal_rows = chips * (3 * own_rows + piece_rows)
    kept_temporal, sent_temporal = run(
        lambda *refs: temporal_grad_kernel(clips, cols, clip_size, lanes, *refs),
        [shape_of((temporal_rows, part), BF16)] * 2,
        [place, *wide_input, *got],
        grid=(steps,),
        in_specs=[SMEM]
        + [across(item.shape[0], mid) for item in wide_input]
        + [fixed(cells + piece_rows, part)] * clip_size,
        out_specs=[fixed(temporal_rows, part)] * 2,
        scratch=[pltpu.VMEM((3 * part, clip_size * cells), BF16)],
    )
    tied = tie((kept_temporal, sent_temporal, first_step))
    kept_temporal, sent_temporal, first_step = tied
    got_temporal = swap(sent_temporal, "row", 1)
    sums_weight = Halving(
        {
            code ^ 1: held[code ^ 1].astype(F32) + values.astype(F32)
            for code, values in first_step.items()
        },
        bits(clip_size),
        clip_step,
        step=1,
    )
    got_temporal = sums_weight.advance(got_temporal)
    sums_temporal = over_chips(kept_temporal, got_temporal)
    back_temporal = sums_temporal.advance(back_temporal)

    (input_grad,) = run(
        lambda *refs: input_kernel(clips, frames, cols, *refs),
        [shape_of((cells, channels), F32)],
        [back_temporal, temporal, back_pooled, slope],
        grid=(steps,),
        in_specs=[
            fixed(cells, mid),
            pl.BlockSpec((3, mid, mid), lambda i: (0, i, 0)),
            across(clips * cols, mid),
            across(cells, mid),
        ],
        out_specs=[across(cells, mid)],
    )
    input_grad = input_grad.reshape(clip_input.shape)

    box_wide = [wide_own.reshape(-1, width), block_part, short_part]
    box_rows = sum(item.shape[0] for item in box_wide)
    if direct:
        groups = [[code for code in range(clip_size) if code & 1 == bit] for bit in (0, 1)]
        kept_box, sent_box = run(
            lambda *refs: blocks_kernel(groups, *refs),
            [shape_of((len(groups[0]) * box_rows, part), BF16)] * 2,
            [block_places, *box_wide],
            in_specs=[SMEM] + [VMEM] * len(box_wide),
        )
        input_grad, kept_box, sent_box = window(
            [input_grad, kept_box, sent_box], [sums_weight, sums_temporal]
        )
        sums_box = Halving(
            {
                code: kept_box[n * box_rows : (n + 1) * box_rows]
                for n, code in enumerate(groups[0])
            },
            bits(clip_size),
            clip_step,
            first=sent_box,
        )
    else:
        (input_grad,) = window([input_grad], [sums_weight, sums_temporal])
        sums_box = over_clips(
            lambda target: jnp.concatenate([lane_block(item, target) for item in box_wide], axis=0)
        )
    sums_weight.got = sums_temporal.advance(sums_weight.got)
    sums_chip = over_chips(sums_weight.finish().astype(BF16))
    sums_chip.advance(())
    sums_box.advance(())
    window([], [sums_temporal, sums_chip, sums_box])
    sums_chip.advance(())
    sums_box.advance(())
    temporal_got = sums_temporal.finish()
    own_temporal = 3 * own_rows
    facts_total = temporal_got[own_temporal:].reshape(mid // part, fact_rows, part)
    facts_total = jnp.concatenate([facts_total[q] for q in range(mid // part)], axis=1)
    all_first = Doubling(temporal_got[:own_temporal].astype(BF16), bits(clip_size), clip_step)
    all_first.advance(())
    window([], [sums_chip, sums_box, all_first])
    all_first.advance(())
    weight_own = sums_chip.finish().astype(BF16)
    box_own = sums_box.finish().astype(BF16)
    all_last = Doubling(
        jnp.concatenate([weight_own, box_own], axis=0), bits(clip_size), clip_step
    )
    all_last.advance(())
    window([], [all_first, all_last])
    all_last.advance(())
    firsts = all_first.finish()
    lasts = all_last.finish()
    class_count = class_fine * width // LANES
    last_counts = [own_rows, 9 * own_mid, class_fine, own_rows, 8 * own_mid, 16, 16, own_rows]
    last_shapes = [(mid, own_rows), (9 * own_mid, mid), (classes, class_count), (own_rows, width)]
    last_shapes += [(8 * own_mid, width), (2, own_mid), (2, own_mid), (own_rows, width)]

    def assemble(parts, counts, shapes, forms):
        if direct:
            return run(
                lambda *refs: lanes_kernel(counts, forms, *refs),
                [shape_of(shape, F32) for shape in shapes],
                [jnp.append(block_places, row.astype(jnp.int32)), *parts],
                in_specs=[SMEM] + [VMEM] * len(parts),
                scratch=[pltpu.VMEM((sum(counts), width), BF16)],
            )
        whole = join_lanes(parts, places)
        ends = [sum(counts[: k + 1]) for k in range(len(counts))]
        outs = []
        for count, end, shape, form in zip(counts, ends, shapes, forms):
            piece = whole[end - count : end]
            if form == 1:
                piece = piece.T
            if form == 2:
                piece = jnp.concatenate(
                    [piece[:, q * LANES : q * LANES + shape[0]].T for q in range(width // LANES)],
                    axis=1,
                )
            if form == 3:
                piece = lax.dynamic_slice_in_dim(piece[: shape[0]], row * shape[1], shape[1], 1)
            outs.append(piece)
        return outs

    (temporal_grad,) = assemble(firsts, [own_temporal], [(own_temporal, mid)], (0,))
    expand_grad, spatial_grad, class_grad, bank_grad, block_grad, *norm_grads, short_grad = assemble(
        lasts, last_counts, last_shapes, (1, 0, 2, 0, 0, 3, 3, 0)
    )
    class_grad = class_grad.T
    temporal_grad = temporal_grad.reshape(3, own_rows, mid)
    spatial_grad = spatial_grad.reshape(3, 3, own_mid, mid)
    block_grad = block_grad.reshape(2, 4, own_mid, width)
    out_gain_all = facts_total[:steps].reshape(-1)
    out_shift_all = facts_total[steps : 2 * steps].reshape(-1)
    out_gain_grad = lax.dynamic_slice_in_dim(out_gain_all, row * own_rows, own_rows, 0)
    out_shift_grad = lax.dynamic_slice_in_dim(out_shift_all, row * own_rows, own_rows, 0)
    gain_all = jnp.stack([facts_total[fact_rows - 2], facts_total[2 * steps]])
    shift_all = jnp.stack([facts_total[fact_rows - 1], facts_total[2 * steps + 1]])
    mid_gain_grad = lax.dynamic_slice_in_dim(gain_all, row * own_mid, own_mid, 1)
    mid_shift_grad = lax.dynamic_slice_in_dim(shift_all, row * own_mid, own_mid, 1)
    return (
        scores,
        input_grad,
        temporal_grad,
        spatial_grad,
        expand_grad,
        mid_gain_grad,
        mid_shift_grad,
        out_gain_grad,
        out_shift_grad,
        short_grad,
        bank_grad,
        block_grad,
        *norm_grads,
        class_grad,
    )


def solution(mesh):
    whole = P()
    in_specs = (
        (P("clip", None, "row", None, None),)
        + (whole,) * 13
        + (
            P("clip", "row", None),
            P("clip", None),
            P("clip", None),
            P("clip"),
            P(("clip", "row")),
            P(("clip", "row"), None),
        )
    )
    out_specs = (
        P(("clip", "row"), None),
        P("clip", None, "row", None, None),
        P(None, "row", None),
        P(None, None, "row", None),
        P(None, "row"),
        P(None, "row"),
        P(None, "row"),
        P("row"),
        P("row"),
        P("row", None),
        P("row", None),
        P(None, None, "row", None),
        P(None, "row"),
        P(None, "row"),
        P("row", None),
    )
    return jax.shard_map(body, mesh=mesh, in_specs=in_specs, out_specs=out_specs, check_vma=False)
```

```python
import math

import jax
import jax.numpy as jnp
from jax import lax
from jax.experimental import pallas as pl
from jax.experimental.pallas import tpu as pltpu
from jax.sharding import PartitionSpec as P

SAMPLES = 14
LANES = 128
SUBLANES = 8
EPSILON = 1e-05
F32 = jnp.float32
BF16 = jnp.bfloat16


def dot(left, right, dims):
    return lax.dot_general(left, right, (dims, ((), ())), preferred_element_type=F32)


def mm(left, right):
    return dot(left, right, ((1,), (0,)))


def mm_nt(left, right):
    return dot(left, right, ((1,), (1,)))


def mm_tn(left, right):
    return dot(left, right, ((0,), (0,)))


def swap(values, axis, mask):
    count = lax.axis_size(axis)
    return lax.ppermute(values, axis, [(i, i ^ mask) for i in range(count)])


def tree_sum(parts):
    while len(parts) > 1:
        parts = [parts[i] + parts[i + 1] for i in range(0, len(parts), 2)]
    return parts[0]


def step_masks(count):
    even = [1 << t for t in range(count.bit_length() - 1)]
    odd = list(even)
    for t in range(0, len(odd) - 1, 2):
        odd[t], odd[t + 1] = odd[t + 1], odd[t]
    return even, odd


def joint_swap(values, even_mask, odd_mask):
    clip_size = lax.axis_size("clip")
    row_size = lax.axis_size("row")
    pairs = []
    for c in range(clip_size):
        for r in range(row_size):
            mask = odd_mask if r % 2 else even_mask
            pairs.append((c * row_size + r, (c ^ mask) * row_size + r))
    return lax.ppermute(values, ("clip", "row"), pairs)


def place_of(code, group, core):
    even, odd = step_masks(lax.axis_size("clip"))
    first = sum(m for t, m in enumerate(even) if code >> t & 1)
    second = sum(m for t, m in enumerate(odd) if code >> t & 1)
    return group ^ (first if first == second else jnp.where(core == 0, first, second))


def give(held, t):
    return jnp.concatenate([held[code].astype(BF16) for code in held if code >> t & 1], axis=0)


def take(held, t, got):
    low = [code for code in held if not code >> t & 1]
    rows = got.shape[0] // len(low)
    return {
        code: held[code].astype(F32) + got[n * rows : (n + 1) * rows].astype(F32)
        for n, code in enumerate(low)
    }


def bits(count):
    return count.bit_length() - 1


def pad_rows(values, rows):
    return jnp.pad(values, ((0, rows - values.shape[0]), (0, 0)))


def axis_weights(low_edge, high_edge, cell_count, first_cell, span_count):
    samples = (jnp.arange(SAMPLES, dtype=F32) + 0.5) / SAMPLES
    start_pos = low_edge.astype(F32) * 0.25
    extent = (high_edge - low_edge).astype(F32) * 0.25
    points = start_pos[:, None] + extent[:, None] * samples[None, :]
    points = jnp.clip(points - 0.5, 0.0, cell_count - 1.0)
    centers = (first_cell + jnp.arange(span_count, dtype=jnp.int32)).astype(F32)
    tents = jnp.maximum(0.0, 1.0 - jnp.abs(points[:, :, None] - centers[None, None, :]))
    return jnp.mean(tents, axis=1)


def box_weights(coords, clip_local, first_row, row_count, rows_total, clip_count, col_count):
    along_rows = axis_weights(coords[:, 0], coords[:, 1], rows_total, first_row, row_count)
    along_cols = axis_weights(coords[:, 2], coords[:, 3], col_count, 0, col_count)
    member = (clip_local[:, None] == jnp.arange(clip_count, dtype=jnp.int32)[None, :]).astype(F32)
    product = along_rows[:, None, :, None] * along_cols[:, None, None, :] * member[:, :, None, None]
    return product.astype(BF16)


def silu_slope(value_in):
    gate = jax.nn.sigmoid(value_in)
    return gate * (1.0 + value_in * (1.0 - gate))


VMEM = pl.BlockSpec(memory_space=pltpu.VMEM)
SMEM = pl.BlockSpec(memory_space=pltpu.SMEM)
MIB = 1024 * 1024
MIB_DEFAULT = 58


ANY = pl.BlockSpec(memory_space=pl.ANY)


class Loads:
    def __init__(self, pairs, sems):
        self.copies = [
            pltpu.make_async_copy(source, target, sems.at[n])
            for n, (source, target) in enumerate(pairs)
        ]
        self.done = 0
        for copy in self.copies:
            copy.start()

    def wait(self, count):
        while self.done < count:
            self.copies[self.done].wait()
            self.done += 1


class Stores:
    def __init__(self, sems):
        self.sems, self.copies = sems, []

    def start(self, source, target):
        copy = pltpu.make_async_copy(source, target, self.sems.at[len(self.copies)])
        copy.start()
        self.copies.append(copy)

    def finish(self):
        for copy in self.copies:
            copy.wait()


def shape_of(shape, dtype):
    return jax.ShapeDtypeStruct(shape, dtype)


def run(kernel, outs, ins, grid=(), in_specs=None, out_specs=None, scratch=(), mib=MIB_DEFAULT):
    return pl.pallas_call(
        kernel,
        grid=grid,
        out_shape=tuple(outs),
        in_specs=in_specs or [VMEM] * len(ins),
        out_specs=tuple(out_specs or [VMEM] * len(outs)),
        scratch_shapes=list(scratch),
        compiler_params=pltpu.CompilerParams(vmem_limit_bytes=mib * MIB),
        cost_estimate=pl.CostEstimate(flops=0, bytes_accessed=0, transcendentals=0),
    )(*ins)


def frame_shift(values, clips, step):
    grid = values.reshape(clips, -1, values.shape[1])
    rows = grid.shape[1]
    zeros = jnp.zeros((clips, abs(step), values.shape[1]), values.dtype)
    if step > 0:
        moved = jnp.concatenate([zeros, grid[:, : rows - step]], axis=1)
    else:
        moved = jnp.concatenate([grid[:, -step:], zeros], axis=1)
    return moved.reshape(values.shape)


def col_shift(values, cols, step):
    col = lax.broadcasted_iota(jnp.int32, (values.shape[0], 1), 0) % cols
    edge = 0 if step > 0 else cols - 1
    rows = values.shape[0]
    return jnp.where(col == edge, 0.0, pltpu.roll(values, step % rows, 0))


def temporal_kernel(clips, cols, starts, x, w, gain, shift, total, out, *pieces):
    step = pl.program_id(0)
    values = x[...]
    for start, piece in zip(starts, pieces):
        piece[...] = x[start : start + piece.shape[0], :]
    term = mm(frame_shift(values, clips, cols), w[0]) + mm(values, w[1])
    term = term + mm(frame_shift(values, clips, -cols), w[2])

    @pl.when(step == 0)
    def _():
        total[...] = term

    @pl.when(step > 0)
    def _():
        total[...] += term

    @pl.when(step == pl.num_programs(0) - 1)
    def _():
        arg = total[...] * gain[0:1, :] + shift[0:1, :]
        out[...] = (arg * jax.nn.sigmoid(arg)).astype(BF16)


def plane_rows_sum(rows, weights, cols):
    sides = []
    for j in range(3):
        term = None
        for values, kernel in zip(rows, weights):
            part = mm(values, kernel[j])
            term = part if term is None else term + part
        sides.append(term)
    return sides[1] + col_shift(sides[0], cols, 1) + col_shift(sides[2], cols, -1)


def plane_own_kernel(cols, own, w, out):
    out[...] = plane_rows_sum([own[...]], [w[0]], cols)


def plane_kernel(
    clips,
    frames,
    cols,
    pos,
    above,
    below,
    first,
    last,
    part,
    gain,
    shift,
    expand,
    x,
    og,
    os,
    weights,
    short,
    classes,
    total,
    out,
    low,
    mine,
    other,
    projected,
):
    step = pl.program_id(0)

    @pl.when(step == 0)
    def _():
        whole = part[...] + plane_rows_sum([above[...], below[...]], [first[0], last[0]], cols)
        total[...] = whole
        arg = whole * gain[1:2, :] + shift[1:2, :]
        out[...] = (arg * jax.nn.sigmoid(arg)).astype(BF16)
        projected[...] = jnp.zeros_like(projected)

    arg = mm(out[...], expand[...]) * og[...] + os[...] + x[...].astype(F32)
    active = arg * jax.nn.sigmoid(arg)
    summed = jnp.sum(active.reshape(clips, frames, cols, -1), axis=1)
    pooled = (summed / frames).reshape(clips * cols, -1).astype(BF16)
    values = mm_tn(weights[...], pooled).astype(BF16)
    lanes = low.shape[2]
    for r in range(low.shape[0]):
        low[r] = values[:, r * lanes : (r + 1) * lanes]
    width = short.shape[1]
    count = classes.shape[0]
    projected[:, :width] += mm(values, short[...])
    projected[:, width : width + count] += mm_nt(values, classes[...])

    @pl.when(step == pl.num_programs(0) - 1)
    def _():
        half = mine.shape[0]
        mine[...] = projected[pl.ds(pos[0] * half, half), :]
        other[...] = projected[pl.ds((1 - pos[0]) * half, half), :].astype(BF16)


def slope_kernel(frames, plane_out, expand, x, og, os, sums, slope):
    expand_sum = mm(plane_out[...], expand[...])
    sums[...] = expand_sum.astype(BF16)
    arg = expand_sum * og[...] + os[...] + x[...].astype(F32)
    slope[...] = (silu_slope(arg) * (1.0 / frames)).astype(BF16)


def box_kernel(
    order,
    classes,
    clip_total,
    pos,
    own,
    other,
    bias,
    gain,
    shift,
    memory_far,
    weights_far,
    class_far,
    short_far,
    roi_far,
    scores,
    back_pooled,
    lefts,
    rights,
    keys,
    mixes,
    stats,
    last_low,
    first_low,
    back_logits_ref,
    norms,
    total,
    facts,
    attention_ref,
    memory,
    weights,
    class_rows,
    short,
    roi,
    sems,
):
    loads = Loads(
        [(weights_far.at[0, 0], weights.at[0, 0]), (weights_far.at[0, 1], weights.at[0, 1])]
        + [(memory_far, memory)]
        + [(weights_far.at[0, k], weights.at[0, k]) for k in (2, 3)]
        + [(weights_far.at[1], weights.at[1]), (class_far, class_rows)]
        + [(short_far, short), (roi_far, roi)],
        sems,
    )
    half = total.shape[0] // 2
    quarter = half // 2
    core, chip = pos[0], pos[1]
    side = chip % 2
    each = (own.shape[0] // 2 - quarter) * 2 // len(order)
    for sums, where in ((own, core), (other, 1 - core)):
        for n in range(2):
            base = n * (sums.shape[0] // 2)
            start = where * half + (side if n == 0 else 1 - side) * quarter
            total[pl.ds(start, quarter), :] = sums[base : base + quarter, :].astype(F32)
            for m in range(len(order) // 2):
                place = 4 * (chip ^ order[n * (len(order) // 2) + m]) + 2 * where
                rows = slice(base + quarter + m * each, base + quarter + (m + 1) * each)
                for part in range(2):
                    facts[pl.ds((place + part) * each, each), :] = sums[
                        rows, part * LANES : (part + 1) * LANES
                    ].astype(F32)
    width = memory.shape[1]
    scale = 1.0 / math.sqrt(width)
    clips, slots = bias.shape
    clip_rows = facts[:, classes + 1 : classes + 2].astype(jnp.int32)

    def select(values):
        chosen = values[:, :slots]
        for c in range(1, clips):
            chosen = jnp.where(clip_rows == c, values[:, c * slots : (c + 1) * slots], chosen)
        return chosen

    def spread(values):
        return jnp.concatenate(
            [jnp.where(clip_rows == c, values, 0.0).astype(BF16) for c in range(clips)], axis=1
        )

    dead = jnp.broadcast_to(bias[0:1, :], (clip_rows.shape[0], slots))
    for c in range(1, clips):
        dead = jnp.where(clip_rows == c, bias[c : c + 1, :], dead)
    stream = total[:, :width]
    kept = []
    for n in range(2):
        stream_low = stream.astype(BF16)
        loads.wait(1 if n == 0 else 6)
        query = mm(stream_low, weights[n, 0]).astype(BF16)
        loads.wait(2)
        query_key = mm_nt(query, weights[n, 1]).astype(BF16)
        loads.wait(3)
        masked = select(mm_nt(query_key, memory[...])) * scale + dead
        peak = jnp.max(masked, axis=1, keepdims=True)
        exponent = jnp.exp(masked - peak)
        whole = jnp.sum(exponent, axis=1, keepdims=True)
        attention = exponent * (1.0 / whole)
        attention_ref[n] = attention
        mixed = mm(spread(attention), memory[...]).astype(BF16)
        loads.wait(5)
        attended = mm(mixed, weights[n, 2])
        centred = attended - jnp.mean(attended, axis=1, keepdims=True)
        inverse = lax.rsqrt(jnp.mean(centred * centred, axis=1, keepdims=True) + EPSILON)
        hatted = centred * inverse
        normed = hatted * gain[n : n + 1, :] + shift[n : n + 1, :]
        hidden = (normed * jax.nn.sigmoid(normed)).astype(BF16)
        stream = stream + mm(hidden, weights[n, 3])
        lefts[4 * n] = stream_low
        lefts[4 * n + 2] = mixed
        lefts[4 * n + 3] = hidden
        rights[4 * n + 1] = query
        keys[n] = query_key
        kept.append((peak + jnp.log(whole), hatted, inverse, normed))
    stream_low = stream.astype(BF16)
    last_low[...] = stream_low
    loads.wait(7)
    split = class_rows.shape[1] - width
    logits = total[:, width : width + classes] + mm_nt(stream_low, class_rows[:, split:])
    chance = jax.nn.sigmoid(logits)
    scores[...] = chance
    valid = facts[:, classes : classes + 1]
    back_logits = (chance - facts[:, :classes]) * valid / clip_total
    back_logits = back_logits.astype(BF16)
    back_logits_ref[...] = back_logits
    back_stream = mm(back_logits, class_rows[:, split:])
    inners = [None, None]
    for n in (1, 0):
        log_sum, hatted, inverse, normed = kept[n]
        back_branch = back_stream.astype(BF16)
        back_normed = mm_nt(back_branch, weights[n, 3]) * silu_slope(normed)
        norms[n : n + 1, :] = jnp.sum(back_normed * hatted, axis=0, keepdims=True)
        norms[n + 2 : n + 3, :] = jnp.sum(back_normed, axis=0, keepdims=True)
        back_hat = back_normed * gain[n : n + 1, :]
        back_attended = inverse * (
            back_hat
            - jnp.mean(back_hat, axis=1, keepdims=True)
            - hatted * jnp.mean(back_hat * hatted, axis=1, keepdims=True)
        )
        back_att_low = back_attended.astype(BF16)
        back_mixed = mm_nt(back_att_low, weights[n, 2]).astype(BF16)
        attention = attention_ref[n]
        back_attention = select(mm_nt(back_mixed, memory[...]))
        inner = jnp.sum(attention * back_attention, axis=1, keepdims=True)
        back_raw = attention * (back_attention - inner) * scale
        back_key_mix = mm(spread(back_raw), memory[...]).astype(BF16)
        back_query = mm(back_key_mix, weights[n, 1]).astype(BF16)
        back_stream = back_stream + mm_nt(back_query, weights[n, 0])
        lefts[4 * n + 1] = back_key_mix
        rights[4 * n] = back_query
        rights[4 * n + 2] = back_att_low
        rights[4 * n + 3] = back_branch
        mixes[n] = back_mixed
        inners[n] = inner
    lane = lax.broadcasted_iota(jnp.int32, stats.shape, 1)
    stats[...] = jnp.where(
        lane == 0,
        kept[0][0],
        jnp.where(
            lane == 1,
            kept[1][0],
            jnp.where(
                lane == 2,
                inners[0],
                jnp.where(lane == 3, inners[1], facts[:, classes + 1 : classes + 2]),
            ),
        ),
    )
    back_low = back_stream.astype(BF16)
    first_low[...] = back_low
    loads.wait(9)
    back_boxes = mm(back_logits, class_rows[:, :split]) + mm_nt(back_low, short[...])
    back_pooled[...] = mm(roi[...], back_boxes.astype(BF16))


def bank_kernel(
    pos, keys, mixes, stats, memory, tag, feats, low, back_logits, last_low, wide, rows
):
    width = memory.shape[1]
    scale = 1.0 / math.sqrt(width)
    allowed = stats[:, 4:5].astype(jnp.int32) == tag[...]
    back_memory = None
    for n in range(2):
        raw = mm_nt(keys[n], memory[...])
        attention = jnp.where(allowed, jnp.exp(raw * scale - stats[:, n : n + 1]), 0.0)
        back_attention = mm_nt(mixes[n], memory[...])
        back_raw = (attention * (back_attention - stats[:, n + 2 : n + 3]) * scale).astype(BF16)
        term = mm_tn(back_raw, keys[n]) + mm_tn(attention.astype(BF16), mixes[n])
        back_memory = term if back_memory is None else back_memory + term
    count, boxes, lanes = low.shape
    low_memory = back_memory.astype(BF16)
    fine = rows.shape[0] // count // (width // LANES)
    for r in range(count):
        values = mm_tn(feats[:, r * lanes : (r + 1) * lanes], low_memory)
        wide[r, fine:, :] = values.astype(BF16)
    classes = back_logits.shape[1]
    rows[...] = jnp.zeros_like(rows)
    for r in range(count):
        rows[r * lanes : (r + 1) * lanes, :classes] = mm_tn(low[r], back_logits[...])
    box = lax.broadcasted_iota(jnp.int32, (boxes, 1), 0)
    mine = (box // (boxes // count)) == 2 * pos[1] + pos[0]
    own_logits = jnp.where(mine, back_logits[...].astype(F32), 0.0).astype(BF16)
    rows[count * lanes :, :classes] = mm_tn(last_low[...], own_logits)
    blocks = width // LANES
    for r in range(count):
        for q in range(blocks):
            start = (r * blocks + q) * fine
            wide[r, :fine, q * LANES : (q + 1) * LANES] = rows[start : start + fine, :].astype(BF16)


def block_kernel(lefts, rights, pick, norms, block):
    own = pick.shape[1]
    for item in range(8):
        columns = mm(lefts[item], pick[...]).astype(BF16)
        block[item * own : (item + 1) * own, :] = mm_tn(columns, rights[item]).astype(BF16)
    block[8 * own :, :] = jnp.zeros((block.shape[0] - 8 * own, block.shape[1]), BF16)
    for n in range(2):
        start = 8 * own + n * 2 * SUBLANES
        block[start : start + 2, :] = norms[2 * n : 2 * n + 2, :].astype(BF16)


def weight_kernel(
    cols, count, pos, far_expand, far_plane, far_rows, far_back, keep_far, send_far, *scratch
):
    back_expand, plane_out, sources, back_plane, keep, send, sems, out_sems = scratch
    lanes = back_expand.shape[1] // count
    pairs = [(far_plane, plane_out)]
    for chip in range(count // 2):
        columns = pl.ds(2 * chip * lanes, 2 * lanes)
        pairs.append((far_expand.at[:, columns], back_expand.at[:, columns]))
    pairs.append((far_back, back_plane))
    pairs += [(source, sources.at[i]) for i, source in enumerate(far_rows)]
    loads = Loads(pairs, sems)
    stores = Stores(out_sems)
    width = plane_out.shape[1]
    rows = width // count

    def put(start, first, second):
        place = slice(start, start + first.shape[0])

        @pl.when(pos[0] == 0)
        def _():
            keep[place, :] = first.astype(BF16)
            send[place, :] = second.astype(BF16)

        @pl.when(pos[0] != 0)
        def _():
            keep[place, :] = second.astype(BF16)
            send[place, :] = first.astype(BF16)

    def out(start, size):
        place = pl.ds(start, size)
        stores.start(send.at[place, :], send_far.at[place, :])
        stores.start(keep.at[place, :], keep_far.at[place, :])

    each = lanes + 9 * rows
    for chip in range(count // 2):
        loads.wait(2 + chip)
        block = mm_tn(back_expand[:, 2 * chip * lanes : 2 * (chip + 1) * lanes], plane_out[...])
        put(chip * each, block[:lanes], block[lanes:])
        out(chip * each, lanes)
    loads.wait(2 + count // 2)
    whole = back_plane[...].astype(F32)
    moved = jnp.concatenate(
        [
            col_shift(whole, cols, -1).astype(BF16),
            back_plane[...],
            col_shift(whole, cols, 1).astype(BF16),
        ],
        axis=1,
    )
    for i in range(3):
        loads.wait(3 + count // 2 + i)
        block = mm_tn(sources[i], moved)
        for chip in range(count // 2):
            start = chip * each + lanes + 3 * i * rows
            top = 2 * chip * rows
            for j in range(3):
                columns = slice(j * width, (j + 1) * width)
                put(
                    start + j * rows,
                    block[top : top + rows, columns],
                    block[top + rows : top + 2 * rows, columns],
                )
            out(start, 3 * rows)
    stores.finish()


def temporal_grad_kernel(clips, cols, count, lanes, pos, *refs):
    keep, send, moved, wide, sems = refs[-5:]
    sources, pieces = refs[: -5 - count], refs[-5 - count : -5]
    chunk = wide.shape[2]
    steps = sources[0].shape[1] // chunk

    def load(step):
        pairs, start = [], 0
        for source in sources:
            end = start + source.shape[0]
            target = wide.at[step % 2, pl.ds(start, source.shape[0]), :]
            pairs.append((source.at[:, pl.ds(step * chunk, chunk)], target))
            start = end
        return Loads(pairs, sems.at[step % 2])

    loads = load(0)
    cells = moved.shape[0] // count
    part = pieces[0].shape[1]
    facts = None
    for s, piece in enumerate(pieces):
        values = piece[:cells, :]
        shifts = (frame_shift(values, clips, -cols), values, frame_shift(values, clips, cols))
        for k in range(3):
            moved[s * cells : (s + 1) * cells, k * part : (k + 1) * part] = shifts[k]
        term = piece[cells:, :].astype(F32)
        facts = term if facts is None else facts + term
    low = facts.astype(BF16)
    each = 3 * lanes + low.shape[0]
    for end in range(each, keep.shape[0] + 1, each):
        keep[end - low.shape[0] : end, :] = low
        send[end - low.shape[0] : end, :] = low
    blocks = chunk // (2 * lanes)
    for step in range(steps):
        loads.wait(len(sources))
        if step + 1 < steps:
            loads = load(step + 1)
        total = mm_tn(wide[step % 2], moved[...])
        for block in range(blocks):
            for k in range(3):
                top = 2 * block * lanes
                columns = slice(k * part, (k + 1) * part)
                first = total[top : top + lanes, columns].astype(BF16)
                second = total[top + lanes : top + 2 * lanes, columns].astype(BF16)
                start = (step * blocks + block) * each + k * lanes
                place = slice(start, start + lanes)

                @pl.when(pos[0] == 0)
                def _():
                    keep[place, :] = first
                    send[place, :] = second

                @pl.when(pos[0] != 0)
                def _():
                    keep[place, :] = second
                    send[place, :] = first


def back_plane_kernel(
    clips,
    frames,
    cols,
    back_pooled,
    slope,
    sums,
    expand,
    og,
    plane_sum,
    gain,
    shift,
    back_expand,
    back_plane,
    facts,
    acc,
    rows,
):
    step = pl.program_id(0)
    steps = pl.num_programs(0)
    cells, lanes = slope.shape

    @pl.when(step == 0)
    def _():
        rows[...] = jnp.zeros_like(rows)

    pooled = back_pooled[...].reshape(clips, 1, cols, lanes)
    final = (pooled * slope[...].astype(F32).reshape(clips, frames, cols, lanes)).reshape(cells, lanes)
    rows[pl.ds(step, 1), :] = jnp.sum(final * sums[...].astype(F32), axis=0, keepdims=True)
    rows[pl.ds(steps + step, 1), :] = jnp.sum(final, axis=0, keepdims=True)
    low = (final * og[...]).astype(BF16)
    back_expand[...] = low
    term = mm_nt(low, expand[...])

    @pl.when(step == 0)
    def _():
        acc[...] = term

    @pl.when(step > 0)
    def _():
        acc[...] += term

    @pl.when(step == steps - 1)
    def _():
        back_arg = acc[...] * silu_slope(plane_sum[...] * gain[1:2, :] + shift[1:2, :])
        rows[pl.ds(2 * steps, 1), :] = jnp.sum(back_arg * plane_sum[...], axis=0, keepdims=True)
        rows[pl.ds(2 * steps + 1, 1), :] = jnp.sum(back_arg, axis=0, keepdims=True)
        back_plane[...] = (back_arg * gain[1:2, :]).astype(BF16)
        facts[...] = rows[...].astype(BF16)


def back_temporal_kernel(
    cols, pos, gain, shift, late, rows, w, temporal_sum, out, facts, *pieces
):
    sides = []
    for j in range(3):
        term = mm_nt(rows[0][...], w[0, j]) + mm_nt(rows[1][...], w[1, j])
        sides.append(term + mm_nt(rows[2][...], w[2, j]))
    back_out = sides[1] + col_shift(sides[0], cols, -1) + col_shift(sides[2], cols, 1)
    back_arg = back_out * silu_slope(temporal_sum[...] * gain[0:1, :] + shift[0:1, :])
    cells, width = out.shape
    facts[...] = late[...].astype(F32)
    facts[facts.shape[0] - 2 : facts.shape[0] - 1, :] = jnp.sum(
        back_arg * temporal_sum[...], axis=0, keepdims=True
    )
    facts[facts.shape[0] - 1 :, :] = jnp.sum(back_arg, axis=0, keepdims=True)
    out[...] = (back_arg * gain[0:1, :]).astype(BF16)
    for s, piece in enumerate(pieces):
        start = pl.multiple_of(pos[2 + s] * LANES, LANES)
        piece[:cells, :] = out[:, pl.ds(start, LANES)]
        rows = facts.shape[0]
        for q in range(width // LANES):
            piece[cells + q * rows : cells + (q + 1) * rows, :] = facts[
                :, q * LANES : (q + 1) * LANES
            ].astype(BF16)


def input_kernel(clips, frames, cols, back, w, back_pooled, slope, out):
    values = back[...]
    cells, lanes = slope.shape
    pooled = back_pooled[...].reshape(clips, 1, cols, lanes)
    total = (pooled * slope[...].astype(F32).reshape(clips, frames, cols, lanes)).reshape(cells, lanes)
    total = total + mm_nt(values, w[1]) + mm_nt(frame_shift(values, clips, -cols), w[0])
    out[...] = total + mm_nt(frame_shift(values, clips, cols), w[2])


def lanes_kernel(counts, forms, pos, *refs):
    outs, whole = refs[-1 - len(counts) : -1], refs[-1]
    rows = whole.shape[0]
    index = 0
    for ref in refs[: -1 - len(counts)]:
        for n in range(ref.shape[0] // rows):
            start = pl.multiple_of(pos[index] * LANES, LANES)
            whole[:, pl.ds(start, LANES)] = ref[n * rows : (n + 1) * rows, :]
            index += 1
    start = 0
    for count, form, out in zip(counts, forms, outs):
        piece = whole[start : start + count, :].astype(F32)
        start += count
        if form == 0:
            out[...] = piece
        elif form == 1:
            out[...] = piece.T
        elif form == 2:
            for q in range(whole.shape[1] // LANES):
                first = q * LANES
                out[:, q * count : (q + 1) * count] = piece[:, first : first + out.shape[0]].T
        else:
            own = out.shape[1]
            shift = whole.shape[1] - pos[pos.shape[0] - 1] * own
            moved = pltpu.roll(piece[: 2 * SUBLANES, :], shift, 1)
            out[...] = moved[: out.shape[0], :own]


def blocks_kernel(codes, pos, *refs):
    sources, outs = refs[: -len(codes)], refs[-len(codes) :]
    for group, out in zip(codes, outs):
        row = 0
        for code in group:
            start = pl.multiple_of(pos[code] * LANES, LANES)
            for source in sources:
                count = source.shape[0]
                out[row : row + count, :] = source[:, pl.ds(start, LANES)]
                row += count


class Halving:
    def __init__(self, held, steps, send, step=0, first=None):
        self.held, self.steps, self.send = held, steps, send
        self.step, self.got, self.first = step, None, first

    def advance(self, hold):
        if self.got is not None:
            self.held = take(self.held, self.step - 1, self.got)
            self.got = None
        if self.step < self.steps:
            buffer = give(self.held, self.step) if self.first is None else self.first
            self.first = None
            buffer, hold = lax.optimization_barrier((buffer, hold))
            self.got = self.send(self.step, buffer)
            self.step += 1
        return hold

    def finish(self):
        while self.got is not None:
            self.advance(())
        return self.held[0]


class Doubling:
    def __init__(self, own, steps, send):
        self.parts, self.steps, self.send = [own], steps, send
        self.step, self.got = 0, None

    def advance(self, hold):
        if self.got is not None:
            self.parts.append(self.got)
            self.got = None
        if self.step < self.steps:
            buffer = self.parts[0] if self.step == 0 else jnp.concatenate(self.parts, axis=0)
            buffer, hold = lax.optimization_barrier((buffer, hold))
            self.got = self.send(self.step, buffer)
            self.step += 1
        return hold

    def finish(self):
        while self.got is not None:
            self.advance(())
        return self.parts


def window(values, chains):
    chains = [chain for chain in chains if chain.got is not None]
    tied = lax.optimization_barrier((tuple(values), tuple(chain.got for chain in chains)))
    for chain, got in zip(chains, tied[1]):
        chain.got = got
    return tied[0]


def join_lanes(parts, places):
    rows = parts[0].shape[0]
    blocks = [part[n * rows : (n + 1) * rows] for part in parts for n in range(part.shape[0] // rows)]
    joined = []
    for target in range(len(blocks)):
        chosen = blocks[0]
        for code in range(1, len(blocks)):
            chosen = jnp.where(places[code] == target, blocks[code], chosen)
        joined.append(chosen)
    return jnp.concatenate(joined, axis=-1).astype(F32)


def body(
    clip_input,
    temporal,
    spatial,
    expand,
    mid_gain,
    mid_shift,
    out_gain,
    out_shift,
    short_weight,
    bank_weight,
    block_weight,
    norm_gain,
    norm_shift,
    class_weight,
    bank_feats,
    bank_mask,
    box_coords,
    box_clip,
    box_valid,
    labels,
):
    row = lax.axis_index("row")
    group = lax.axis_index("clip")
    row_size = lax.axis_size("row")
    clip_size = lax.axis_size("clip")
    core = row % 2
    chip = row // 2
    chips = row_size // 2
    clips, frames, rows_local, cols, channels = clip_input.shape
    mid = temporal.shape[2]
    width = short_weight.shape[1]
    classes = class_weight.shape[1]
    cells = clips * frames * cols
    boxes = box_coords.shape[0]
    box_local = labels.shape[0]
    slots_local = bank_feats.shape[1]
    part = mid // clip_size
    steps = channels // mid
    lanes = channels // row_size
    crossed = clip_size == 4
    masks = [(s, s) for s in range(clip_size)]
    if crossed:
        masks = [(0, 0), (1, 2), (2, 1), (3, 3)]
    targets = [group ^ jnp.where(core == 0, first, second) for first, second in masks]
    place = jnp.stack([core, chip, *targets]).astype(jnp.int32)
    og, os = out_gain[None], out_shift[None]

    tie = lax.optimization_barrier
    source = clip_input.reshape(cells, channels)

    wide_input = [source]
    if not crossed:
        wide_input += [swap(source, "clip", s) for s in range(1, clip_size)]

    def passed(values, after, even_mask, odd_mask):
        values, _ = tie((values, after))
        return joint_swap(values, even_mask, odd_mask)

    def kernel_row(i):
        return pl.BlockSpec((1, 3, mid, mid), lambda _: (i, 0, 0, 0))

    def fixed(*shape):
        return pl.BlockSpec(shape, lambda i: (0,) * len(shape))

    def across(height, lane_count):
        return pl.BlockSpec((height, lane_count), lambda i: (0, i))

    eighth = cells // 8
    cuts = [(0, 2), (2, 4), (6, 2), (0, 1), (1, 6), (7, 1)] if crossed else []
    temporal_sum, temporal_out, *cut_rows = run(
        lambda *refs: temporal_kernel(clips, cols, [start * eighth for start, _ in cuts], *refs),
        [shape_of((cells, mid), F32), shape_of((cells, mid), BF16)]
        + [shape_of((count * eighth, channels), BF16) for _, count in cuts],
        [source, temporal, mid_gain, mid_shift],
        grid=(steps,),
        in_specs=[
            across(cells, mid),
            pl.BlockSpec((3, mid, mid), lambda i: (0, i, 0)),
            fixed(2, mid),
            fixed(2, mid),
        ],
        out_specs=[fixed(cells, mid), fixed(cells, mid)]
        + [across(count * eighth, mid) for _, count in cuts],
    )

    def halo(values):
        ends = row_size - 1
        above = lax.ppermute(values, "row", [(i, i + 1) for i in range(ends)])
        below = lax.ppermute(values, "row", [(i + 1, i) for i in range(ends)])
        return above, below

    above_row, below_row = halo(temporal_out)

    if crossed:
        first_a = joint_swap(cut_rows[0], 1, 2)
    feats, box_coords, temporal_out = tie(
        (bank_feats.reshape(clips * slots_local, channels), box_coords, temporal_out)
    )
    memory_own = mm(feats, bank_weight).astype(BF16)
    clip_group = box_clip - group * clips
    weights = box_weights(
        box_coords, clip_group, row * rows_local, rows_local, rows_local * row_size, clips, cols
    ).reshape(boxes, clips * cols).T
    class_rows = class_weight.T

    (plane_part,) = run(
        lambda *refs: plane_own_kernel(cols, *refs),
        [shape_of((cells, mid), F32)],
        [temporal_out, spatial],
        grid=(1,),
        in_specs=[fixed(cells, mid), kernel_row(1)],
        out_specs=[fixed(cells, mid)],
    )
    above_row, below_row, memory_own, plane_part = tie(
        (above_row, below_row, memory_own, plane_part)
    )
    memory = lax.all_gather(
        memory_own.reshape(clips, slots_local, width), "row", axis=1, tiled=True
    ).reshape(-1, width)
    tied = (above_row, below_row, plane_part, weights, class_rows)
    if crossed:
        *tied, first_a = tie((*tied, first_a))
    else:
        tied = tie(tied)
    above_row, below_row, plane_part, weights, class_rows = tied
    if crossed:
        first_b = passed(cut_rows[1], above_row, 1, 2)
    half = boxes // 2
    joint = width + LANES
    plane_sum, plane_out, partial_low, mine, other = run(
        lambda *refs: plane_kernel(clips, frames, cols, *refs),
        [
            shape_of((cells, mid), F32),
            shape_of((cells, mid), BF16),
            shape_of((row_size, boxes, lanes), BF16),
            shape_of((half, joint), F32),
            shape_of((half, joint), BF16),
        ],
        [
            place,
            above_row,
            below_row,
            spatial,
            spatial,
            plane_part,
            mid_gain,
            mid_shift,
            expand,
            source,
            og,
            os,
            weights,
            short_weight,
            class_rows,
        ],
        grid=(steps,),
        in_specs=[
            SMEM,
            fixed(cells, mid),
            fixed(cells, mid),
            kernel_row(0),
            kernel_row(2),
            fixed(cells, mid),
            fixed(2, mid),
            fixed(2, mid),
            across(mid, mid),
            across(cells, mid),
            across(1, mid),
            across(1, mid),
            fixed(clips * cols, boxes),
            pl.BlockSpec((mid, width), lambda i: (i, 0)),
            across(classes, mid),
        ],
        out_specs=[
            fixed(cells, mid),
            fixed(cells, mid),
            pl.BlockSpec((mid // lanes, boxes, lanes), lambda i: (i, 0, 0)),
            fixed(half, joint),
            fixed(half, joint),
        ],
        scratch=[pltpu.VMEM((boxes, joint), F32)],
    )

    if crossed:
        mine, other, plane_out, first_b = tie((mine, other, plane_out, first_b))
        first_c = passed(cut_rows[2], mine, 1, 2)
        second_a = passed(cut_rows[3], mine, 2, 1)
    clip_own = lax.dynamic_slice_in_dim(clip_group, row * box_local, box_local, 0)
    facts = jnp.concatenate(
        [labels.astype(BF16), box_valid.astype(BF16)[:, None], clip_own.astype(BF16)[:, None]], axis=1
    )
    facts = jnp.pad(facts, ((0, 0), (0, LANES - facts.shape[1])))
    facts = jnp.concatenate([facts[: box_local // 2], facts[box_local // 2 :]], axis=1)
    facts = jnp.pad(facts, ((0, 0), (0, joint - 2 * LANES)))
    half_sum = mine + swap(other, "row", 1).astype(F32)
    quarter = half // 2
    side = chip % 2
    got = swap(
        lax.dynamic_slice_in_dim(half_sum, (1 - side) * quarter, quarter, 0).astype(BF16), "row", 2
    )
    plane_late, _ = tie((plane_out, half_sum))
    expand_sums, slope = run(
        lambda *refs: slope_kernel(frames, *refs),
        [shape_of((cells, channels), BF16), shape_of((cells, channels), BF16)],
        [plane_late, expand, source, og, os],
        grid=(steps,),
        in_specs=[
            fixed(cells, mid),
            across(mid, mid),
            across(cells, mid),
            across(1, mid),
            across(1, mid),
        ],
        out_specs=[across(cells, mid)] * 2,
    )
    if crossed:
        got, slope, first_c, second_a = tie((got, slope, first_c, second_a))
    else:
        got, slope = tie((got, slope))
    part_sum = lax.dynamic_slice_in_dim(half_sum, side * quarter, quarter, 0) + got.astype(F32)
    label_rows, codes = [facts], [0]
    for t in range(1, bits(chips)):
        payload = jnp.concatenate([part_sum.astype(BF16)] + label_rows, axis=0)
        got = swap(payload, "row", 2 << t)
        part_sum = part_sum + got[:quarter].astype(F32)
        each = facts.shape[0]
        label_rows = label_rows + [
            got[quarter + n * each : quarter + (n + 1) * each] for n in range(len(codes))
        ]
        codes = codes + [code ^ (1 << t) for code in codes]
    payload = jnp.concatenate([part_sum.astype(BF16)] + label_rows, axis=0)
    got = swap(payload, "row", 2)
    live = bank_mask == 1
    tags = jnp.where(live, jnp.arange(clips, dtype=jnp.int32)[:, None], -1)
    tags_own = lax.dynamic_slice_in_dim(tags, row * slots_local, slots_local, 1).reshape(1, -1)
    bias = jnp.where(live, 0.0, -jnp.inf).astype(F32)
    got, memory, bias = tie((got, memory, bias))
    totals_own = jnp.concatenate([payload, got], axis=0)
    label_order = codes + [code ^ 1 for code in codes]
    totals_other = swap(totals_own, "row", 1)
    if crossed:
        second_b = passed(cut_rows[4], totals_own, 2, 1)

    partial_low, totals_other = tie((partial_low, totals_other))
    short_columns = lax.psum_scatter(partial_low, "row", scatter_dimension=0, tiled=False)

    slots = bias.shape[1]
    stream_shape = (boxes, width)
    (
        scores_all,
        back_pooled,
        lefts,
        rights,
        keys,
        mixes,
        stats,
        last_low,
        first_low,
        back_logits,
        norms,
    ) = run(
        lambda *refs: box_kernel(label_order, classes, float(clips * clip_size), *refs),
        [
            shape_of((boxes, classes), F32),
            shape_of((clips * cols, channels), F32),
            shape_of((8, *stream_shape), BF16),
            shape_of((8, *stream_shape), BF16),
            shape_of((2, *stream_shape), BF16),
            shape_of((2, *stream_shape), BF16),
            shape_of((boxes, LANES), F32),
            shape_of(stream_shape, BF16),
            shape_of(stream_shape, BF16),
            shape_of((boxes, classes), BF16),
            shape_of((4, width), F32),
        ],
        [
            place,
            totals_own,
            totals_other,
            bias,
            norm_gain,
            norm_shift,
            memory,
            block_weight,
            class_rows,
            short_weight,
            weights,
        ],
        in_specs=[SMEM] + [VMEM] * 5 + [ANY] * 5,
        scratch=[
            pltpu.VMEM((boxes, joint), F32),
            pltpu.VMEM((boxes, LANES), F32),
            pltpu.VMEM((2, boxes, slots), F32),
            pltpu.VMEM(memory.shape, BF16),
            pltpu.VMEM(block_weight.shape, BF16),
            pltpu.VMEM(class_rows.shape, BF16),
            pltpu.VMEM(short_weight.shape, BF16),
            pltpu.VMEM(weights.shape, BF16),
            pltpu.SemaphoreType.DMA((9,)),
        ],
    )
    scores = lax.dynamic_slice_in_dim(scores_all, row * box_local, box_local, 0)

    if crossed:
        back_pooled, second_b = tie((back_pooled, second_b))
        third_a = passed(first_a, back_pooled, 2, 1)

    fact_rows = -(-(2 * steps + 2) // 16) * 16
    back_expand, back_plane, second_facts = run(
        lambda *refs: back_plane_kernel(clips, frames, cols, *refs),
        [
            shape_of((cells, channels), BF16),
            shape_of((cells, mid), BF16),
            shape_of((fact_rows, mid), BF16),
        ],
        [
            back_pooled,
            slope,
            expand_sums,
            expand,
            og,
            plane_sum,
            mid_gain,
            mid_shift,
        ],
        grid=(steps,),
        in_specs=[
            across(clips * cols, mid),
            across(cells, mid),
            across(cells, mid),
            across(mid, mid),
            across(1, mid),
            fixed(cells, mid),
            fixed(2, mid),
            fixed(2, mid),
        ],
        out_specs=[
            across(cells, mid),
            fixed(cells, mid),
            fixed(fact_rows, mid),
        ],
        scratch=[pltpu.VMEM((cells, mid), F32), pltpu.VMEM((fact_rows, mid), F32)],
    )

    if crossed:
        back_plane, back_expand, second_facts, third_a = tie(
            (back_plane, back_expand, second_facts, third_a)
        )
        second_c = passed(cut_rows[5], back_plane, 2, 1)
        third_b = passed(first_b, back_plane, 2, 1)
    back_above, back_below = halo(back_plane)

    fact_count = second_facts.shape[0]
    own_mid = mid // row_size
    own_rows = channels // row_size

    weight_rows = own_rows + 9 * own_mid
    weight_shape = (chips * weight_rows, mid)
    kept_weight, sent_weight = run(
        lambda pos, expand_ref, plane_ref, above_ref, own_ref, below_ref, back_ref, *refs: weight_kernel(
            cols, row_size, pos, expand_ref, plane_ref, (above_ref, own_ref, below_ref), back_ref, *refs
        ),
        [shape_of(weight_shape, BF16)] * 2,
        [
            place,
            back_expand,
            plane_out,
            above_row,
            temporal_out,
            below_row,
            back_plane,
        ],
        in_specs=[SMEM] + [ANY] * 6,
        out_specs=[ANY] * 2,
        scratch=[
            pltpu.VMEM((cells, channels), BF16),
            pltpu.VMEM((cells, mid), BF16),
            pltpu.VMEM((3, cells, mid), BF16),
            pltpu.VMEM((cells, mid), BF16),
            pltpu.VMEM(weight_shape, BF16),
            pltpu.VMEM(weight_shape, BF16),
            pltpu.SemaphoreType.DMA((5 + chips,)),
            pltpu.SemaphoreType.DMA((8 * chips,)),
        ],
    )
    tied = (back_above, back_below, kept_weight, sent_weight, short_columns)
    if crossed:
        *tied, second_c, third_b = tie((*tied, second_c, third_b))
        third_c = passed(first_c, sent_weight, 2, 1)
        wide_input += [first_a, first_b, first_c, second_a, second_b, second_c]
        wide_input += [third_a, third_b, third_c]
    else:
        tied = tie(tied)
    back_above, back_below, kept_weight, sent_weight, short_columns = tied
    got_weight = swap(sent_weight, "row", 1)

    even, odd = step_masks(clip_size)
    places = [place_of(code, group, core) for code in range(clip_size)]
    block_places = jnp.stack([jnp.asarray(item, jnp.int32) for item in places])

    def clip_step(t, values):
        return joint_swap(values, even[t], odd[t])

    def chip_step(t, values):
        return swap(values, "row", 2 << t)

    def lane_block(values, target):
        return lax.dynamic_slice_in_dim(values, target * part, part, 1)

    def chip_rows(target, *values):
        each = values[0].shape[0] // chips
        rows = [lax.dynamic_slice_in_dim(item, target * each, each, 0) for item in values]
        if len(rows) == 1:
            return rows[0]
        return tree_sum([item.astype(F32) for item in rows]).astype(BF16)

    def over_chips(*values):
        return Halving(
            {code: chip_rows(chip ^ code, *values) for code in range(chips)}, bits(chips), chip_step
        )

    def over_clips(piece):
        return Halving(
            {code: piece(places[code]) for code in range(clip_size)}, bits(clip_size), clip_step
        )

    class_fine = (channels + width) // row_size * LANES // width
    keys, _ = tie((keys, sent_weight))
    (wide_part,) = run(
        bank_kernel,
        [shape_of((row_size, class_fine + own_rows, width), BF16)],
        [
            place,
            keys,
            mixes,
            stats,
            memory_own,
            tags_own,
            feats,
            partial_low,
            back_logits,
            last_low,
        ],
        in_specs=[SMEM] + [VMEM] * 9,
        scratch=[pltpu.VMEM((channels + width, LANES), F32)],
    )
    if crossed:
        got_weight, wide_part, third_c = tie((got_weight, wide_part, third_c))
        wide_input[-3:] = [third_a, third_b, third_c]
    else:
        got_weight, wide_part = tie((got_weight, wide_part))
    wide_own = lax.psum_scatter(wide_part, "row", scatter_dimension=0, tiled=False)

    def weight_blocks(codes):
        return {
            code: (
                lane_block(kept_weight, places[code]).astype(F32)
                + lane_block(got_weight, places[code]).astype(F32)
            ).astype(BF16)
            for code in codes
        }

    high = [code for code in range(clip_size) if code & 1]
    late, early = high[: len(high) // 2], high[len(high) // 2 :]
    held = weight_blocks(early)
    buffers, back_above = tie((tuple(held[code] for code in early), back_above))
    first_step = {code: clip_step(0, values) for code, values in zip(early, buffers)}

    direct = part == LANES
    piece_rows = fact_rows * (mid // part)
    back_temporal, facts_own, *pieces = run(
        lambda pos, gain, shift, late, below, own, above, *refs: back_temporal_kernel(
            cols, pos, gain, shift, late, (below, own, above), *refs
        ),
        [shape_of((cells, mid), BF16), shape_of((fact_rows, mid), F32)]
        + [shape_of((cells + piece_rows, part), BF16)] * (clip_size if direct else 0),
        [
            place,
            mid_gain,
            mid_shift,
            second_facts,
            back_below,
            back_plane,
            back_above,
            spatial,
            temporal_sum,
        ],
        in_specs=[SMEM] + [VMEM] * 8,
    )
    if not direct:
        facts_flat = jnp.concatenate(
            [facts_own[:, q * part : (q + 1) * part] for q in range(mid // part)], axis=0
        ).astype(BF16)
        pieces = [
            jnp.concatenate(
                [lax.dynamic_slice_in_dim(back_temporal, target * part, part, 1), facts_flat], axis=0
            )
            for target in targets
        ]
    back_temporal, first_step, pieces = tie((back_temporal, first_step, tuple(pieces)))

    got = pieces[:1] + tuple(
        joint_swap(piece, *step_mask) for piece, step_mask in zip(pieces[1:], masks[1:])
    )
    kept_weight, got_weight, _ = tie((kept_weight, got_weight, back_temporal))
    held.update(weight_blocks([code for code in range(clip_size) if code not in early]))
    pick = (
        jnp.arange(width, dtype=jnp.int32)[:, None]
        == row * own_mid + jnp.arange(own_mid, dtype=jnp.int32)[None, :]
    ).astype(BF16)
    lefts, _ = tie((lefts, back_temporal))
    (block_part,) = run(
        block_kernel,
        [shape_of((8 * own_mid + 32, width), BF16)],
        [lefts, rights, pick, norms],
    )
    short_part = mm_tn(short_columns, first_low).astype(BF16)
    got, block_part, short_part, held = tie((got, block_part, short_part, held))

    buffers, got = tie((tuple(held[code] for code in late), got))
    first_step.update({code: clip_step(0, values) for code, values in zip(late, buffers)})
    temporal_rows = chips * (3 * own_rows + piece_rows)
    kept_temporal, sent_temporal = run(
        lambda *refs: temporal_grad_kernel(clips, cols, clip_size, lanes, *refs),
        [shape_of((temporal_rows, part), BF16)] * 2,
        [place, *wide_input, *got],
        in_specs=[SMEM] + [ANY] * len(wide_input) + [VMEM] * clip_size,
        scratch=[
            pltpu.VMEM((clip_size * cells, 3 * part), BF16),
            pltpu.VMEM((2, clip_size * cells, mid), BF16),
            pltpu.SemaphoreType.DMA((2, len(wide_input))),
        ],
    )
    tied = tie((kept_temporal, sent_temporal, first_step))
    kept_temporal, sent_temporal, first_step = tied
    got_temporal = swap(sent_temporal, "row", 1)
    sums_weight = Halving(
        {
            code ^ 1: held[code ^ 1].astype(F32) + values.astype(F32)
            for code, values in first_step.items()
        },
        bits(clip_size),
        clip_step,
        step=1,
    )
    got_temporal = sums_weight.advance(got_temporal)
    sums_temporal = over_chips(kept_temporal, got_temporal)
    back_temporal = sums_temporal.advance(back_temporal)

    (input_grad,) = run(
        lambda *refs: input_kernel(clips, frames, cols, *refs),
        [shape_of((cells, channels), F32)],
        [back_temporal, temporal, back_pooled, slope],
        grid=(steps,),
        in_specs=[
            fixed(cells, mid),
            pl.BlockSpec((3, mid, mid), lambda i: (0, i, 0)),
            across(clips * cols, mid),
            across(cells, mid),
        ],
        out_specs=[across(cells, mid)],
    )
    input_grad = input_grad.reshape(clip_input.shape)

    box_wide = [wide_own.reshape(-1, width), block_part, short_part]
    box_rows = sum(item.shape[0] for item in box_wide)
    if direct:
        groups = [[code for code in range(clip_size) if code & 1 == bit] for bit in (0, 1)]
        kept_box, sent_box = run(
            lambda *refs: blocks_kernel(groups, *refs),
            [shape_of((len(groups[0]) * box_rows, part), BF16)] * 2,
            [block_places, *box_wide],
            in_specs=[SMEM] + [VMEM] * len(box_wide),
        )
        input_grad, kept_box, sent_box = window(
            [input_grad, kept_box, sent_box], [sums_weight, sums_temporal]
        )
        sums_box = Halving(
            {
                code: kept_box[n * box_rows : (n + 1) * box_rows]
                for n, code in enumerate(groups[0])
            },
            bits(clip_size),
            clip_step,
            first=sent_box,
        )
    else:
        (input_grad,) = window([input_grad], [sums_weight, sums_temporal])
        sums_box = over_clips(
            lambda target: jnp.concatenate([lane_block(item, target) for item in box_wide], axis=0)
        )
    sums_weight.got = sums_temporal.advance(sums_weight.got)
    sums_chip = over_chips(tie(sums_weight.finish().astype(BF16)))
    sums_chip.advance(())
    sums_box.advance(())
    window([], [sums_temporal, sums_chip, sums_box])
    sums_chip.advance(())
    sums_box.advance(())
    temporal_got = sums_temporal.finish()
    own_temporal = 3 * own_rows
    facts_total = temporal_got[own_temporal:].reshape(mid // part, fact_rows, part)
    facts_total = jnp.concatenate([facts_total[q] for q in range(mid // part)], axis=1)
    all_first = Doubling(temporal_got[:own_temporal].astype(BF16), bits(clip_size), clip_step)
    all_first.advance(())
    window([], [sums_chip, sums_box, all_first])
    all_first.advance(())
    weight_own = sums_chip.finish().astype(BF16)
    box_own = sums_box.finish().astype(BF16)
    all_last = Doubling(
        jnp.concatenate([weight_own, box_own], axis=0), bits(clip_size), clip_step
    )
    all_last.advance(())
    window([], [all_first, all_last])
    all_last.advance(())
    firsts = all_first.finish()
    lasts = all_last.finish()
    class_count = class_fine * width // LANES
    last_counts = [own_rows, 9 * own_mid, class_fine, own_rows, 8 * own_mid, 16, 16, own_rows]
    last_shapes = [(mid, own_rows), (9 * own_mid, mid), (classes, class_count), (own_rows, width)]
    last_shapes += [(8 * own_mid, width), (2, own_mid), (2, own_mid), (own_rows, width)]

    def assemble(parts, counts, shapes, forms):
        if direct:
            return run(
                lambda *refs: lanes_kernel(counts, forms, *refs),
                [shape_of(shape, F32) for shape in shapes],
                [jnp.append(block_places, row.astype(jnp.int32)), *parts],
                in_specs=[SMEM] + [VMEM] * len(parts),
                scratch=[pltpu.VMEM((sum(counts), width), BF16)],
            )
        whole = join_lanes(parts, places)
        ends = [sum(counts[: k + 1]) for k in range(len(counts))]
        outs = []
        for count, end, shape, form in zip(counts, ends, shapes, forms):
            piece = whole[end - count : end]
            if form == 1:
                piece = piece.T
            if form == 2:
                piece = jnp.concatenate(
                    [piece[:, q * LANES : q * LANES + shape[0]].T for q in range(width // LANES)],
                    axis=1,
                )
            if form == 3:
                piece = lax.dynamic_slice_in_dim(piece[: shape[0]], row * shape[1], shape[1], 1)
            outs.append(piece)
        return outs

    (temporal_grad,) = assemble(firsts, [own_temporal], [(own_temporal, mid)], (0,))
    expand_grad, spatial_grad, class_grad, bank_grad, block_grad, *norm_grads, short_grad = assemble(
        lasts, last_counts, last_shapes, (1, 0, 2, 0, 0, 3, 3, 0)
    )
    class_grad = class_grad.T
    temporal_grad = temporal_grad.reshape(3, own_rows, mid)
    spatial_grad = spatial_grad.reshape(3, 3, own_mid, mid)
    block_grad = block_grad.reshape(2, 4, own_mid, width)
    out_gain_all = facts_total[:steps].reshape(-1)
    out_shift_all = facts_total[steps : 2 * steps].reshape(-1)
    out_gain_grad = lax.dynamic_slice_in_dim(out_gain_all, row * own_rows, own_rows, 0)
    out_shift_grad = lax.dynamic_slice_in_dim(out_shift_all, row * own_rows, own_rows, 0)
    gain_all = jnp.stack([facts_total[fact_rows - 2], facts_total[2 * steps]])
    shift_all = jnp.stack([facts_total[fact_rows - 1], facts_total[2 * steps + 1]])
    mid_gain_grad = lax.dynamic_slice_in_dim(gain_all, row * own_mid, own_mid, 1)
    mid_shift_grad = lax.dynamic_slice_in_dim(shift_all, row * own_mid, own_mid, 1)
    return (
        scores,
        input_grad,
        temporal_grad,
        spatial_grad,
        expand_grad,
        mid_gain_grad,
        mid_shift_grad,
        out_gain_grad,
        out_shift_grad,
        short_grad,
        bank_grad,
        block_grad,
        *norm_grads,
        class_grad,
    )


def solution(mesh):
    whole = P()
    in_specs = (
        (P("clip", None, "row", None, None),)
        + (whole,) * 13
        + (
            P("clip", "row", None),
            P("clip", None),
            P("clip", None),
            P("clip"),
            P(("clip", "row")),
            P(("clip", "row"), None),
        )
    )
    out_specs = (
        P(("clip", "row"), None),
        P("clip", None, "row", None, None),
        P(None, "row", None),
        P(None, None, "row", None),
        P(None, "row"),
        P(None, "row"),
        P(None, "row"),
        P("row"),
        P("row"),
        P("row", None),
        P("row", None),
        P(None, None, "row", None),
        P(None, "row"),
        P(None, "row"),
        P("row", None),
    )
    return jax.shard_map(body, mesh=mesh, in_specs=in_specs, out_specs=out_specs, check_vma=False)
```

```python
import math

import jax
import jax.numpy as jnp
from jax import lax
from jax.experimental import pallas as pl
from jax.experimental.pallas import tpu as pltpu
from jax.sharding import PartitionSpec as P

SAMPLES = 14
LANES = 128
SUBLANES = 8
EPSILON = 1e-05
F32 = jnp.float32
BF16 = jnp.bfloat16


def dot(left, right, dims):
    return lax.dot_general(left, right, (dims, ((), ())), preferred_element_type=F32)


def mm(left, right):
    return dot(left, right, ((1,), (0,)))


def mm_nt(left, right):
    return dot(left, right, ((1,), (1,)))


def mm_tn(left, right):
    return dot(left, right, ((0,), (0,)))


def swap(values, axis, mask):
    count = lax.axis_size(axis)
    return lax.ppermute(values, axis, [(i, i ^ mask) for i in range(count)])


def tree_sum(parts):
    while len(parts) > 1:
        parts = [parts[i] + parts[i + 1] for i in range(0, len(parts), 2)]
    return parts[0]


def step_masks(count):
    even = [1 << t for t in range(count.bit_length() - 1)]
    odd = list(even)
    for t in range(0, len(odd) - 1, 2):
        odd[t], odd[t + 1] = odd[t + 1], odd[t]
    return even, odd


def joint_swap(values, even_mask, odd_mask):
    clip_size = lax.axis_size("clip")
    row_size = lax.axis_size("row")
    pairs = []
    for c in range(clip_size):
        for r in range(row_size):
            mask = odd_mask if r % 2 else even_mask
            pairs.append((c * row_size + r, (c ^ mask) * row_size + r))
    return lax.ppermute(values, ("clip", "row"), pairs)


def place_of(code, group, core):
    even, odd = step_masks(lax.axis_size("clip"))
    first = sum(m for t, m in enumerate(even) if code >> t & 1)
    second = sum(m for t, m in enumerate(odd) if code >> t & 1)
    return group ^ (first if first == second else jnp.where(core == 0, first, second))


def give(held, t):
    return jnp.concatenate([held[code].astype(BF16) for code in held if code >> t & 1], axis=0)


def take(held, t, got):
    low = [code for code in held if not code >> t & 1]
    rows = got.shape[0] // len(low)
    return {
        code: held[code].astype(F32) + got[n * rows : (n + 1) * rows].astype(F32)
        for n, code in enumerate(low)
    }


def bits(count):
    return count.bit_length() - 1


def pad_rows(values, rows):
    return jnp.pad(values, ((0, rows - values.shape[0]), (0, 0)))


def axis_weights(low_edge, high_edge, cell_count, first_cell, span_count):
    samples = (jnp.arange(SAMPLES, dtype=F32) + 0.5) / SAMPLES
    start_pos = low_edge.astype(F32) * 0.25
    extent = (high_edge - low_edge).astype(F32) * 0.25
    points = start_pos[:, None] + extent[:, None] * samples[None, :]
    points = jnp.clip(points - 0.5, 0.0, cell_count - 1.0)
    centers = (first_cell + jnp.arange(span_count, dtype=jnp.int32)).astype(F32)
    tents = jnp.maximum(0.0, 1.0 - jnp.abs(points[:, :, None] - centers[None, None, :]))
    return jnp.mean(tents, axis=1)


def box_weights(coords, clip_local, first_row, row_count, rows_total, clip_count, col_count):
    along_rows = axis_weights(coords[:, 0], coords[:, 1], rows_total, first_row, row_count)
    along_cols = axis_weights(coords[:, 2], coords[:, 3], col_count, 0, col_count)
    member = (clip_local[:, None] == jnp.arange(clip_count, dtype=jnp.int32)[None, :]).astype(F32)
    product = along_rows[:, None, :, None] * along_cols[:, None, None, :] * member[:, :, None, None]
    return product.astype(BF16)


def silu_slope(value_in):
    gate = jax.nn.sigmoid(value_in)
    return gate * (1.0 + value_in * (1.0 - gate))


VMEM = pl.BlockSpec(memory_space=pltpu.VMEM)
SMEM = pl.BlockSpec(memory_space=pltpu.SMEM)
MIB = 1024 * 1024
MIB_DEFAULT = 58


ANY = pl.BlockSpec(memory_space=pl.ANY)


class Loads:
    def __init__(self, pairs, sems):
        self.copies = [
            pltpu.make_async_copy(source, target, sems.at[n])
            for n, (source, target) in enumerate(pairs)
        ]
        self.done = 0
        for copy in self.copies:
            copy.start()

    def wait(self, count):
        while self.done < count:
            self.copies[self.done].wait()
            self.done += 1


def shape_of(shape, dtype):
    return jax.ShapeDtypeStruct(shape, dtype)


def run(kernel, outs, ins, grid=(), in_specs=None, out_specs=None, scratch=(), mib=MIB_DEFAULT):
    return pl.pallas_call(
        kernel,
        grid=grid,
        out_shape=tuple(outs),
        in_specs=in_specs or [VMEM] * len(ins),
        out_specs=tuple(out_specs or [VMEM] * len(outs)),
        scratch_shapes=list(scratch),
        compiler_params=pltpu.CompilerParams(vmem_limit_bytes=mib * MIB),
        cost_estimate=pl.CostEstimate(flops=0, bytes_accessed=0, transcendentals=0),
    )(*ins)


def frame_shift(values, clips, step):
    grid = values.reshape(clips, -1, values.shape[1])
    rows = grid.shape[1]
    zeros = jnp.zeros((clips, abs(step), values.shape[1]), values.dtype)
    if step > 0:
        moved = jnp.concatenate([zeros, grid[:, : rows - step]], axis=1)
    else:
        moved = jnp.concatenate([grid[:, -step:], zeros], axis=1)
    return moved.reshape(values.shape)


def col_shift(values, cols, step):
    col = lax.broadcasted_iota(jnp.int32, (values.shape[0], 1), 0) % cols
    edge = 0 if step > 0 else cols - 1
    rows = values.shape[0]
    return jnp.where(col == edge, 0.0, pltpu.roll(values, step % rows, 0))


def temporal_kernel(clips, cols, starts, x, w, gain, shift, total, out, *pieces):
    step = pl.program_id(0)
    values = x[...]
    for start, piece in zip(starts, pieces):
        piece[...] = x[start : start + piece.shape[0], :]
    term = mm(frame_shift(values, clips, cols), w[0]) + mm(values, w[1])
    term = term + mm(frame_shift(values, clips, -cols), w[2])

    @pl.when(step == 0)
    def _():
        total[...] = term

    @pl.when(step > 0)
    def _():
        total[...] += term

    @pl.when(step == pl.num_programs(0) - 1)
    def _():
        arg = total[...] * gain[0:1, :] + shift[0:1, :]
        out[...] = (arg * jax.nn.sigmoid(arg)).astype(BF16)


def plane_rows_sum(rows, weights, cols):
    sides = []
    for j in range(3):
        term = None
        for values, kernel in zip(rows, weights):
            part = mm(values, kernel[j])
            term = part if term is None else term + part
        sides.append(term)
    return sides[1] + col_shift(sides[0], cols, 1) + col_shift(sides[2], cols, -1)


def plane_own_kernel(cols, own, w, out):
    out[...] = plane_rows_sum([own[...]], [w[0]], cols)


def plane_kernel(
    clips,
    frames,
    cols,
    pos,
    above,
    below,
    first,
    last,
    part,
    gain,
    shift,
    expand,
    x,
    og,
    os,
    weights,
    short,
    classes,
    total,
    out,
    low,
    mine,
    other,
    projected,
):
    step = pl.program_id(0)

    @pl.when(step == 0)
    def _():
        whole = part[...] + plane_rows_sum([above[...], below[...]], [first[0], last[0]], cols)
        total[...] = whole
        arg = whole * gain[1:2, :] + shift[1:2, :]
        out[...] = (arg * jax.nn.sigmoid(arg)).astype(BF16)
        projected[...] = jnp.zeros_like(projected)

    arg = mm(out[...], expand[...]) * og[...] + os[...] + x[...].astype(F32)
    active = arg * jax.nn.sigmoid(arg)
    summed = jnp.sum(active.reshape(clips, frames, cols, -1), axis=1)
    pooled = (summed / frames).reshape(clips * cols, -1).astype(BF16)
    values = mm_tn(weights[...], pooled).astype(BF16)
    lanes = low.shape[2]
    for r in range(low.shape[0]):
        low[r] = values[:, r * lanes : (r + 1) * lanes]
    width = short.shape[1]
    count = classes.shape[0]
    projected[:, :width] += mm(values, short[...])
    projected[:, width : width + count] += mm_nt(values, classes[...])

    @pl.when(step == pl.num_programs(0) - 1)
    def _():
        half = mine.shape[0]
        mine[...] = projected[pl.ds(pos[0] * half, half), :]
        other[...] = projected[pl.ds((1 - pos[0]) * half, half), :].astype(BF16)


def slope_kernel(frames, plane_out, expand, x, og, os, sums, slope):
    expand_sum = mm(plane_out[...], expand[...])
    sums[...] = expand_sum.astype(BF16)
    arg = expand_sum * og[...] + os[...] + x[...].astype(F32)
    slope[...] = (silu_slope(arg) * (1.0 / frames)).astype(BF16)


def box_kernel(
    order,
    classes,
    clip_total,
    pos,
    own,
    other,
    bias,
    gain,
    shift,
    memory_far,
    weights_far,
    class_far,
    short_far,
    roi_far,
    scores,
    back_pooled,
    lefts,
    rights,
    keys,
    mixes,
    stats,
    last_low,
    first_low,
    back_logits_ref,
    norms,
    total,
    facts,
    attention_ref,
    memory,
    weights,
    class_rows,
    short,
    roi,
    sems,
):
    loads = Loads(
        [(weights_far.at[0, 0], weights.at[0, 0]), (weights_far.at[0, 1], weights.at[0, 1])]
        + [(memory_far, memory)]
        + [(weights_far.at[0, k], weights.at[0, k]) for k in (2, 3)]
        + [(weights_far.at[1], weights.at[1]), (class_far, class_rows)]
        + [(short_far, short), (roi_far, roi)],
        sems,
    )
    half = total.shape[0] // 2
    quarter = half // 2
    core, chip = pos[0], pos[1]
    side = chip % 2
    each = (own.shape[0] // 2 - quarter) * 2 // len(order)
    for sums, where in ((own, core), (other, 1 - core)):
        for n in range(2):
            base = n * (sums.shape[0] // 2)
            start = where * half + (side if n == 0 else 1 - side) * quarter
            total[pl.ds(start, quarter), :] = sums[base : base + quarter, :].astype(F32)
            for m in range(len(order) // 2):
                place = 4 * (chip ^ order[n * (len(order) // 2) + m]) + 2 * where
                rows = slice(base + quarter + m * each, base + quarter + (m + 1) * each)
                for part in range(2):
                    facts[pl.ds((place + part) * each, each), :] = sums[
                        rows, part * LANES : (part + 1) * LANES
                    ].astype(F32)
    width = memory.shape[1]
    scale = 1.0 / math.sqrt(width)
    clips, slots = bias.shape
    clip_rows = facts[:, classes + 1 : classes + 2].astype(jnp.int32)

    def select(values):
        chosen = values[:, :slots]
        for c in range(1, clips):
            chosen = jnp.where(clip_rows == c, values[:, c * slots : (c + 1) * slots], chosen)
        return chosen

    def spread(values):
        return jnp.concatenate(
            [jnp.where(clip_rows == c, values, 0.0).astype(BF16) for c in range(clips)], axis=1
        )

    dead = jnp.broadcast_to(bias[0:1, :], (clip_rows.shape[0], slots))
    for c in range(1, clips):
        dead = jnp.where(clip_rows == c, bias[c : c + 1, :], dead)
    stream = total[:, :width]
    kept = []
    for n in range(2):
        stream_low = stream.astype(BF16)
        loads.wait(1 if n == 0 else 6)
        query = mm(stream_low, weights[n, 0]).astype(BF16)
        loads.wait(2)
        query_key = mm_nt(query, weights[n, 1]).astype(BF16)
        loads.wait(3)
        masked = select(mm_nt(query_key, memory[...])) * scale + dead
        peak = jnp.max(masked, axis=1, keepdims=True)
        exponent = jnp.exp(masked - peak)
        whole = jnp.sum(exponent, axis=1, keepdims=True)
        attention = exponent * (1.0 / whole)
        attention_ref[n] = attention
        mixed = mm(spread(attention), memory[...]).astype(BF16)
        loads.wait(5)
        attended = mm(mixed, weights[n, 2])
        centred = attended - jnp.mean(attended, axis=1, keepdims=True)
        inverse = lax.rsqrt(jnp.mean(centred * centred, axis=1, keepdims=True) + EPSILON)
        hatted = centred * inverse
        normed = hatted * gain[n : n + 1, :] + shift[n : n + 1, :]
        hidden = (normed * jax.nn.sigmoid(normed)).astype(BF16)
        stream = stream + mm(hidden, weights[n, 3])
        lefts[4 * n] = stream_low
        lefts[4 * n + 2] = mixed
        lefts[4 * n + 3] = hidden
        rights[4 * n + 1] = query
        keys[n] = query_key
        kept.append((peak + jnp.log(whole), hatted, inverse, normed))
    stream_low = stream.astype(BF16)
    last_low[...] = stream_low
    loads.wait(7)
    split = class_rows.shape[1] - width
    logits = total[:, width : width + classes] + mm_nt(stream_low, class_rows[:, split:])
    chance = jax.nn.sigmoid(logits)
    scores[...] = chance
    valid = facts[:, classes : classes + 1]
    back_logits = (chance - facts[:, :classes]) * valid / clip_total
    back_logits = back_logits.astype(BF16)
    back_logits_ref[...] = back_logits
    back_stream = mm(back_logits, class_rows[:, split:])
    inners = [None, None]
    for n in (1, 0):
        log_sum, hatted, inverse, normed = kept[n]
        back_branch = back_stream.astype(BF16)
        back_normed = mm_nt(back_branch, weights[n, 3]) * silu_slope(normed)
        norms[n : n + 1, :] = jnp.sum(back_normed * hatted, axis=0, keepdims=True)
        norms[n + 2 : n + 3, :] = jnp.sum(back_normed, axis=0, keepdims=True)
        back_hat = back_normed * gain[n : n + 1, :]
        back_attended = inverse * (
            back_hat
            - jnp.mean(back_hat, axis=1, keepdims=True)
            - hatted * jnp.mean(back_hat * hatted, axis=1, keepdims=True)
        )
        back_att_low = back_attended.astype(BF16)
        back_mixed = mm_nt(back_att_low, weights[n, 2]).astype(BF16)
        attention = attention_ref[n]
        back_attention = select(mm_nt(back_mixed, memory[...]))
        inner = jnp.sum(attention * back_attention, axis=1, keepdims=True)
        back_raw = attention * (back_attention - inner) * scale
        back_key_mix = mm(spread(back_raw), memory[...]).astype(BF16)
        back_query = mm(back_key_mix, weights[n, 1]).astype(BF16)
        back_stream = back_stream + mm_nt(back_query, weights[n, 0])
        lefts[4 * n + 1] = back_key_mix
        rights[4 * n] = back_query
        rights[4 * n + 2] = back_att_low
        rights[4 * n + 3] = back_branch
        mixes[n] = back_mixed
        inners[n] = inner
    lane = lax.broadcasted_iota(jnp.int32, stats.shape, 1)
    stats[...] = jnp.where(
        lane == 0,
        kept[0][0],
        jnp.where(
            lane == 1,
            kept[1][0],
            jnp.where(
                lane == 2,
                inners[0],
                jnp.where(lane == 3, inners[1], facts[:, classes + 1 : classes + 2]),
            ),
        ),
    )
    back_low = back_stream.astype(BF16)
    first_low[...] = back_low
    loads.wait(9)
    back_boxes = mm(back_logits, class_rows[:, :split]) + mm_nt(back_low, short[...])
    back_pooled[...] = mm(roi[...], back_boxes.astype(BF16))


def bank_kernel(
    pos, keys, mixes, stats, memory, tag, feats, low, back_logits, last_low, wide, rows
):
    width = memory.shape[1]
    scale = 1.0 / math.sqrt(width)
    allowed = stats[:, 4:5].astype(jnp.int32) == tag[...]
    back_memory = None
    for n in range(2):
        raw = mm_nt(keys[n], memory[...])
        attention = jnp.where(allowed, jnp.exp(raw * scale - stats[:, n : n + 1]), 0.0)
        back_attention = mm_nt(mixes[n], memory[...])
        back_raw = (attention * (back_attention - stats[:, n + 2 : n + 3]) * scale).astype(BF16)
        term = mm_tn(back_raw, keys[n]) + mm_tn(attention.astype(BF16), mixes[n])
        back_memory = term if back_memory is None else back_memory + term
    count, boxes, lanes = low.shape
    low_memory = back_memory.astype(BF16)
    fine = rows.shape[0] // count // (width // LANES)
    for r in range(count):
        values = mm_tn(feats[:, r * lanes : (r + 1) * lanes], low_memory)
        wide[r, fine:, :] = values.astype(BF16)
    classes = back_logits.shape[1]
    rows[...] = jnp.zeros_like(rows)
    for r in range(count):
        rows[r * lanes : (r + 1) * lanes, :classes] = mm_tn(low[r], back_logits[...])
    box = lax.broadcasted_iota(jnp.int32, (boxes, 1), 0)
    mine = (box // (boxes // count)) == 2 * pos[1] + pos[0]
    own_logits = jnp.where(mine, back_logits[...].astype(F32), 0.0).astype(BF16)
    rows[count * lanes :, :classes] = mm_tn(last_low[...], own_logits)
    blocks = width // LANES
    for r in range(count):
        for q in range(blocks):
            start = (r * blocks + q) * fine
            wide[r, :fine, q * LANES : (q + 1) * LANES] = rows[start : start + fine, :].astype(BF16)


def block_kernel(lefts, rights, pick, norms, block):
    own = pick.shape[1]
    for item in range(8):
        columns = mm(lefts[item], pick[...]).astype(BF16)
        block[item * own : (item + 1) * own, :] = mm_tn(columns, rights[item]).astype(BF16)
    block[8 * own :, :] = jnp.zeros((block.shape[0] - 8 * own, block.shape[1]), BF16)
    for n in range(2):
        start = 8 * own + n * 2 * SUBLANES
        block[start : start + 2, :] = norms[2 * n : 2 * n + 2, :].astype(BF16)


def weight_kernel(cols, count, pos, back_expand, plane_out, above, own, below, back_plane, keep, send):
    width = plane_out.shape[1]
    lanes = back_expand.shape[1] // count
    rows = width // count

    def put(start, first, second):
        place = slice(start, start + first.shape[0])

        @pl.when(pos[0] == 0)
        def _():
            keep[place, :] = first.astype(BF16)
            send[place, :] = second.astype(BF16)

        @pl.when(pos[0] != 0)
        def _():
            keep[place, :] = second.astype(BF16)
            send[place, :] = first.astype(BF16)

    each = lanes + 9 * rows
    for chip in range(count // 2):
        block = mm_tn(back_expand[:, 2 * chip * lanes : 2 * (chip + 1) * lanes], plane_out[...])
        put(chip * each, block[:lanes], block[lanes:])
    whole = back_plane[...].astype(F32)
    moved = jnp.concatenate(
        [
            col_shift(whole, cols, -1).astype(BF16),
            back_plane[...],
            col_shift(whole, cols, 1).astype(BF16),
        ],
        axis=1,
    )
    for i, source in enumerate((above, own, below)):
        block = mm_tn(source[...], moved)
        for j in range(3):
            for chip in range(count // 2):
                start = chip * each + lanes + (3 * i + j) * rows
                top = 2 * chip * rows
                columns = slice(j * width, (j + 1) * width)
                put(
                    start,
                    block[top : top + rows, columns],
                    block[top + rows : top + 2 * rows, columns],
                )


def temporal_grad_kernel(clips, cols, count, lanes, pos, *refs):
    sources, pieces = refs[: -3 - count], refs[-3 - count : -3]
    keep, send, moved = refs[-3:]
    step = pl.program_id(0)
    cells, wide = sources[0].shape
    part = pieces[0].shape[1]

    @pl.when(step == 0)
    def _():
        facts = None
        for s, piece in enumerate(pieces):
            values = piece[:cells, :]
            shifts = (frame_shift(values, clips, -cols), values, frame_shift(values, clips, cols))
            for k in range(3):
                moved[k * part : (k + 1) * part, s * cells : (s + 1) * cells] = shifts[k].T
            term = piece[cells:, :].astype(F32)
            facts = term if facts is None else facts + term
        low = facts.astype(BF16)
        each = 3 * lanes + low.shape[0]
        for end in range(each, keep.shape[0] + 1, each):
            keep[end - low.shape[0] : end, :] = low
            send[end - low.shape[0] : end, :] = low

    total, start = None, 0
    for source in sources:
        end = start + source.shape[0]
        term = mm(moved[:, start:end], source[...])
        total = term if total is None else total + term
        start = end
    blocks = wide // (2 * lanes)
    each = 3 * lanes + pieces[0].shape[0] - cells
    for block in range(blocks):
        for k in range(3):
            turned = total[k * part : (k + 1) * part, 2 * block * lanes : 2 * (block + 1) * lanes].T
            start = pl.multiple_of(step * (blocks * each), 16) + block * each + k * lanes
            first = turned[:lanes].astype(BF16)
            second = turned[lanes:].astype(BF16)

            @pl.when(pos[0] == 0)
            def _():
                keep[pl.ds(start, lanes), :] = first
                send[pl.ds(start, lanes), :] = second

            @pl.when(pos[0] != 0)
            def _():
                keep[pl.ds(start, lanes), :] = second
                send[pl.ds(start, lanes), :] = first


def back_plane_kernel(
    clips,
    frames,
    cols,
    back_pooled,
    slope,
    sums,
    expand,
    og,
    plane_sum,
    gain,
    shift,
    back_expand,
    back_plane,
    facts,
    acc,
    rows,
):
    step = pl.program_id(0)
    steps = pl.num_programs(0)
    cells, lanes = slope.shape

    @pl.when(step == 0)
    def _():
        rows[...] = jnp.zeros_like(rows)

    pooled = back_pooled[...].reshape(clips, 1, cols, lanes)
    final = (pooled * slope[...].astype(F32).reshape(clips, frames, cols, lanes)).reshape(cells, lanes)
    rows[pl.ds(step, 1), :] = jnp.sum(final * sums[...].astype(F32), axis=0, keepdims=True)
    rows[pl.ds(steps + step, 1), :] = jnp.sum(final, axis=0, keepdims=True)
    low = (final * og[...]).astype(BF16)
    back_expand[...] = low
    term = mm_nt(low, expand[...])

    @pl.when(step == 0)
    def _():
        acc[...] = term

    @pl.when(step > 0)
    def _():
        acc[...] += term

    @pl.when(step == steps - 1)
    def _():
        back_arg = acc[...] * silu_slope(plane_sum[...] * gain[1:2, :] + shift[1:2, :])
        rows[pl.ds(2 * steps, 1), :] = jnp.sum(back_arg * plane_sum[...], axis=0, keepdims=True)
        rows[pl.ds(2 * steps + 1, 1), :] = jnp.sum(back_arg, axis=0, keepdims=True)
        back_plane[...] = (back_arg * gain[1:2, :]).astype(BF16)
        facts[...] = rows[...].astype(BF16)


def back_temporal_kernel(
    cols, pos, gain, shift, late, rows, w, temporal_sum, out, facts, *pieces
):
    sides = []
    for j in range(3):
        term = mm_nt(rows[0][...], w[0, j]) + mm_nt(rows[1][...], w[1, j])
        sides.append(term + mm_nt(rows[2][...], w[2, j]))
    back_out = sides[1] + col_shift(sides[0], cols, -1) + col_shift(sides[2], cols, 1)
    back_arg = back_out * silu_slope(temporal_sum[...] * gain[0:1, :] + shift[0:1, :])
    cells, width = out.shape
    facts[...] = late[...].astype(F32)
    facts[facts.shape[0] - 2 : facts.shape[0] - 1, :] = jnp.sum(
        back_arg * temporal_sum[...], axis=0, keepdims=True
    )
    facts[facts.shape[0] - 1 :, :] = jnp.sum(back_arg, axis=0, keepdims=True)
    out[...] = (back_arg * gain[0:1, :]).astype(BF16)
    for s, piece in enumerate(pieces):
        start = pl.multiple_of(pos[2 + s] * LANES, LANES)
        piece[:cells, :] = out[:, pl.ds(start, LANES)]
        rows = facts.shape[0]
        for q in range(width // LANES):
            piece[cells + q * rows : cells + (q + 1) * rows, :] = facts[
                :, q * LANES : (q + 1) * LANES
            ].astype(BF16)


def input_kernel(clips, frames, cols, back, w, back_pooled, slope, out):
    values = back[...]
    cells, lanes = slope.shape
    pooled = back_pooled[...].reshape(clips, 1, cols, lanes)
    total = (pooled * slope[...].astype(F32).reshape(clips, frames, cols, lanes)).reshape(cells, lanes)
    total = total + mm_nt(values, w[1]) + mm_nt(frame_shift(values, clips, -cols), w[0])
    out[...] = total + mm_nt(frame_shift(values, clips, cols), w[2])


def lanes_kernel(counts, forms, pos, *refs):
    outs, whole = refs[-1 - len(counts) : -1], refs[-1]
    rows = whole.shape[0]
    index = 0
    for ref in refs[: -1 - len(counts)]:
        for n in range(ref.shape[0] // rows):
            start = pl.multiple_of(pos[index] * LANES, LANES)
            whole[:, pl.ds(start, LANES)] = ref[n * rows : (n + 1) * rows, :]
            index += 1
    start = 0
    for count, form, out in zip(counts, forms, outs):
        piece = whole[start : start + count, :].astype(F32)
        start += count
        if form == 0:
            out[...] = piece
        elif form == 1:
            out[...] = piece.T
        elif form == 2:
            for q in range(whole.shape[1] // LANES):
                first = q * LANES
                out[:, q * count : (q + 1) * count] = piece[:, first : first + out.shape[0]].T
        else:
            own = out.shape[1]
            shift = whole.shape[1] - pos[pos.shape[0] - 1] * own
            moved = pltpu.roll(piece[: 2 * SUBLANES, :], shift, 1)
            out[...] = moved[: out.shape[0], :own]


def blocks_kernel(codes, pos, *refs):
    sources, outs = refs[: -len(codes)], refs[-len(codes) :]
    for group, out in zip(codes, outs):
        row = 0
        for code in group:
            start = pl.multiple_of(pos[code] * LANES, LANES)
            for source in sources:
                count = source.shape[0]
                out[row : row + count, :] = source[:, pl.ds(start, LANES)]
                row += count


class Halving:
    def __init__(self, held, steps, send, step=0, first=None):
        self.held, self.steps, self.send = held, steps, send
        self.step, self.got, self.first = step, None, first

    def advance(self, hold):
        if self.got is not None:
            self.held = take(self.held, self.step - 1, self.got)
            self.got = None
        if self.step < self.steps:
            buffer = give(self.held, self.step) if self.first is None else self.first
            self.first = None
            buffer, hold = lax.optimization_barrier((buffer, hold))
            self.got = self.send(self.step, buffer)
            self.step += 1
        return hold

    def finish(self):
        while self.got is not None:
            self.advance(())
        return self.held[0]


class Doubling:
    def __init__(self, own, steps, send):
        self.parts, self.steps, self.send = [own], steps, send
        self.step, self.got = 0, None

    def advance(self, hold):
        if self.got is not None:
            self.parts.append(self.got)
            self.got = None
        if self.step < self.steps:
            buffer = self.parts[0] if self.step == 0 else jnp.concatenate(self.parts, axis=0)
            buffer, hold = lax.optimization_barrier((buffer, hold))
            self.got = self.send(self.step, buffer)
            self.step += 1
        return hold

    def finish(self):
        while self.got is not None:
            self.advance(())
        return self.parts


def window(values, chains):
    chains = [chain for chain in chains if chain.got is not None]
    tied = lax.optimization_barrier((tuple(values), tuple(chain.got for chain in chains)))
    for chain, got in zip(chains, tied[1]):
        chain.got = got
    return tied[0]


def join_lanes(parts, places):
    rows = parts[0].shape[0]
    blocks = [part[n * rows : (n + 1) * rows] for part in parts for n in range(part.shape[0] // rows)]
    joined = []
    for target in range(len(blocks)):
        chosen = blocks[0]
        for code in range(1, len(blocks)):
            chosen = jnp.where(places[code] == target, blocks[code], chosen)
        joined.append(chosen)
    return jnp.concatenate(joined, axis=-1).astype(F32)


def body(
    clip_input,
    temporal,
    spatial,
    expand,
    mid_gain,
    mid_shift,
    out_gain,
    out_shift,
    short_weight,
    bank_weight,
    block_weight,
    norm_gain,
    norm_shift,
    class_weight,
    bank_feats,
    bank_mask,
    box_coords,
    box_clip,
    box_valid,
    labels,
):
    row = lax.axis_index("row")
    group = lax.axis_index("clip")
    row_size = lax.axis_size("row")
    clip_size = lax.axis_size("clip")
    core = row % 2
    chip = row // 2
    chips = row_size // 2
    clips, frames, rows_local, cols, channels = clip_input.shape
    mid = temporal.shape[2]
    width = short_weight.shape[1]
    classes = class_weight.shape[1]
    cells = clips * frames * cols
    boxes = box_coords.shape[0]
    box_local = labels.shape[0]
    slots_local = bank_feats.shape[1]
    part = mid // clip_size
    steps = channels // mid
    lanes = channels // row_size
    crossed = clip_size == 4
    masks = [(s, s) for s in range(clip_size)]
    if crossed:
        masks = [(0, 0), (1, 2), (2, 1), (3, 3)]
    targets = [group ^ jnp.where(core == 0, first, second) for first, second in masks]
    place = jnp.stack([core, chip, *targets]).astype(jnp.int32)
    og, os = out_gain[None], out_shift[None]

    tie = lax.optimization_barrier
    source = clip_input.reshape(cells, channels)

    wide_input = [source]
    if not crossed:
        wide_input += [swap(source, "clip", s) for s in range(1, clip_size)]

    def passed(values, after, even_mask, odd_mask):
        values, _ = tie((values, after))
        return joint_swap(values, even_mask, odd_mask)

    def kernel_row(i):
        return pl.BlockSpec((1, 3, mid, mid), lambda _: (i, 0, 0, 0))

    def fixed(*shape):
        return pl.BlockSpec(shape, lambda i: (0,) * len(shape))

    def across(height, lane_count):
        return pl.BlockSpec((height, lane_count), lambda i: (0, i))

    eighth = cells // 8
    cuts = [(0, 2), (2, 4), (6, 2), (0, 1), (1, 6), (7, 1)] if crossed else []
    temporal_sum, temporal_out, *cut_rows = run(
        lambda *refs: temporal_kernel(clips, cols, [start * eighth for start, _ in cuts], *refs),
        [shape_of((cells, mid), F32), shape_of((cells, mid), BF16)]
        + [shape_of((count * eighth, channels), BF16) for _, count in cuts],
        [source, temporal, mid_gain, mid_shift],
        grid=(steps,),
        in_specs=[
            across(cells, mid),
            pl.BlockSpec((3, mid, mid), lambda i: (0, i, 0)),
            fixed(2, mid),
            fixed(2, mid),
        ],
        out_specs=[fixed(cells, mid), fixed(cells, mid)]
        + [across(count * eighth, mid) for _, count in cuts],
    )

    def halo(values):
        ends = row_size - 1
        above = lax.ppermute(values, "row", [(i, i + 1) for i in range(ends)])
        below = lax.ppermute(values, "row", [(i + 1, i) for i in range(ends)])
        return above, below

    above_row, below_row = halo(temporal_out)

    if crossed:
        first_a = joint_swap(cut_rows[0], 1, 2)
    feats, box_coords, temporal_out = tie(
        (bank_feats.reshape(clips * slots_local, channels), box_coords, temporal_out)
    )
    memory_own = mm(feats, bank_weight).astype(BF16)
    clip_group = box_clip - group * clips
    weights = box_weights(
        box_coords, clip_group, row * rows_local, rows_local, rows_local * row_size, clips, cols
    ).reshape(boxes, clips * cols).T
    class_rows = class_weight.T

    (plane_part,) = run(
        lambda *refs: plane_own_kernel(cols, *refs),
        [shape_of((cells, mid), F32)],
        [temporal_out, spatial],
        grid=(1,),
        in_specs=[fixed(cells, mid), kernel_row(1)],
        out_specs=[fixed(cells, mid)],
    )
    above_row, below_row, memory_own, plane_part = tie(
        (above_row, below_row, memory_own, plane_part)
    )
    memory = lax.all_gather(
        memory_own.reshape(clips, slots_local, width), "row", axis=1, tiled=True
    ).reshape(-1, width)
    tied = (above_row, below_row, plane_part, weights, class_rows)
    if crossed:
        *tied, first_a = tie((*tied, first_a))
    else:
        tied = tie(tied)
    above_row, below_row, plane_part, weights, class_rows = tied
    if crossed:
        first_b = passed(cut_rows[1], above_row, 1, 2)
    half = boxes // 2
    joint = width + LANES
    plane_sum, plane_out, partial_low, mine, other = run(
        lambda *refs: plane_kernel(clips, frames, cols, *refs),
        [
            shape_of((cells, mid), F32),
            shape_of((cells, mid), BF16),
            shape_of((row_size, boxes, lanes), BF16),
            shape_of((half, joint), F32),
            shape_of((half, joint), BF16),
        ],
        [
            place,
            above_row,
            below_row,
            spatial,
            spatial,
            plane_part,
            mid_gain,
            mid_shift,
            expand,
            source,
            og,
            os,
            weights,
            short_weight,
            class_rows,
        ],
        grid=(steps,),
        in_specs=[
            SMEM,
            fixed(cells, mid),
            fixed(cells, mid),
            kernel_row(0),
            kernel_row(2),
            fixed(cells, mid),
            fixed(2, mid),
            fixed(2, mid),
            across(mid, mid),
            across(cells, mid),
            across(1, mid),
            across(1, mid),
            fixed(clips * cols, boxes),
            pl.BlockSpec((mid, width), lambda i: (i, 0)),
            across(classes, mid),
        ],
        out_specs=[
            fixed(cells, mid),
            fixed(cells, mid),
            pl.BlockSpec((mid // lanes, boxes, lanes), lambda i: (i, 0, 0)),
            fixed(half, joint),
            fixed(half, joint),
        ],
        scratch=[pltpu.VMEM((boxes, joint), F32)],
    )

    if crossed:
        mine, other, plane_out, first_b = tie((mine, other, plane_out, first_b))
        first_c = passed(cut_rows[2], mine, 1, 2)
        second_a = passed(cut_rows[3], mine, 2, 1)
    clip_own = lax.dynamic_slice_in_dim(clip_group, row * box_local, box_local, 0)
    facts = jnp.concatenate(
        [labels.astype(BF16), box_valid.astype(BF16)[:, None], clip_own.astype(BF16)[:, None]], axis=1
    )
    facts = jnp.pad(facts, ((0, 0), (0, LANES - facts.shape[1])))
    facts = jnp.concatenate([facts[: box_local // 2], facts[box_local // 2 :]], axis=1)
    facts = jnp.pad(facts, ((0, 0), (0, joint - 2 * LANES)))
    half_sum = mine + swap(other, "row", 1).astype(F32)
    quarter = half // 2
    side = chip % 2
    got = swap(
        lax.dynamic_slice_in_dim(half_sum, (1 - side) * quarter, quarter, 0).astype(BF16), "row", 2
    )
    plane_late, _ = tie((plane_out, half_sum))
    expand_sums, slope = run(
        lambda *refs: slope_kernel(frames, *refs),
        [shape_of((cells, channels), BF16), shape_of((cells, channels), BF16)],
        [plane_late, expand, source, og, os],
        grid=(steps,),
        in_specs=[
            fixed(cells, mid),
            across(mid, mid),
            across(cells, mid),
            across(1, mid),
            across(1, mid),
        ],
        out_specs=[across(cells, mid)] * 2,
    )
    if crossed:
        got, slope, first_c, second_a = tie((got, slope, first_c, second_a))
    else:
        got, slope = tie((got, slope))
    part_sum = lax.dynamic_slice_in_dim(half_sum, side * quarter, quarter, 0) + got.astype(F32)
    label_rows, codes = [facts], [0]
    for t in range(1, bits(chips)):
        payload = jnp.concatenate([part_sum.astype(BF16)] + label_rows, axis=0)
        got = swap(payload, "row", 2 << t)
        part_sum = part_sum + got[:quarter].astype(F32)
        each = facts.shape[0]
        label_rows = label_rows + [
            got[quarter + n * each : quarter + (n + 1) * each] for n in range(len(codes))
        ]
        codes = codes + [code ^ (1 << t) for code in codes]
    payload = jnp.concatenate([part_sum.astype(BF16)] + label_rows, axis=0)
    got = swap(payload, "row", 2)
    live = bank_mask == 1
    tags = jnp.where(live, jnp.arange(clips, dtype=jnp.int32)[:, None], -1)
    tags_own = lax.dynamic_slice_in_dim(tags, row * slots_local, slots_local, 1).reshape(1, -1)
    bias = jnp.where(live, 0.0, -jnp.inf).astype(F32)
    got, memory, bias = tie((got, memory, bias))
    totals_own = jnp.concatenate([payload, got], axis=0)
    label_order = codes + [code ^ 1 for code in codes]
    totals_other = swap(totals_own, "row", 1)
    if crossed:
        second_b = passed(cut_rows[4], totals_own, 2, 1)

    partial_low, totals_other = tie((partial_low, totals_other))
    short_columns = lax.psum_scatter(partial_low, "row", scatter_dimension=0, tiled=False)

    slots = bias.shape[1]
    stream_shape = (boxes, width)
    (
        scores_all,
        back_pooled,
        lefts,
        rights,
        keys,
        mixes,
        stats,
        last_low,
        first_low,
        back_logits,
        norms,
    ) = run(
        lambda *refs: box_kernel(label_order, classes, float(clips * clip_size), *refs),
        [
            shape_of((boxes, classes), F32),
            shape_of((clips * cols, channels), F32),
            shape_of((8, *stream_shape), BF16),
            shape_of((8, *stream_shape), BF16),
            shape_of((2, *stream_shape), BF16),
            shape_of((2, *stream_shape), BF16),
            shape_of((boxes, LANES), F32),
            shape_of(stream_shape, BF16),
            shape_of(stream_shape, BF16),
            shape_of((boxes, classes), BF16),
            shape_of((4, width), F32),
        ],
        [
            place,
            totals_own,
            totals_other,
            bias,
            norm_gain,
            norm_shift,
            memory,
            block_weight,
            class_rows,
            short_weight,
            weights,
        ],
        in_specs=[SMEM] + [VMEM] * 5 + [ANY] * 5,
        scratch=[
            pltpu.VMEM((boxes, joint), F32),
            pltpu.VMEM((boxes, LANES), F32),
            pltpu.VMEM((2, boxes, slots), F32),
            pltpu.VMEM(memory.shape, BF16),
            pltpu.VMEM(block_weight.shape, BF16),
            pltpu.VMEM(class_rows.shape, BF16),
            pltpu.VMEM(short_weight.shape, BF16),
            pltpu.VMEM(weights.shape, BF16),
            pltpu.SemaphoreType.DMA((9,)),
        ],
    )
    scores = lax.dynamic_slice_in_dim(scores_all, row * box_local, box_local, 0)

    if crossed:
        back_pooled, second_b = tie((back_pooled, second_b))
        third_a = passed(first_a, back_pooled, 2, 1)

    fact_rows = -(-(2 * steps + 2) // 16) * 16
    back_expand, back_plane, second_facts = run(
        lambda *refs: back_plane_kernel(clips, frames, cols, *refs),
        [
            shape_of((cells, channels), BF16),
            shape_of((cells, mid), BF16),
            shape_of((fact_rows, mid), BF16),
        ],
        [
            back_pooled,
            slope,
            expand_sums,
            expand,
            og,
            plane_sum,
            mid_gain,
            mid_shift,
        ],
        grid=(steps,),
        in_specs=[
            across(clips * cols, mid),
            across(cells, mid),
            across(cells, mid),
            across(mid, mid),
            across(1, mid),
            fixed(cells, mid),
            fixed(2, mid),
            fixed(2, mid),
        ],
        out_specs=[
            across(cells, mid),
            fixed(cells, mid),
            fixed(fact_rows, mid),
        ],
        scratch=[pltpu.VMEM((cells, mid), F32), pltpu.VMEM((fact_rows, mid), F32)],
    )

    if crossed:
        back_plane, back_expand, second_facts, third_a = tie(
            (back_plane, back_expand, second_facts, third_a)
        )
        second_c = passed(cut_rows[5], back_plane, 2, 1)
        third_b = passed(first_b, back_plane, 2, 1)
    back_above, back_below = halo(back_plane)

    fact_count = second_facts.shape[0]
    own_mid = mid // row_size
    own_rows = channels // row_size

    weight_rows = own_rows + 9 * own_mid
    kept_weight, sent_weight = run(
        lambda *refs: weight_kernel(cols, row_size, *refs),
        [shape_of((chips * weight_rows, mid), BF16)] * 2,
        [
            place,
            back_expand,
            plane_out,
            above_row,
            temporal_out,
            below_row,
            back_plane,
        ],
        in_specs=[SMEM] + [VMEM] * 6,
    )
    tied = (back_above, back_below, kept_weight, sent_weight, short_columns)
    if crossed:
        *tied, second_c, third_b = tie((*tied, second_c, third_b))
        third_c = passed(first_c, sent_weight, 2, 1)
        wide_input += [first_a, first_b, first_c, second_a, second_b, second_c]
        wide_input += [third_a, third_b, third_c]
    else:
        tied = tie(tied)
    back_above, back_below, kept_weight, sent_weight, short_columns = tied
    got_weight = swap(sent_weight, "row", 1)

    even, odd = step_masks(clip_size)
    places = [place_of(code, group, core) for code in range(clip_size)]
    block_places = jnp.stack([jnp.asarray(item, jnp.int32) for item in places])

    def clip_step(t, values):
        return joint_swap(values, even[t], odd[t])

    def chip_step(t, values):
        return swap(values, "row", 2 << t)

    def lane_block(values, target):
        return lax.dynamic_slice_in_dim(values, target * part, part, 1)

    def chip_rows(target, *values):
        each = values[0].shape[0] // chips
        rows = [lax.dynamic_slice_in_dim(item, target * each, each, 0) for item in values]
        if len(rows) == 1:
            return rows[0]
        return tree_sum([item.astype(F32) for item in rows]).astype(BF16)

    def over_chips(*values):
        return Halving(
            {code: chip_rows(chip ^ code, *values) for code in range(chips)}, bits(chips), chip_step
        )

    def over_clips(piece):
        return Halving(
            {code: piece(places[code]) for code in range(clip_size)}, bits(clip_size), clip_step
        )

    class_fine = (channels + width) // row_size * LANES // width
    keys, _ = tie((keys, sent_weight))
    (wide_part,) = run(
        bank_kernel,
        [shape_of((row_size, class_fine + own_rows, width), BF16)],
        [
            place,
            keys,
            mixes,
            stats,
            memory_own,
            tags_own,
            feats,
            partial_low,
            back_logits,
            last_low,
        ],
        in_specs=[SMEM] + [VMEM] * 9,
        scratch=[pltpu.VMEM((channels + width, LANES), F32)],
    )
    if crossed:
        got_weight, wide_part, third_c = tie((got_weight, wide_part, third_c))
        wide_input[-3:] = [third_a, third_b, third_c]
    else:
        got_weight, wide_part = tie((got_weight, wide_part))
    wide_own = lax.psum_scatter(wide_part, "row", scatter_dimension=0, tiled=False)

    def weight_blocks(codes):
        return {
            code: (
                lane_block(kept_weight, places[code]).astype(F32)
                + lane_block(got_weight, places[code]).astype(F32)
            ).astype(BF16)
            for code in codes
        }

    high = [code for code in range(clip_size) if code & 1]
    late, early = high[: len(high) // 2], high[len(high) // 2 :]
    held = weight_blocks(early)
    buffers, back_above = tie((tuple(held[code] for code in early), back_above))
    first_step = {code: clip_step(0, values) for code, values in zip(early, buffers)}

    direct = part == LANES
    piece_rows = fact_rows * (mid // part)
    back_temporal, facts_own, *pieces = run(
        lambda pos, gain, shift, late, below, own, above, *refs: back_temporal_kernel(
            cols, pos, gain, shift, late, (below, own, above), *refs
        ),
        [shape_of((cells, mid), BF16), shape_of((fact_rows, mid), F32)]
        + [shape_of((cells + piece_rows, part), BF16)] * (clip_size if direct else 0),
        [
            place,
            mid_gain,
            mid_shift,
            second_facts,
            back_below,
            back_plane,
            back_above,
            spatial,
            temporal_sum,
        ],
        in_specs=[SMEM] + [VMEM] * 8,
    )
    if not direct:
        facts_flat = jnp.concatenate(
            [facts_own[:, q * part : (q + 1) * part] for q in range(mid // part)], axis=0
        ).astype(BF16)
        pieces = [
            jnp.concatenate(
                [lax.dynamic_slice_in_dim(back_temporal, target * part, part, 1), facts_flat], axis=0
            )
            for target in targets
        ]
    back_temporal, first_step, pieces = tie((back_temporal, first_step, tuple(pieces)))

    got = pieces[:1] + tuple(
        joint_swap(piece, *step_mask) for piece, step_mask in zip(pieces[1:], masks[1:])
    )
    kept_weight, got_weight, _ = tie((kept_weight, got_weight, back_temporal))
    held.update(weight_blocks([code for code in range(clip_size) if code not in early]))
    pick = (
        jnp.arange(width, dtype=jnp.int32)[:, None]
        == row * own_mid + jnp.arange(own_mid, dtype=jnp.int32)[None, :]
    ).astype(BF16)
    lefts, _ = tie((lefts, back_temporal))
    (block_part,) = run(
        block_kernel,
        [shape_of((8 * own_mid + 32, width), BF16)],
        [lefts, rights, pick, norms],
    )
    short_part = mm_tn(short_columns, first_low).astype(BF16)
    got, block_part, short_part, held = tie((got, block_part, short_part, held))

    buffers, got = tie((tuple(held[code] for code in late), got))
    first_step.update({code: clip_step(0, values) for code, values in zip(late, buffers)})
    temporal_rows = chips * (3 * own_rows + piece_rows)
    kept_temporal, sent_temporal = run(
        lambda *refs: temporal_grad_kernel(clips, cols, clip_size, lanes, *refs),
        [shape_of((temporal_rows, part), BF16)] * 2,
        [place, *wide_input, *got],
        grid=(steps,),
        in_specs=[SMEM]
        + [across(item.shape[0], mid) for item in wide_input]
        + [fixed(cells + piece_rows, part)] * clip_size,
        out_specs=[fixed(temporal_rows, part)] * 2,
        scratch=[pltpu.VMEM((3 * part, clip_size * cells), BF16)],
    )
    tied = tie((kept_temporal, sent_temporal, first_step))
    kept_temporal, sent_temporal, first_step = tied
    got_temporal = swap(sent_temporal, "row", 1)
    sums_weight = Halving(
        {
            code ^ 1: held[code ^ 1].astype(F32) + values.astype(F32)
            for code, values in first_step.items()
        },
        bits(clip_size),
        clip_step,
        step=1,
    )
    got_temporal = sums_weight.advance(got_temporal)
    sums_temporal = over_chips(kept_temporal, got_temporal)
    back_temporal = sums_temporal.advance(back_temporal)

    (input_grad,) = run(
        lambda *refs: input_kernel(clips, frames, cols, *refs),
        [shape_of((cells, channels), F32)],
        [back_temporal, temporal, back_pooled, slope],
        grid=(steps,),
        in_specs=[
            fixed(cells, mid),
            pl.BlockSpec((3, mid, mid), lambda i: (0, i, 0)),
            across(clips * cols, mid),
            across(cells, mid),
        ],
        out_specs=[across(cells, mid)],
    )
    input_grad = input_grad.reshape(clip_input.shape)

    box_wide = [wide_own.reshape(-1, width), block_part, short_part]
    box_rows = sum(item.shape[0] for item in box_wide)
    if direct:
        groups = [[code for code in range(clip_size) if code & 1 == bit] for bit in (0, 1)]
        kept_box, sent_box = run(
            lambda *refs: blocks_kernel(groups, *refs),
            [shape_of((len(groups[0]) * box_rows, part), BF16)] * 2,
            [block_places, *box_wide],
            in_specs=[SMEM] + [VMEM] * len(box_wide),
        )
        input_grad, kept_box, sent_box = window(
            [input_grad, kept_box, sent_box], [sums_weight, sums_temporal]
        )
        sums_box = Halving(
            {
                code: kept_box[n * box_rows : (n + 1) * box_rows]
                for n, code in enumerate(groups[0])
            },
            bits(clip_size),
            clip_step,
            first=sent_box,
        )
    else:
        (input_grad,) = window([input_grad], [sums_weight, sums_temporal])
        sums_box = over_clips(
            lambda target: jnp.concatenate([lane_block(item, target) for item in box_wide], axis=0)
        )
    sums_weight.got = sums_temporal.advance(sums_weight.got)
    sums_chip = over_chips(tie(sums_weight.finish().astype(BF16)))
    sums_chip.advance(())
    sums_box.advance(())
    window([], [sums_temporal, sums_chip, sums_box])
    sums_chip.advance(())
    sums_box.advance(())
    temporal_got = sums_temporal.finish()
    own_temporal = 3 * own_rows
    facts_total = temporal_got[own_temporal:].reshape(mid // part, fact_rows, part)
    facts_total = jnp.concatenate([facts_total[q] for q in range(mid // part)], axis=1)
    all_first = Doubling(temporal_got[:own_temporal].astype(BF16), bits(clip_size), clip_step)
    all_first.advance(())
    window([], [sums_chip, sums_box, all_first])
    all_first.advance(())
    weight_own = sums_chip.finish().astype(BF16)
    box_own = sums_box.finish().astype(BF16)
    all_last = Doubling(
        jnp.concatenate([weight_own, box_own], axis=0), bits(clip_size), clip_step
    )
    all_last.advance(())
    window([], [all_first, all_last])
    all_last.advance(())
    firsts = all_first.finish()
    lasts = all_last.finish()
    class_count = class_fine * width // LANES
    last_counts = [own_rows, 9 * own_mid, class_fine, own_rows, 8 * own_mid, 16, 16, own_rows]
    last_shapes = [(mid, own_rows), (9 * own_mid, mid), (classes, class_count), (own_rows, width)]
    last_shapes += [(8 * own_mid, width), (2, own_mid), (2, own_mid), (own_rows, width)]

    def assemble(parts, counts, shapes, forms):
        if direct:
            return run(
                lambda *refs: lanes_kernel(counts, forms, *refs),
                [shape_of(shape, F32) for shape in shapes],
                [jnp.append(block_places, row.astype(jnp.int32)), *parts],
                in_specs=[SMEM] + [VMEM] * len(parts),
                scratch=[pltpu.VMEM((sum(counts), width), BF16)],
            )
        whole = join_lanes(parts, places)
        ends = [sum(counts[: k + 1]) for k in range(len(counts))]
        outs = []
        for count, end, shape, form in zip(counts, ends, shapes, forms):
            piece = whole[end - count : end]
            if form == 1:
                piece = piece.T
            if form == 2:
                piece = jnp.concatenate(
                    [piece[:, q * LANES : q * LANES + shape[0]].T for q in range(width // LANES)],
                    axis=1,
                )
            if form == 3:
                piece = lax.dynamic_slice_in_dim(piece[: shape[0]], row * shape[1], shape[1], 1)
            outs.append(piece)
        return outs

    (temporal_grad,) = assemble(firsts, [own_temporal], [(own_temporal, mid)], (0,))
    expand_grad, spatial_grad, class_grad, bank_grad, block_grad, *norm_grads, short_grad = assemble(
        lasts, last_counts, last_shapes, (1, 0, 2, 0, 0, 3, 3, 0)
    )
    class_grad = class_grad.T
    temporal_grad = temporal_grad.reshape(3, own_rows, mid)
    spatial_grad = spatial_grad.reshape(3, 3, own_mid, mid)
    block_grad = block_grad.reshape(2, 4, own_mid, width)
    out_gain_all = facts_total[:steps].reshape(-1)
    out_shift_all = facts_total[steps : 2 * steps].reshape(-1)
    out_gain_grad = lax.dynamic_slice_in_dim(out_gain_all, row * own_rows, own_rows, 0)
    out_shift_grad = lax.dynamic_slice_in_dim(out_shift_all, row * own_rows, own_rows, 0)
    gain_all = jnp.stack([facts_total[fact_rows - 2], facts_total[2 * steps]])
    shift_all = jnp.stack([facts_total[fact_rows - 1], facts_total[2 * steps + 1]])
    mid_gain_grad = lax.dynamic_slice_in_dim(gain_all, row * own_mid, own_mid, 1)
    mid_shift_grad = lax.dynamic_slice_in_dim(shift_all, row * own_mid, own_mid, 1)
    return (
        scores,
        input_grad,
        temporal_grad,
        spatial_grad,
        expand_grad,
        mid_gain_grad,
        mid_shift_grad,
        out_gain_grad,
        out_shift_grad,
        short_grad,
        bank_grad,
        block_grad,
        *norm_grads,
        class_grad,
    )


def solution(mesh):
    whole = P()
    in_specs = (
        (P("clip", None, "row", None, None),)
        + (whole,) * 13
        + (
            P("clip", "row", None),
            P("clip", None),
            P("clip", None),
            P("clip"),
            P(("clip", "row")),
            P(("clip", "row"), None),
        )
    )
    out_specs = (
        P(("clip", "row"), None),
        P("clip", None, "row", None, None),
        P(None, "row", None),
        P(None, None, "row", None),
        P(None, "row"),
        P(None, "row"),
        P(None, "row"),
        P("row"),
        P("row"),
        P("row", None),
        P("row", None),
        P(None, None, "row", None),
        P(None, "row"),
        P(None, "row"),
        P("row", None),
    )
    return jax.shard_map(body, mesh=mesh, in_specs=in_specs, out_specs=out_specs, check_vma=False)
```

```python
import math

import jax
import jax.numpy as jnp
from jax import lax
from jax.experimental import pallas as pl
from jax.experimental.pallas import tpu as pltpu
from jax.sharding import PartitionSpec as P

SAMPLES = 14
LANES = 128
SUBLANES = 8
EPSILON = 1e-05
F32 = jnp.float32
BF16 = jnp.bfloat16


def dot(left, right, dims):
    return lax.dot_general(left, right, (dims, ((), ())), preferred_element_type=F32)


def mm(left, right):
    return dot(left, right, ((1,), (0,)))


def mm_nt(left, right):
    return dot(left, right, ((1,), (1,)))


def mm_tn(left, right):
    return dot(left, right, ((0,), (0,)))


def swap(values, axis, mask):
    count = lax.axis_size(axis)
    return lax.ppermute(values, axis, [(i, i ^ mask) for i in range(count)])


def tree_sum(parts):
    while len(parts) > 1:
        parts = [parts[i] + parts[i + 1] for i in range(0, len(parts), 2)]
    return parts[0]


def step_masks(count):
    even = [1 << t for t in range(count.bit_length() - 1)]
    odd = list(even)
    for t in range(0, len(odd) - 1, 2):
        odd[t], odd[t + 1] = odd[t + 1], odd[t]
    return even, odd


def joint_swap(values, even_mask, odd_mask):
    clip_size = lax.axis_size("clip")
    row_size = lax.axis_size("row")
    pairs = []
    for c in range(clip_size):
        for r in range(row_size):
            mask = odd_mask if r % 2 else even_mask
            pairs.append((c * row_size + r, (c ^ mask) * row_size + r))
    return lax.ppermute(values, ("clip", "row"), pairs)


def place_of(code, group, core):
    even, odd = step_masks(lax.axis_size("clip"))
    first = sum(m for t, m in enumerate(even) if code >> t & 1)
    second = sum(m for t, m in enumerate(odd) if code >> t & 1)
    return group ^ (first if first == second else jnp.where(core == 0, first, second))


def give(held, t):
    return jnp.concatenate([held[code].astype(BF16) for code in held if code >> t & 1], axis=0)


def take(held, t, got):
    low = [code for code in held if not code >> t & 1]
    rows = got.shape[0] // len(low)
    return {
        code: held[code].astype(F32) + got[n * rows : (n + 1) * rows].astype(F32)
        for n, code in enumerate(low)
    }


def bits(count):
    return count.bit_length() - 1


def pad_rows(values, rows):
    return jnp.pad(values, ((0, rows - values.shape[0]), (0, 0)))


def axis_weights(low_edge, high_edge, cell_count, first_cell, span_count):
    samples = (jnp.arange(SAMPLES, dtype=F32) + 0.5) / SAMPLES
    start_pos = low_edge.astype(F32) * 0.25
    extent = (high_edge - low_edge).astype(F32) * 0.25
    points = start_pos[:, None] + extent[:, None] * samples[None, :]
    points = jnp.clip(points - 0.5, 0.0, cell_count - 1.0)
    centers = (first_cell + jnp.arange(span_count, dtype=jnp.int32)).astype(F32)
    tents = jnp.maximum(0.0, 1.0 - jnp.abs(points[:, :, None] - centers[None, None, :]))
    return jnp.mean(tents, axis=1)


def box_weights(coords, clip_local, first_row, row_count, rows_total, clip_count, col_count):
    along_rows = axis_weights(coords[:, 0], coords[:, 1], rows_total, first_row, row_count)
    along_cols = axis_weights(coords[:, 2], coords[:, 3], col_count, 0, col_count)
    member = (clip_local[:, None] == jnp.arange(clip_count, dtype=jnp.int32)[None, :]).astype(F32)
    product = along_rows[:, None, :, None] * along_cols[:, None, None, :] * member[:, :, None, None]
    return product.astype(BF16)


def silu_slope(value_in):
    gate = jax.nn.sigmoid(value_in)
    return gate * (1.0 + value_in * (1.0 - gate))


VMEM = pl.BlockSpec(memory_space=pltpu.VMEM)
SMEM = pl.BlockSpec(memory_space=pltpu.SMEM)
MIB = 1024 * 1024
MIB_DEFAULT = 56


ANY = pl.BlockSpec(memory_space=pl.ANY)


class Loads:
    def __init__(self, pairs, sems):
        self.copies = [
            pltpu.make_async_copy(source, target, sems.at[n])
            for n, (source, target) in enumerate(pairs)
        ]
        self.done = 0
        for copy in self.copies:
            copy.start()

    def wait(self, count):
        while self.done < count:
            self.copies[self.done].wait()
            self.done += 1


def shape_of(shape, dtype):
    return jax.ShapeDtypeStruct(shape, dtype)


def run(kernel, outs, ins, grid=(), in_specs=None, out_specs=None, scratch=(), mib=MIB_DEFAULT):
    return pl.pallas_call(
        kernel,
        grid=grid,
        out_shape=tuple(outs),
        in_specs=in_specs or [VMEM] * len(ins),
        out_specs=tuple(out_specs or [VMEM] * len(outs)),
        scratch_shapes=list(scratch),
        compiler_params=pltpu.CompilerParams(vmem_limit_bytes=mib * MIB),
        cost_estimate=pl.CostEstimate(flops=0, bytes_accessed=0, transcendentals=0),
    )(*ins)


def frame_shift(values, clips, step):
    grid = values.reshape(clips, -1, values.shape[1])
    rows = grid.shape[1]
    zeros = jnp.zeros((clips, abs(step), values.shape[1]), values.dtype)
    if step > 0:
        moved = jnp.concatenate([zeros, grid[:, : rows - step]], axis=1)
    else:
        moved = jnp.concatenate([grid[:, -step:], zeros], axis=1)
    return moved.reshape(values.shape)


def col_shift(values, cols, step):
    col = lax.broadcasted_iota(jnp.int32, (values.shape[0], 1), 0) % cols
    edge = 0 if step > 0 else cols - 1
    rows = values.shape[0]
    return jnp.where(col == edge, 0.0, pltpu.roll(values, step % rows, 0))


def temporal_kernel(clips, cols, starts, x, w, gain, shift, total, out, *pieces):
    step = pl.program_id(0)
    values = x[...]
    for start, piece in zip(starts, pieces):
        piece[...] = x[start : start + piece.shape[0], :]
    term = mm(frame_shift(values, clips, cols), w[0]) + mm(values, w[1])
    term = term + mm(frame_shift(values, clips, -cols), w[2])

    @pl.when(step == 0)
    def _():
        total[...] = term

    @pl.when(step > 0)
    def _():
        total[...] += term

    @pl.when(step == pl.num_programs(0) - 1)
    def _():
        arg = total[...] * gain[0:1, :] + shift[0:1, :]
        out[...] = (arg * jax.nn.sigmoid(arg)).astype(BF16)


def plane_rows_sum(rows, weights, cols):
    sides = []
    for j in range(3):
        term = None
        for values, kernel in zip(rows, weights):
            part = mm(values, kernel[j])
            term = part if term is None else term + part
        sides.append(term)
    return sides[1] + col_shift(sides[0], cols, 1) + col_shift(sides[2], cols, -1)


def plane_own_kernel(cols, own, w, out):
    out[...] = plane_rows_sum([own[...]], [w[0]], cols)


def plane_kernel(
    clips,
    frames,
    cols,
    above,
    below,
    first,
    last,
    part,
    gain,
    shift,
    expand,
    x,
    og,
    os,
    weights,
    short,
    classes,
    total,
    out,
    low,
    mine,
    other,
    projected,
):
    step = pl.program_id(0)

    @pl.when(step == 0)
    def _():
        whole = part[...] + plane_rows_sum([above[...], below[...]], [first[0], last[0]], cols)
        total[...] = whole
        arg = whole * gain[1:2, :] + shift[1:2, :]
        out[...] = (arg * jax.nn.sigmoid(arg)).astype(BF16)
        projected[...] = jnp.zeros_like(projected)

    arg = mm(out[...], expand[...]) * og[...] + os[...] + x[...].astype(F32)
    active = arg * jax.nn.sigmoid(arg)
    summed = jnp.sum(active.reshape(clips, frames, cols, -1), axis=1)
    pooled = (summed / frames).reshape(clips * cols, -1).astype(BF16)
    values = mm_tn(weights[...], pooled).astype(BF16)
    lanes = low.shape[2]
    for r in range(low.shape[0]):
        low[r] = values[:, r * lanes : (r + 1) * lanes]
    width = short.shape[1]
    count = classes.shape[0]
    projected[:, :width] += mm(values, short[...])
    projected[:, width : width + count] += mm_nt(values, classes[...])

    @pl.when(step == pl.num_programs(0) - 1)
    def _():
        half = mine.shape[0]
        core = lax.rem(lax.axis_index("row"), 2)
        mine[...] = projected[pl.ds(core * half, half), :]
        other[...] = projected[pl.ds((1 - core) * half, half), :].astype(BF16)


def slope_kernel(frames, plane_out, expand, x, og, os, sums, slope):
    expand_sum = mm(plane_out[...], expand[...])
    sums[...] = expand_sum.astype(BF16)
    arg = expand_sum * og[...] + os[...] + x[...].astype(F32)
    slope[...] = (silu_slope(arg) * (1.0 / frames)).astype(BF16)


def box_kernel(
    order,
    classes,
    clip_total,
    pos,
    own,
    other,
    bias,
    gain,
    shift,
    memory_far,
    weights_far,
    class_far,
    short_far,
    roi_far,
    scores,
    back_pooled,
    lefts,
    rights,
    keys,
    mixes,
    stats,
    last_low,
    first_low,
    back_logits_ref,
    norms,
    total,
    facts,
    attention_ref,
    memory,
    weights,
    class_rows,
    short,
    roi,
    sems,
):
    loads = Loads(
        [(weights_far.at[0, 0], weights.at[0, 0]), (weights_far.at[0, 1], weights.at[0, 1])]
        + [(memory_far, memory)]
        + [(weights_far.at[0, k], weights.at[0, k]) for k in (2, 3)]
        + [(weights_far.at[1], weights.at[1]), (class_far, class_rows)]
        + [(short_far, short), (roi_far, roi)],
        sems,
    )
    half = total.shape[0] // 2
    quarter = half // 2
    core, chip = pos[0], pos[1]
    side = chip % 2
    each = (own.shape[0] // 2 - quarter) * 2 // len(order)
    for sums, where in ((own, core), (other, 1 - core)):
        for n in range(2):
            base = n * (sums.shape[0] // 2)
            start = where * half + (side if n == 0 else 1 - side) * quarter
            total[pl.ds(start, quarter), :] = sums[base : base + quarter, :].astype(F32)
            for m in range(len(order) // 2):
                place = 4 * (chip ^ order[n * (len(order) // 2) + m]) + 2 * where
                rows = slice(base + quarter + m * each, base + quarter + (m + 1) * each)
                for part in range(2):
                    facts[pl.ds((place + part) * each, each), :] = sums[
                        rows, part * LANES : (part + 1) * LANES
                    ].astype(F32)
    width = memory.shape[1]
    scale = 1.0 / math.sqrt(width)
    clips, slots = bias.shape
    clip_rows = facts[:, classes + 1 : classes + 2].astype(jnp.int32)

    def select(values):
        chosen = values[:, :slots]
        for c in range(1, clips):
            chosen = jnp.where(clip_rows == c, values[:, c * slots : (c + 1) * slots], chosen)
        return chosen

    def spread(values):
        return jnp.concatenate(
            [jnp.where(clip_rows == c, values, 0.0).astype(BF16) for c in range(clips)], axis=1
        )

    dead = jnp.broadcast_to(bias[0:1, :], (clip_rows.shape[0], slots))
    for c in range(1, clips):
        dead = jnp.where(clip_rows == c, bias[c : c + 1, :], dead)
    stream = total[:, :width]
    kept = []
    for n in range(2):
        stream_low = stream.astype(BF16)
        loads.wait(1 if n == 0 else 6)
        query = mm(stream_low, weights[n, 0]).astype(BF16)
        loads.wait(2)
        query_key = mm_nt(query, weights[n, 1]).astype(BF16)
        loads.wait(3)
        masked = select(mm_nt(query_key, memory[...])) * scale + dead
        peak = jnp.max(masked, axis=1, keepdims=True)
        exponent = jnp.exp(masked - peak)
        whole = jnp.sum(exponent, axis=1, keepdims=True)
        attention = exponent * (1.0 / whole)
        attention_ref[n] = attention
        mixed = mm(spread(attention), memory[...]).astype(BF16)
        loads.wait(5)
        attended = mm(mixed, weights[n, 2])
        centred = attended - jnp.mean(attended, axis=1, keepdims=True)
        inverse = lax.rsqrt(jnp.mean(centred * centred, axis=1, keepdims=True) + EPSILON)
        hatted = centred * inverse
        normed = hatted * gain[n : n + 1, :] + shift[n : n + 1, :]
        hidden = (normed * jax.nn.sigmoid(normed)).astype(BF16)
        stream = stream + mm(hidden, weights[n, 3])
        lefts[4 * n] = stream_low
        lefts[4 * n + 2] = mixed
        lefts[4 * n + 3] = hidden
        rights[4 * n + 1] = query
        keys[n] = query_key
        kept.append((peak + jnp.log(whole), hatted, inverse, normed))
    stream_low = stream.astype(BF16)
    last_low[...] = stream_low
    loads.wait(7)
    split = class_rows.shape[1] - width
    logits = total[:, width : width + classes] + mm_nt(stream_low, class_rows[:, split:])
    chance = jax.nn.sigmoid(logits)
    scores[...] = chance
    valid = facts[:, classes : classes + 1]
    back_logits = (chance - facts[:, :classes]) * valid / clip_total
    back_logits = back_logits.astype(BF16)
    back_logits_ref[...] = back_logits
    back_stream = mm(back_logits, class_rows[:, split:])
    inners = [None, None]
    for n in (1, 0):
        log_sum, hatted, inverse, normed = kept[n]
        back_branch = back_stream.astype(BF16)
        back_normed = mm_nt(back_branch, weights[n, 3]) * silu_slope(normed)
        norms[n : n + 1, :] = jnp.sum(back_normed * hatted, axis=0, keepdims=True)
        norms[n + 2 : n + 3, :] = jnp.sum(back_normed, axis=0, keepdims=True)
        back_hat = back_normed * gain[n : n + 1, :]
        back_attended = inverse * (
            back_hat
            - jnp.mean(back_hat, axis=1, keepdims=True)
            - hatted * jnp.mean(back_hat * hatted, axis=1, keepdims=True)
        )
        back_att_low = back_attended.astype(BF16)
        back_mixed = mm_nt(back_att_low, weights[n, 2]).astype(BF16)
        attention = attention_ref[n]
        back_attention = select(mm_nt(back_mixed, memory[...]))
        inner = jnp.sum(attention * back_attention, axis=1, keepdims=True)
        back_raw = attention * (back_attention - inner) * scale
        back_key_mix = mm(spread(back_raw), memory[...]).astype(BF16)
        back_query = mm(back_key_mix, weights[n, 1]).astype(BF16)
        back_stream = back_stream + mm_nt(back_query, weights[n, 0])
        lefts[4 * n + 1] = back_key_mix
        rights[4 * n] = back_query
        rights[4 * n + 2] = back_att_low
        rights[4 * n + 3] = back_branch
        mixes[n] = back_mixed
        inners[n] = inner
    lane = lax.broadcasted_iota(jnp.int32, stats.shape, 1)
    stats[...] = jnp.where(
        lane == 0,
        kept[0][0],
        jnp.where(
            lane == 1,
            kept[1][0],
            jnp.where(
                lane == 2,
                inners[0],
                jnp.where(lane == 3, inners[1], facts[:, classes + 1 : classes + 2]),
            ),
        ),
    )
    back_low = back_stream.astype(BF16)
    first_low[...] = back_low
    loads.wait(9)
    back_boxes = mm(back_logits, class_rows[:, :split]) + mm_nt(back_low, short[...])
    back_pooled[...] = mm(roi[...], back_boxes.astype(BF16))


def bank_kernel(
    pos, keys, mixes, stats, memory, tag, feats, low, back_logits, last_low, wide, rows
):
    width = memory.shape[1]
    scale = 1.0 / math.sqrt(width)
    allowed = stats[:, 4:5].astype(jnp.int32) == tag[...]
    back_memory = None
    for n in range(2):
        raw = mm_nt(keys[n], memory[...])
        attention = jnp.where(allowed, jnp.exp(raw * scale - stats[:, n : n + 1]), 0.0)
        back_attention = mm_nt(mixes[n], memory[...])
        back_raw = (attention * (back_attention - stats[:, n + 2 : n + 3]) * scale).astype(BF16)
        term = mm_tn(back_raw, keys[n]) + mm_tn(attention.astype(BF16), mixes[n])
        back_memory = term if back_memory is None else back_memory + term
    count, boxes, lanes = low.shape
    low_memory = back_memory.astype(BF16)
    fine = rows.shape[0] // count // (width // LANES)
    for r in range(count):
        values = mm_tn(feats[:, r * lanes : (r + 1) * lanes], low_memory)
        wide[r, fine:, :] = values.astype(BF16)
    classes = back_logits.shape[1]
    rows[...] = jnp.zeros_like(rows)
    for r in range(count):
        rows[r * lanes : (r + 1) * lanes, :classes] = mm_tn(low[r], back_logits[...])
    box = lax.broadcasted_iota(jnp.int32, (boxes, 1), 0)
    mine = (box // (boxes // count)) == 2 * pos[1] + pos[0]
    own_logits = jnp.where(mine, back_logits[...].astype(F32), 0.0).astype(BF16)
    rows[count * lanes :, :classes] = mm_tn(last_low[...], own_logits)
    blocks = width // LANES
    for r in range(count):
        for q in range(blocks):
            start = (r * blocks + q) * fine
            wide[r, :fine, q * LANES : (q + 1) * LANES] = rows[start : start + fine, :].astype(BF16)


def block_kernel(lefts, rights, pick, norms, block):
    own = pick.shape[1]
    for item in range(8):
        columns = mm(lefts[item], pick[...]).astype(BF16)
        block[item * own : (item + 1) * own, :] = mm_tn(columns, rights[item]).astype(BF16)
    block[8 * own :, :] = jnp.zeros((block.shape[0] - 8 * own, block.shape[1]), BF16)
    for n in range(2):
        start = 8 * own + n * 2 * SUBLANES
        block[start : start + 2, :] = norms[2 * n : 2 * n + 2, :].astype(BF16)


def weight_kernel(cols, count, pos, back_expand, plane_out, above, own, below, back_plane, keep, send):
    width = plane_out.shape[1]
    lanes = back_expand.shape[1] // count
    rows = width // count

    def put(start, first, second):
        place = slice(start, start + first.shape[0])

        @pl.when(pos[0] == 0)
        def _():
            keep[place, :] = first.astype(BF16)
            send[place, :] = second.astype(BF16)

        @pl.when(pos[0] != 0)
        def _():
            keep[place, :] = second.astype(BF16)
            send[place, :] = first.astype(BF16)

    each = lanes + 9 * rows
    for chip in range(count // 2):
        block = mm_tn(back_expand[:, 2 * chip * lanes : 2 * (chip + 1) * lanes], plane_out[...])
        put(chip * each, block[:lanes], block[lanes:])
    whole = back_plane[...].astype(F32)
    moved = jnp.concatenate(
        [
            col_shift(whole, cols, -1).astype(BF16),
            back_plane[...],
            col_shift(whole, cols, 1).astype(BF16),
        ],
        axis=1,
    )
    for i, source in enumerate((above, own, below)):
        block = mm_tn(source[...], moved)
        for j in range(3):
            for chip in range(count // 2):
                start = chip * each + lanes + (3 * i + j) * rows
                top = 2 * chip * rows
                columns = slice(j * width, (j + 1) * width)
                put(
                    start,
                    block[top : top + rows, columns],
                    block[top + rows : top + 2 * rows, columns],
                )


def temporal_grad_kernel(clips, cols, count, lanes, pos, *refs):
    sources, pieces = refs[: -3 - count], refs[-3 - count : -3]
    keep, send, moved = refs[-3:]
    step = pl.program_id(0)
    cells, wide = sources[0].shape
    part = pieces[0].shape[1]

    @pl.when(step == 0)
    def _():
        facts = None
        for s, piece in enumerate(pieces):
            values = piece[:cells, :]
            shifts = (frame_shift(values, clips, -cols), values, frame_shift(values, clips, cols))
            for k in range(3):
                moved[k * part : (k + 1) * part, s * cells : (s + 1) * cells] = shifts[k].T
            term = piece[cells:, :].astype(F32)
            facts = term if facts is None else facts + term
        low = facts.astype(BF16)
        each = 3 * lanes + low.shape[0]
        for end in range(each, keep.shape[0] + 1, each):
            keep[end - low.shape[0] : end, :] = low
            send[end - low.shape[0] : end, :] = low

    total, start = None, 0
    for source in sources:
        end = start + source.shape[0]
        term = mm(moved[:, start:end], source[...])
        total = term if total is None else total + term
        start = end
    blocks = wide // (2 * lanes)
    each = 3 * lanes + pieces[0].shape[0] - cells
    for block in range(blocks):
        for k in range(3):
            turned = total[k * part : (k + 1) * part, 2 * block * lanes : 2 * (block + 1) * lanes].T
            start = pl.multiple_of(step * (blocks * each), 16) + block * each + k * lanes
            first = turned[:lanes].astype(BF16)
            second = turned[lanes:].astype(BF16)

            @pl.when(pos[0] == 0)
            def _():
                keep[pl.ds(start, lanes), :] = first
                send[pl.ds(start, lanes), :] = second

            @pl.when(pos[0] != 0)
            def _():
                keep[pl.ds(start, lanes), :] = second
                send[pl.ds(start, lanes), :] = first


def back_plane_kernel(
    clips,
    frames,
    cols,
    back_pooled,
    slope,
    sums,
    expand,
    og,
    plane_sum,
    gain,
    shift,
    back_expand,
    back_plane,
    facts,
    acc,
    rows,
):
    step = pl.program_id(0)
    steps = pl.num_programs(0)
    cells, lanes = slope.shape

    @pl.when(step == 0)
    def _():
        rows[...] = jnp.zeros_like(rows)

    pooled = back_pooled[...].reshape(clips, 1, cols, lanes)
    final = (pooled * slope[...].astype(F32).reshape(clips, frames, cols, lanes)).reshape(cells, lanes)
    rows[pl.ds(step, 1), :] = jnp.sum(final * sums[...].astype(F32), axis=0, keepdims=True)
    rows[pl.ds(steps + step, 1), :] = jnp.sum(final, axis=0, keepdims=True)
    low = (final * og[...]).astype(BF16)
    back_expand[...] = low
    term = mm_nt(low, expand[...])

    @pl.when(step == 0)
    def _():
        acc[...] = term

    @pl.when(step > 0)
    def _():
        acc[...] += term

    @pl.when(step == steps - 1)
    def _():
        back_arg = acc[...] * silu_slope(plane_sum[...] * gain[1:2, :] + shift[1:2, :])
        rows[pl.ds(2 * steps, 1), :] = jnp.sum(back_arg * plane_sum[...], axis=0, keepdims=True)
        rows[pl.ds(2 * steps + 1, 1), :] = jnp.sum(back_arg, axis=0, keepdims=True)
        back_plane[...] = (back_arg * gain[1:2, :]).astype(BF16)
        facts[...] = rows[...].astype(BF16)


def back_temporal_kernel(
    cols, pos, gain, shift, late, rows, w, temporal_sum, out, facts, *pieces
):
    sides = []
    for j in range(3):
        term = mm_nt(rows[0][...], w[0, j]) + mm_nt(rows[1][...], w[1, j])
        sides.append(term + mm_nt(rows[2][...], w[2, j]))
    back_out = sides[1] + col_shift(sides[0], cols, -1) + col_shift(sides[2], cols, 1)
    back_arg = back_out * silu_slope(temporal_sum[...] * gain[0:1, :] + shift[0:1, :])
    cells, width = out.shape
    facts[...] = late[...].astype(F32)
    facts[facts.shape[0] - 2 : facts.shape[0] - 1, :] = jnp.sum(
        back_arg * temporal_sum[...], axis=0, keepdims=True
    )
    facts[facts.shape[0] - 1 :, :] = jnp.sum(back_arg, axis=0, keepdims=True)
    out[...] = (back_arg * gain[0:1, :]).astype(BF16)
    for s, piece in enumerate(pieces):
        start = pl.multiple_of(pos[2 + s] * LANES, LANES)
        piece[:cells, :] = out[:, pl.ds(start, LANES)]
        rows = facts.shape[0]
        for q in range(width // LANES):
            piece[cells + q * rows : cells + (q + 1) * rows, :] = facts[
                :, q * LANES : (q + 1) * LANES
            ].astype(BF16)


def input_kernel(clips, frames, cols, back, w, back_pooled, slope, out):
    values = back[...]
    cells, lanes = slope.shape
    pooled = back_pooled[...].reshape(clips, 1, cols, lanes)
    total = (pooled * slope[...].astype(F32).reshape(clips, frames, cols, lanes)).reshape(cells, lanes)
    total = total + mm_nt(values, w[1]) + mm_nt(frame_shift(values, clips, -cols), w[0])
    out[...] = total + mm_nt(frame_shift(values, clips, cols), w[2])


def lanes_kernel(counts, forms, pos, *refs):
    outs, whole = refs[-1 - len(counts) : -1], refs[-1]
    rows = whole.shape[0]
    index = 0
    for ref in refs[: -1 - len(counts)]:
        for n in range(ref.shape[0] // rows):
            start = pl.multiple_of(pos[index] * LANES, LANES)
            whole[:, pl.ds(start, LANES)] = ref[n * rows : (n + 1) * rows, :]
            index += 1
    start = 0
    for count, form, out in zip(counts, forms, outs):
        piece = whole[start : start + count, :].astype(F32)
        start += count
        if form == 0:
            out[...] = piece
        elif form == 1:
            out[...] = piece.T
        elif form == 2:
            for q in range(whole.shape[1] // LANES):
                first = q * LANES
                out[:, q * count : (q + 1) * count] = piece[:, first : first + out.shape[0]].T
        else:
            own = out.shape[1]
            shift = whole.shape[1] - pos[pos.shape[0] - 1] * own
            moved = pltpu.roll(piece[: 2 * SUBLANES, :], shift, 1)
            out[...] = moved[: out.shape[0], :own]


def blocks_kernel(codes, pos, *refs):
    sources, outs = refs[: -len(codes)], refs[-len(codes) :]
    for group, out in zip(codes, outs):
        row = 0
        for code in group:
            start = pl.multiple_of(pos[code] * LANES, LANES)
            for source in sources:
                count = source.shape[0]
                out[row : row + count, :] = source[:, pl.ds(start, LANES)]
                row += count


class Halving:
    def __init__(self, held, steps, send, step=0, first=None):
        self.held, self.steps, self.send = held, steps, send
        self.step, self.got, self.first = step, None, first

    def advance(self, hold):
        if self.got is not None:
            self.held = take(self.held, self.step - 1, self.got)
            self.got = None
        if self.step < self.steps:
            buffer = give(self.held, self.step) if self.first is None else self.first
            self.first = None
            buffer, hold = lax.optimization_barrier((buffer, hold))
            self.got = self.send(self.step, buffer)
            self.step += 1
        return hold

    def finish(self):
        while self.got is not None:
            self.advance(())
        return self.held[0]


class Doubling:
    def __init__(self, own, steps, send):
        self.parts, self.steps, self.send = [own], steps, send
        self.step, self.got = 0, None

    def advance(self, hold):
        if self.got is not None:
            self.parts.append(self.got)
            self.got = None
        if self.step < self.steps:
            buffer = self.parts[0] if self.step == 0 else jnp.concatenate(self.parts, axis=0)
            buffer, hold = lax.optimization_barrier((buffer, hold))
            self.got = self.send(self.step, buffer)
            self.step += 1
        return hold

    def finish(self):
        while self.got is not None:
            self.advance(())
        return self.parts


def window(values, chains):
    chains = [chain for chain in chains if chain.got is not None]
    tied = lax.optimization_barrier((tuple(values), tuple(chain.got for chain in chains)))
    for chain, got in zip(chains, tied[1]):
        chain.got = got
    return tied[0]


def join_lanes(parts, places):
    rows = parts[0].shape[0]
    blocks = [part[n * rows : (n + 1) * rows] for part in parts for n in range(part.shape[0] // rows)]
    joined = []
    for target in range(len(blocks)):
        chosen = blocks[0]
        for code in range(1, len(blocks)):
            chosen = jnp.where(places[code] == target, blocks[code], chosen)
        joined.append(chosen)
    return jnp.concatenate(joined, axis=-1).astype(F32)


def body(
    clip_input,
    temporal,
    spatial,
    expand,
    mid_gain,
    mid_shift,
    out_gain,
    out_shift,
    short_weight,
    bank_weight,
    block_weight,
    norm_gain,
    norm_shift,
    class_weight,
    bank_feats,
    bank_mask,
    box_coords,
    box_clip,
    box_valid,
    labels,
):
    row = lax.axis_index("row")
    group = lax.axis_index("clip")
    row_size = lax.axis_size("row")
    clip_size = lax.axis_size("clip")
    core = row % 2
    chip = row // 2
    chips = row_size // 2
    clips, frames, rows_local, cols, channels = clip_input.shape
    mid = temporal.shape[2]
    width = short_weight.shape[1]
    classes = class_weight.shape[1]
    cells = clips * frames * cols
    boxes = box_coords.shape[0]
    box_local = labels.shape[0]
    slots_local = bank_feats.shape[1]
    part = mid // clip_size
    steps = channels // mid
    lanes = channels // row_size
    crossed = clip_size == 4
    masks = [(s, s) for s in range(clip_size)]
    if crossed:
        masks = [(0, 0), (1, 2), (2, 1), (3, 3)]
    targets = [group ^ jnp.where(core == 0, first, second) for first, second in masks]
    place = jnp.stack([core, chip, *targets]).astype(jnp.int32)
    og, os = out_gain[None], out_shift[None]

    tie = lax.optimization_barrier
    source = clip_input.reshape(cells, channels)

    wide_input = [source]
    if not crossed:
        wide_input += [swap(source, "clip", s) for s in range(1, clip_size)]

    def passed(values, after, even_mask, odd_mask):
        values, _ = tie((values, after))
        return joint_swap(values, even_mask, odd_mask)

    def kernel_row(i):
        return pl.BlockSpec((1, 3, mid, mid), lambda _: (i, 0, 0, 0))

    def fixed(*shape):
        return pl.BlockSpec(shape, lambda i: (0,) * len(shape))

    def across(height, lane_count):
        return pl.BlockSpec((height, lane_count), lambda i: (0, i))

    eighth = cells // 8
    cuts = [(0, 2), (2, 4), (6, 2), (0, 1), (1, 6), (7, 1)] if crossed else []
    temporal_sum, temporal_out, *cut_rows = run(
        lambda *refs: temporal_kernel(clips, cols, [start * eighth for start, _ in cuts], *refs),
        [shape_of((cells, mid), F32), shape_of((cells, mid), BF16)]
        + [shape_of((count * eighth, channels), BF16) for _, count in cuts],
        [source, temporal, mid_gain, mid_shift],
        grid=(steps,),
        in_specs=[
            across(cells, mid),
            pl.BlockSpec((3, mid, mid), lambda i: (0, i, 0)),
            fixed(2, mid),
            fixed(2, mid),
        ],
        out_specs=[fixed(cells, mid), fixed(cells, mid)]
        + [across(count * eighth, mid) for _, count in cuts],
    )

    def halo(values):
        ends = row_size - 1
        above = lax.ppermute(values, "row", [(i, i + 1) for i in range(ends)])
        below = lax.ppermute(values, "row", [(i + 1, i) for i in range(ends)])
        return above, below

    above_row, below_row = halo(temporal_out)

    if crossed:
        first_a = joint_swap(cut_rows[0], 1, 2)
    feats, box_coords, temporal_out = tie(
        (bank_feats.reshape(clips * slots_local, channels), box_coords, temporal_out)
    )
    memory_own = mm(feats, bank_weight).astype(BF16)
    clip_group = box_clip - group * clips
    weights = box_weights(
        box_coords, clip_group, row * rows_local, rows_local, rows_local * row_size, clips, cols
    ).reshape(boxes, clips * cols).T
    class_rows = class_weight.T

    (plane_part,) = run(
        lambda *refs: plane_own_kernel(cols, *refs),
        [shape_of((cells, mid), F32)],
        [temporal_out, spatial],
        grid=(1,),
        in_specs=[fixed(cells, mid), kernel_row(1)],
        out_specs=[fixed(cells, mid)],
    )
    above_row, below_row, memory_own, plane_part = tie(
        (above_row, below_row, memory_own, plane_part)
    )
    memory = lax.all_gather(
        memory_own.reshape(clips, slots_local, width), "row", axis=1, tiled=True
    ).reshape(-1, width)
    tied = (above_row, below_row, plane_part, weights, class_rows)
    if crossed:
        *tied, first_a = tie((*tied, first_a))
    else:
        tied = tie(tied)
    above_row, below_row, plane_part, weights, class_rows = tied
    if crossed:
        first_b = passed(cut_rows[1], above_row, 1, 2)
    half = boxes // 2
    joint = width + LANES
    plane_sum, plane_out, partial_low, mine, other = run(
        lambda *refs: plane_kernel(clips, frames, cols, *refs),
        [
            shape_of((cells, mid), F32),
            shape_of((cells, mid), BF16),
            shape_of((row_size, boxes, lanes), BF16),
            shape_of((half, joint), F32),
            shape_of((half, joint), BF16),
        ],
        [
            above_row,
            below_row,
            spatial,
            spatial,
            plane_part,
            mid_gain,
            mid_shift,
            expand,
            source,
            og,
            os,
            weights,
            short_weight,
            class_rows,
        ],
        grid=(steps,),
        in_specs=[
            fixed(cells, mid),
            fixed(cells, mid),
            kernel_row(0),
            kernel_row(2),
            fixed(cells, mid),
            fixed(2, mid),
            fixed(2, mid),
            across(mid, mid),
            across(cells, mid),
            across(1, mid),
            across(1, mid),
            fixed(clips * cols, boxes),
            pl.BlockSpec((mid, width), lambda i: (i, 0)),
            across(classes, mid),
        ],
        out_specs=[
            fixed(cells, mid),
            fixed(cells, mid),
            pl.BlockSpec((mid // lanes, boxes, lanes), lambda i: (i, 0, 0)),
            fixed(half, joint),
            fixed(half, joint),
        ],
        scratch=[pltpu.VMEM((boxes, joint), F32)],
    )

    if crossed:
        mine, other, plane_out, first_b = tie((mine, other, plane_out, first_b))
        first_c = passed(cut_rows[2], mine, 1, 2)
        second_a = passed(cut_rows[3], mine, 2, 1)
    clip_own = lax.dynamic_slice_in_dim(clip_group, row * box_local, box_local, 0)
    facts = jnp.concatenate(
        [labels.astype(BF16), box_valid.astype(BF16)[:, None], clip_own.astype(BF16)[:, None]], axis=1
    )
    facts = jnp.pad(facts, ((0, 0), (0, LANES - facts.shape[1])))
    facts = jnp.concatenate([facts[: box_local // 2], facts[box_local // 2 :]], axis=1)
    facts = jnp.pad(facts, ((0, 0), (0, joint - 2 * LANES)))
    half_sum = mine + swap(other, "row", 1).astype(F32)
    quarter = half // 2
    side = chip % 2
    got = swap(
        lax.dynamic_slice_in_dim(half_sum, (1 - side) * quarter, quarter, 0).astype(BF16), "row", 2
    )
    plane_late, _ = tie((plane_out, half_sum))
    expand_sums, slope = run(
        lambda *refs: slope_kernel(frames, *refs),
        [shape_of((cells, channels), BF16), shape_of((cells, channels), BF16)],
        [plane_late, expand, source, og, os],
        grid=(steps,),
        in_specs=[
            fixed(cells, mid),
            across(mid, mid),
            across(cells, mid),
            across(1, mid),
            across(1, mid),
        ],
        out_specs=[across(cells, mid)] * 2,
    )
    if crossed:
        got, slope, first_c, second_a = tie((got, slope, first_c, second_a))
    else:
        got, slope = tie((got, slope))
    part_sum = lax.dynamic_slice_in_dim(half_sum, side * quarter, quarter, 0) + got.astype(F32)
    label_rows, codes = [facts], [0]
    for t in range(1, bits(chips)):
        payload = jnp.concatenate([part_sum.astype(BF16)] + label_rows, axis=0)
        got = swap(payload, "row", 2 << t)
        part_sum = part_sum + got[:quarter].astype(F32)
        each = facts.shape[0]
        label_rows = label_rows + [
            got[quarter + n * each : quarter + (n + 1) * each] for n in range(len(codes))
        ]
        codes = codes + [code ^ (1 << t) for code in codes]
    payload = jnp.concatenate([part_sum.astype(BF16)] + label_rows, axis=0)
    got = swap(payload, "row", 2)
    live = bank_mask == 1
    tags = jnp.where(live, jnp.arange(clips, dtype=jnp.int32)[:, None], -1)
    tags_own = lax.dynamic_slice_in_dim(tags, row * slots_local, slots_local, 1).reshape(1, -1)
    bias = jnp.where(live, 0.0, -jnp.inf).astype(F32)
    got, memory, bias = tie((got, memory, bias))
    totals_own = jnp.concatenate([payload, got], axis=0)
    label_order = codes + [code ^ 1 for code in codes]
    totals_other = swap(totals_own, "row", 1)
    if crossed:
        second_b = passed(cut_rows[4], totals_own, 2, 1)

    partial_low, totals_other = tie((partial_low, totals_other))
    short_columns = lax.psum_scatter(partial_low, "row", scatter_dimension=0, tiled=False)

    slots = bias.shape[1]
    stream_shape = (boxes, width)
    (
        scores_all,
        back_pooled,
        lefts,
        rights,
        keys,
        mixes,
        stats,
        last_low,
        first_low,
        back_logits,
        norms,
    ) = run(
        lambda *refs: box_kernel(label_order, classes, float(clips * clip_size), *refs),
        [
            shape_of((boxes, classes), F32),
            shape_of((clips * cols, channels), F32),
            shape_of((8, *stream_shape), BF16),
            shape_of((8, *stream_shape), BF16),
            shape_of((2, *stream_shape), BF16),
            shape_of((2, *stream_shape), BF16),
            shape_of((boxes, LANES), F32),
            shape_of(stream_shape, BF16),
            shape_of(stream_shape, BF16),
            shape_of((boxes, classes), BF16),
            shape_of((4, width), F32),
        ],
        [
            place,
            totals_own,
            totals_other,
            bias,
            norm_gain,
            norm_shift,
            memory,
            block_weight,
            class_rows,
            short_weight,
            weights,
        ],
        in_specs=[SMEM] + [VMEM] * 5 + [ANY] * 5,
        scratch=[
            pltpu.VMEM((boxes, joint), F32),
            pltpu.VMEM((boxes, LANES), F32),
            pltpu.VMEM((2, boxes, slots), F32),
            pltpu.VMEM(memory.shape, BF16),
            pltpu.VMEM(block_weight.shape, BF16),
            pltpu.VMEM(class_rows.shape, BF16),
            pltpu.VMEM(short_weight.shape, BF16),
            pltpu.VMEM(weights.shape, BF16),
            pltpu.SemaphoreType.DMA((9,)),
        ],
    )
    scores = lax.dynamic_slice_in_dim(scores_all, row * box_local, box_local, 0)

    if crossed:
        back_pooled, second_b = tie((back_pooled, second_b))
        third_a = passed(first_a, back_pooled, 2, 1)

    fact_rows = -(-(2 * steps + 2) // 16) * 16
    back_expand, back_plane, second_facts = run(
        lambda *refs: back_plane_kernel(clips, frames, cols, *refs),
        [
            shape_of((cells, channels), BF16),
            shape_of((cells, mid), BF16),
            shape_of((fact_rows, mid), BF16),
        ],
        [
            back_pooled,
            slope,
            expand_sums,
            expand,
            og,
            plane_sum,
            mid_gain,
            mid_shift,
        ],
        grid=(steps,),
        in_specs=[
            across(clips * cols, mid),
            across(cells, mid),
            across(cells, mid),
            across(mid, mid),
            across(1, mid),
            fixed(cells, mid),
            fixed(2, mid),
            fixed(2, mid),
        ],
        out_specs=[
            across(cells, mid),
            fixed(cells, mid),
            fixed(fact_rows, mid),
        ],
        scratch=[pltpu.VMEM((cells, mid), F32), pltpu.VMEM((fact_rows, mid), F32)],
    )

    if crossed:
        back_plane, back_expand, second_facts, third_a = tie(
            (back_plane, back_expand, second_facts, third_a)
        )
        second_c = passed(cut_rows[5], back_plane, 2, 1)
        third_b = passed(first_b, back_plane, 2, 1)
    back_above, back_below = halo(back_plane)

    fact_count = second_facts.shape[0]
    own_mid = mid // row_size
    own_rows = channels // row_size

    weight_rows = own_rows + 9 * own_mid
    kept_weight, sent_weight = run(
        lambda *refs: weight_kernel(cols, row_size, *refs),
        [shape_of((chips * weight_rows, mid), BF16)] * 2,
        [
            place,
            back_expand,
            plane_out,
            above_row,
            temporal_out,
            below_row,
            back_plane,
        ],
        in_specs=[SMEM] + [VMEM] * 6,
    )
    tied = (back_above, back_below, kept_weight, sent_weight, short_columns)
    if crossed:
        *tied, second_c, third_b = tie((*tied, second_c, third_b))
        third_c = passed(first_c, sent_weight, 2, 1)
        wide_input += [first_a, first_b, first_c, second_a, second_b, second_c]
        wide_input += [third_a, third_b, third_c]
    else:
        tied = tie(tied)
    back_above, back_below, kept_weight, sent_weight, short_columns = tied
    got_weight = swap(sent_weight, "row", 1)

    even, odd = step_masks(clip_size)
    places = [place_of(code, group, core) for code in range(clip_size)]
    block_places = jnp.stack([jnp.asarray(item, jnp.int32) for item in places])

    def clip_step(t, values):
        return joint_swap(values, even[t], odd[t])

    def chip_step(t, values):
        return swap(values, "row", 2 << t)

    def lane_block(values, target):
        return lax.dynamic_slice_in_dim(values, target * part, part, 1)

    def chip_rows(target, *values):
        each = values[0].shape[0] // chips
        rows = [lax.dynamic_slice_in_dim(item, target * each, each, 0) for item in values]
        if len(rows) == 1:
            return rows[0]
        return tree_sum([item.astype(F32) for item in rows]).astype(BF16)

    def over_chips(*values):
        return Halving(
            {code: chip_rows(chip ^ code, *values) for code in range(chips)}, bits(chips), chip_step
        )

    def over_clips(piece):
        return Halving(
            {code: piece(places[code]) for code in range(clip_size)}, bits(clip_size), clip_step
        )

    class_fine = (channels + width) // row_size * LANES // width
    keys, _ = tie((keys, sent_weight))
    (wide_part,) = run(
        bank_kernel,
        [shape_of((row_size, class_fine + own_rows, width), BF16)],
        [
            place,
            keys,
            mixes,
            stats,
            memory_own,
            tags_own,
            feats,
            partial_low,
            back_logits,
            last_low,
        ],
        in_specs=[SMEM] + [VMEM] * 9,
        scratch=[pltpu.VMEM((channels + width, LANES), F32)],
    )
    if crossed:
        got_weight, wide_part, third_c = tie((got_weight, wide_part, third_c))
        wide_input[-3:] = [third_a, third_b, third_c]
    else:
        got_weight, wide_part = tie((got_weight, wide_part))
    wide_own = lax.psum_scatter(wide_part, "row", scatter_dimension=0, tiled=False)

    def weight_blocks(codes):
        return {
            code: (
                lane_block(kept_weight, places[code]).astype(F32)
                + lane_block(got_weight, places[code]).astype(F32)
            ).astype(BF16)
            for code in codes
        }

    high = [code for code in range(clip_size) if code & 1]
    late, early = high[: len(high) // 2], high[len(high) // 2 :]
    held = weight_blocks(early)
    buffers, back_above = tie((tuple(held[code] for code in early), back_above))
    first_step = {code: clip_step(0, values) for code, values in zip(early, buffers)}

    direct = part == LANES
    piece_rows = fact_rows * (mid // part)
    back_temporal, facts_own, *pieces = run(
        lambda pos, gain, shift, late, below, own, above, *refs: back_temporal_kernel(
            cols, pos, gain, shift, late, (below, own, above), *refs
        ),
        [shape_of((cells, mid), BF16), shape_of((fact_rows, mid), F32)]
        + [shape_of((cells + piece_rows, part), BF16)] * (clip_size if direct else 0),
        [
            place,
            mid_gain,
            mid_shift,
            second_facts,
            back_below,
            back_plane,
            back_above,
            spatial,
            temporal_sum,
        ],
        in_specs=[SMEM] + [VMEM] * 8,
    )
    if not direct:
        facts_flat = jnp.concatenate(
            [facts_own[:, q * part : (q + 1) * part] for q in range(mid // part)], axis=0
        ).astype(BF16)
        pieces = [
            jnp.concatenate(
                [lax.dynamic_slice_in_dim(back_temporal, target * part, part, 1), facts_flat], axis=0
            )
            for target in targets
        ]
    back_temporal, first_step, pieces = tie((back_temporal, first_step, tuple(pieces)))

    got = pieces[:1] + tuple(
        joint_swap(piece, *step_mask) for piece, step_mask in zip(pieces[1:], masks[1:])
    )
    kept_weight, got_weight, _ = tie((kept_weight, got_weight, back_temporal))
    held.update(weight_blocks([code for code in range(clip_size) if code not in early]))
    pick = (
        jnp.arange(width, dtype=jnp.int32)[:, None]
        == row * own_mid + jnp.arange(own_mid, dtype=jnp.int32)[None, :]
    ).astype(BF16)
    lefts, _ = tie((lefts, back_temporal))
    (block_part,) = run(
        block_kernel,
        [shape_of((8 * own_mid + 32, width), BF16)],
        [lefts, rights, pick, norms],
    )
    short_part = mm_tn(short_columns, first_low).astype(BF16)
    got, block_part, short_part, held = tie((got, block_part, short_part, held))

    buffers, got = tie((tuple(held[code] for code in late), got))
    first_step.update({code: clip_step(0, values) for code, values in zip(late, buffers)})
    temporal_rows = chips * (3 * own_rows + piece_rows)
    kept_temporal, sent_temporal = run(
        lambda *refs: temporal_grad_kernel(clips, cols, clip_size, lanes, *refs),
        [shape_of((temporal_rows, part), BF16)] * 2,
        [place, *wide_input, *got],
        grid=(steps,),
        in_specs=[SMEM]
        + [across(item.shape[0], mid) for item in wide_input]
        + [fixed(cells + piece_rows, part)] * clip_size,
        out_specs=[fixed(temporal_rows, part)] * 2,
        scratch=[pltpu.VMEM((3 * part, clip_size * cells), BF16)],
    )
    tied = tie((kept_temporal, sent_temporal, first_step))
    kept_temporal, sent_temporal, first_step = tied
    got_temporal = swap(sent_temporal, "row", 1)
    sums_weight = Halving(
        {
            code ^ 1: held[code ^ 1].astype(F32) + values.astype(F32)
            for code, values in first_step.items()
        },
        bits(clip_size),
        clip_step,
        step=1,
    )
    got_temporal = sums_weight.advance(got_temporal)
    sums_temporal = over_chips(kept_temporal, got_temporal)
    back_temporal = sums_temporal.advance(back_temporal)

    (input_grad,) = run(
        lambda *refs: input_kernel(clips, frames, cols, *refs),
        [shape_of((cells, channels), F32)],
        [back_temporal, temporal, back_pooled, slope],
        grid=(steps,),
        in_specs=[
            fixed(cells, mid),
            pl.BlockSpec((3, mid, mid), lambda i: (0, i, 0)),
            across(clips * cols, mid),
            across(cells, mid),
        ],
        out_specs=[across(cells, mid)],
    )
    input_grad = input_grad.reshape(clip_input.shape)

    box_wide = [wide_own.reshape(-1, width), block_part, short_part]
    box_rows = sum(item.shape[0] for item in box_wide)
    if direct:
        groups = [[code for code in range(clip_size) if code & 1 == bit] for bit in (0, 1)]
        kept_box, sent_box = run(
            lambda *refs: blocks_kernel(groups, *refs),
            [shape_of((len(groups[0]) * box_rows, part), BF16)] * 2,
            [block_places, *box_wide],
            in_specs=[SMEM] + [VMEM] * len(box_wide),
        )
        input_grad, kept_box, sent_box = window(
            [input_grad, kept_box, sent_box], [sums_weight, sums_temporal]
        )
        sums_box = Halving(
            {
                code: kept_box[n * box_rows : (n + 1) * box_rows]
                for n, code in enumerate(groups[0])
            },
            bits(clip_size),
            clip_step,
            first=sent_box,
        )
    else:
        (input_grad,) = window([input_grad], [sums_weight, sums_temporal])
        sums_box = over_clips(
            lambda target: jnp.concatenate([lane_block(item, target) for item in box_wide], axis=0)
        )
    sums_weight.got = sums_temporal.advance(sums_weight.got)
    sums_chip = over_chips(tie(sums_weight.finish().astype(BF16)))
    sums_chip.advance(())
    sums_box.advance(())
    window([], [sums_temporal, sums_chip, sums_box])
    sums_chip.advance(())
    sums_box.advance(())
    temporal_got = sums_temporal.finish()
    own_temporal = 3 * own_rows
    facts_total = temporal_got[own_temporal:].reshape(mid // part, fact_rows, part)
    facts_total = jnp.concatenate([facts_total[q] for q in range(mid // part)], axis=1)
    all_first = Doubling(temporal_got[:own_temporal].astype(BF16), bits(clip_size), clip_step)
    all_first.advance(())
    window([], [sums_chip, sums_box, all_first])
    all_first.advance(())
    weight_own = sums_chip.finish().astype(BF16)
    box_own = sums_box.finish().astype(BF16)
    all_last = Doubling(
        jnp.concatenate([weight_own, box_own], axis=0), bits(clip_size), clip_step
    )
    all_last.advance(())
    window([], [all_first, all_last])
    all_last.advance(())
    firsts = all_first.finish()
    lasts = all_last.finish()
    class_count = class_fine * width // LANES
    last_counts = [own_rows, 9 * own_mid, class_fine, own_rows, 8 * own_mid, 16, 16, own_rows]
    last_shapes = [(mid, own_rows), (9 * own_mid, mid), (classes, class_count), (own_rows, width)]
    last_shapes += [(8 * own_mid, width), (2, own_mid), (2, own_mid), (own_rows, width)]

    def assemble(parts, counts, shapes, forms):
        if direct:
            return run(
                lambda *refs: lanes_kernel(counts, forms, *refs),
                [shape_of(shape, F32) for shape in shapes],
                [jnp.append(block_places, row.astype(jnp.int32)), *parts],
                in_specs=[SMEM] + [VMEM] * len(parts),
                scratch=[pltpu.VMEM((sum(counts), width), BF16)],
            )
        whole = join_lanes(parts, places)
        ends = [sum(counts[: k + 1]) for k in range(len(counts))]
        outs = []
        for count, end, shape, form in zip(counts, ends, shapes, forms):
            piece = whole[end - count : end]
            if form == 1:
                piece = piece.T
            if form == 2:
                piece = jnp.concatenate(
                    [piece[:, q * LANES : q * LANES + shape[0]].T for q in range(width // LANES)],
                    axis=1,
                )
            if form == 3:
                piece = lax.dynamic_slice_in_dim(piece[: shape[0]], row * shape[1], shape[1], 1)
            outs.append(piece)
        return outs

    (temporal_grad,) = assemble(firsts, [own_temporal], [(own_temporal, mid)], (0,))
    expand_grad, spatial_grad, class_grad, bank_grad, block_grad, *norm_grads, short_grad = assemble(
        lasts, last_counts, last_shapes, (1, 0, 2, 0, 0, 3, 3, 0)
    )
    class_grad = class_grad.T
    temporal_grad = temporal_grad.reshape(3, own_rows, mid)
    spatial_grad = spatial_grad.reshape(3, 3, own_mid, mid)
    block_grad = block_grad.reshape(2, 4, own_mid, width)
    out_gain_all = facts_total[:steps].reshape(-1)
    out_shift_all = facts_total[steps : 2 * steps].reshape(-1)
    out_gain_grad = lax.dynamic_slice_in_dim(out_gain_all, row * own_rows, own_rows, 0)
    out_shift_grad = lax.dynamic_slice_in_dim(out_shift_all, row * own_rows, own_rows, 0)
    gain_all = jnp.stack([facts_total[fact_rows - 2], facts_total[2 * steps]])
    shift_all = jnp.stack([facts_total[fact_rows - 1], facts_total[2 * steps + 1]])
    mid_gain_grad = lax.dynamic_slice_in_dim(gain_all, row * own_mid, own_mid, 1)
    mid_shift_grad = lax.dynamic_slice_in_dim(shift_all, row * own_mid, own_mid, 1)
    return (
        scores,
        input_grad,
        temporal_grad,
        spatial_grad,
        expand_grad,
        mid_gain_grad,
        mid_shift_grad,
        out_gain_grad,
        out_shift_grad,
        short_grad,
        bank_grad,
        block_grad,
        *norm_grads,
        class_grad,
    )


def solution(mesh):
    whole = P()
    in_specs = (
        (P("clip", None, "row", None, None),)
        + (whole,) * 13
        + (
            P("clip", "row", None),
            P("clip", None),
            P("clip", None),
            P("clip"),
            P(("clip", "row")),
            P(("clip", "row"), None),
        )
    )
    out_specs = (
        P(("clip", "row"), None),
        P("clip", None, "row", None, None),
        P(None, "row", None),
        P(None, None, "row", None),
        P(None, "row"),
        P(None, "row"),
        P(None, "row"),
        P("row"),
        P("row"),
        P("row", None),
        P("row", None),
        P(None, None, "row", None),
        P(None, "row"),
        P(None, "row"),
        P("row", None),
    )
    return jax.shard_map(body, mesh=mesh, in_specs=in_specs, out_specs=out_specs, check_vma=False)
```
